32 devices in a mesh: seq: 4 (over y, x), seg: 8 (over z, core).
Axes of the slice: x: 2, y: 2, z: 4, core: 2. Of those that a mesh axis runs over, the one named last changes fastest.
Arguments:
- tokens: bfloat16 [8, 512, 2048], P('seg', 'seq'), may hold values from -6 to 6
- cotangent: bfloat16 [8, 512, 2048], P('seg', 'seq'), may hold values from -6 to 6
- start_state: float32 [8, 2560], P('seg'), may hold values from -6 to 6
- start_window: float32 [8, 3, 2560], P('seg'), may hold values from -6 to 6
- first_gain: float32 [2048], replicated, may hold values from 0.1 to 1.9
- recur_in: bfloat16 [2048, 2, 2560], P('seg', None, 'seq'), may hold values from -0.125 to 0.125
- conv_taps: float32 [4, 2560], replicated, may hold values from -3 to 3
- conv_bias: float32 [2560], replicated, may hold values from -3 to 3
- decay_gate: bfloat16 [10, 256, 256], replicated, may hold values from -0.375 to 0.375
- input_gate: bfloat16 [10, 256, 256], replicated, may hold values from -0.375 to 0.375
- decay_bias: float32 [2560], replicated, may hold values from -4 to 4
- input_bias: float32 [2560], replicated, may hold values from -4 to 4
- decay_logit: float32 [2560], replicated, may hold values from -9.3 to -3.4
- recur_out: bfloat16 [2048, 2560], P('seg', 'seq'), may hold values from -0.125 to 0.125
- second_gain: float32 [2048], replicated, may hold values from 0.1 to 1.9
- feed_in: bfloat16 [2048, 2, 6144], P('seg', None, 'seq'), may hold values from -0.125 to 0.125
- feed_out: bfloat16 [2048, 6144], P('seg', 'seq'), may hold values from -0.078125 to 0.078125
Outputs:
- output: bfloat16 [8, 512, 2048], P('seg', 'seq')
- input_grad: bfloat16 [8, 512, 2048], P('seg', 'seq')
- start_state_grad: float32 [8, 2560], P('seg')
- start_window_grad: float32 [8, 3, 2560], P('seg')
- first_gain_grad: float32 [2048], replicated
- recur_in_grad: float32 [2048, 2, 2560], P('seg', None, 'seq')
- conv_taps_grad: float32 [4, 2560], replicated
- conv_bias_grad: float32 [2560], replicated
- decay_gate_grad: float32 [10, 256, 256], replicated
- input_gate_grad: float32 [10, 256, 256], replicated
- decay_bias_grad: float32 [2560], replicated
- input_bias_grad: float32 [2560], replicated
- decay_logit_grad: float32 [2560], replicated
- recur_out_grad: float32 [2048, 2560], P('seg', 'seq')
- second_gain_grad: float32 [2048], replicated
- feed_in_grad: float32 [2048, 2, 6144], P('seg', None, 'seq')
- feed_out_grad: float32 [2048, 6144], P('seg', 'seq')
The draws below stay inside these ranges and needn't reach their ends.
All inputs are finite; a program needn't handle non-finite values.
Results may differ from the reference program's by a relative error of at most 0.011.
Values may be sent and summed in bfloat16 or wider, within the bound.
No kernel may reach another device: no remote copies, remote signals or barrier semaphores. Data moves between devices by JAX's collectives and lax.ppermute only.
A program may use at most 448 MiB of HBM per device.

```python
import jax
import jax.numpy as jnp
from jax import lax

D = 2048
HEADS = 10
BLOCK = 256
R = 2560
FF = 6144
KW = 4
SEQ_LEN = 512
SEGS = 8


def draw_decay_logit(key, part):
    key = jax.random.fold_in(key, 7)
    lowest, highest = (0.0001, 0.03)
    spread = jax.random.uniform(key, (R,), jnp.float32)
    rates = jnp.exp(jnp.log(lowest) + spread * (jnp.log(highest) - jnp.log(lowest)))
    return jnp.log(jnp.expm1(rates))


def block_scale(key, extent, shards, smallest, top_value):
    loudness, own = 1.0, jax.random.fold_in(key, 6)
    for dim, blocks in shards:
        steps = jnp.exp(jax.random.uniform(jax.random.fold_in(own, dim), (blocks,), jnp.float32, smallest / len(shards), top_value / len(shards)))
        loudness = loudness * jnp.repeat(steps, extent[dim] // blocks).reshape([-1 if axis == dim else 1 for axis in range(len(extent))])
    return loudness


def normal_values(own_key, shape, width, reach, cuts=(), kind=jnp.bfloat16):
    drawn = width * jax.random.normal(own_key, shape, jnp.float32)
    if cuts:
        drawn = drawn * block_scale(own_key, shape, cuts, -0.22, 0.18)
    return jnp.clip(drawn, -reach, reach).astype(kind)


def setup_inputs(seed: int = 0) -> dict:
    splits = jax.random.split(jax.random.key(seed), 18)
    tokens = normal_values(splits[0], (SEGS, SEQ_LEN, D), 1.0, 6.0, ((0, 8), (1, 4)))
    cotangent = normal_values(splits[1], (SEGS, SEQ_LEN, D), 1.0, 6.0, ((0, 8), (1, 4)))
    start_state = normal_values(splits[2], (SEGS, R), 1.0, 6.0, ((0, 8),), jnp.float32)
    start_window = normal_values(splits[3], (SEGS, KW - 1, R), 1.0, 6.0, ((0, 8),), jnp.float32)
    first_gain = jnp.clip(1.0 + 0.18 * jax.random.normal(splits[4], (D,), jnp.float32), 0.1, 1.9)
    recur_in = normal_values(splits[5], (D, 2, R), D ** -0.5, 0.125, ((0, 8), (2, 4)))
    conv_taps = normal_values(splits[6], (KW, R), 0.5, 3.0, (), jnp.float32)
    conv_bias = normal_values(splits[7], (R,), 0.5, 3.0, (), jnp.float32)
    decay_gate = normal_values(splits[8], (HEADS, BLOCK, BLOCK), BLOCK ** -0.5, 0.375)
    input_gate = normal_values(splits[9], (HEADS, BLOCK, BLOCK), BLOCK ** -0.5, 0.375)
    decay_bias = normal_values(splits[10], (R,), 1.0, 4.0, (), jnp.float32)
    input_bias = normal_values(splits[11], (R,), 1.0, 4.0, (), jnp.float32)
    decay_logit = draw_decay_logit(jax.random.fold_in(splits[17], 71), 0)
    recur_out = normal_values(splits[13], (D, R), R ** -0.5, 0.125, ((0, 8), (1, 4)))
    second_gain = jnp.clip(1.0 + 0.18 * jax.random.normal(splits[14], (D,), jnp.float32), 0.1, 1.9)
    feed_in = normal_values(splits[15], (D, 2, FF), D ** -0.5, 0.125, ((0, 8), (2, 4)))
    feed_out = normal_values(splits[16], (D, FF), FF ** -0.5, 0.078125, ((0, 8), (1, 4)))
    return {"tokens": tokens, "cotangent": cotangent, "start_state": start_state, "start_window": start_window, "first_gain": first_gain, "recur_in": recur_in, "conv_taps": conv_taps, "conv_bias": conv_bias, "decay_gate": decay_gate, "input_gate": input_gate, "decay_bias": decay_bias, "input_bias": input_bias, "decay_logit": decay_logit, "recur_out": recur_out, "second_gain": second_gain, "feed_in": feed_in, "feed_out": feed_out}


EPSILON = 1e-06
RATE_SCALE = 8.0
HIGHEST_PRECISION = lax.Precision.HIGHEST

@jax.custom_vjp
def low(v):
    return lax.optimization_barrier(v.astype(jnp.bfloat16)).astype(jnp.float32)

@jax.custom_vjp
def low_back(v):
    return v

def low_keep(v):
    return (low(v), None)

def low_pass(kept, grad):
    return (grad,)

def back_keep(v):
    return (v, None)

def back_low(kept, grad):
    return (low(grad),)
low.defvjp(low_keep, low_pass)
low_back.defvjp(back_keep, back_low)

def matmul(left, right):
    return jnp.dot(left, right, precision=HIGHEST_PRECISION)

def rms_norm(values, scale_gain):
    factor = lax.rsqrt(lax.optimization_barrier(jnp.mean(values * values, axis=-1, keepdims=True)) + EPSILON)
    return values * factor * scale_gain

def gelu_tanh(values):
    return jax.nn.gelu(values, approximate=True)

def combine_pairs(earlier, later):
    return (earlier[0] * later[0], later[0] * earlier[1] + later[1])

def conv_apply(padded, taps, offset):
    edge_rows = taps.shape[0] - 1
    length = padded.shape[-2] - edge_rows
    summed = padded[..., edge_rows:, :] * taps[0] + offset
    for back_step in range(1, taps.shape[0]):
        summed = summed + padded[..., edge_rows - back_step:edge_rows - back_step + length, :] * taps[back_step]
    return summed

def recurrence_terms(gate_pre, input_pre, conv_out, decay_logit):
    log_decay = -RATE_SCALE * jax.nn.sigmoid(gate_pre) * jax.nn.softplus(decay_logit)
    decays = jnp.exp(log_decay)
    drive_terms = jnp.sqrt(-jnp.expm1(2.0 * log_decay)) * jax.nn.sigmoid(input_pre) * conv_out
    return (decays, drive_terms)

def segment(inputs, start_state, start_window, params):
    first_gain, recur_in, conv_taps, conv_bias, decay_gate, input_gate, decay_bias, input_bias, decay_logit, recur_out, second_gain, feed_in, feed_out = params
    recur_width = conv_taps.shape[1]
    head_count = decay_gate.shape[0]
    block_size = decay_gate.shape[1]
    length = inputs.shape[0]
    normed1 = low(rms_norm(inputs, first_gain))
    branch_pre = low_back(matmul(normed1, recur_in[:, 0, :]))
    conv_in = low_back(matmul(normed1, recur_in[:, 1, :]))
    padded = jnp.concatenate([start_window, conv_in], axis=0)
    conv_out = conv_apply(padded, conv_taps, conv_bias)
    conv_low = low(conv_out).reshape(length, head_count, block_size)
    gate_pre = low_back(jnp.einsum('nhb,hbc->nhc', conv_low, decay_gate, precision=HIGHEST_PRECISION).reshape(length, recur_width) + decay_bias)
    input_pre = low_back(jnp.einsum('nhb,hbc->nhc', conv_low, input_gate, precision=HIGHEST_PRECISION).reshape(length, recur_width) + input_bias)
    decays, drive_terms = recurrence_terms(gate_pre, input_pre, conv_out, decay_logit)
    prod_all, state_all = lax.associative_scan(combine_pairs, (decays, drive_terms), axis=0)
    states = prod_all * start_state + state_all
    mixed_low = low(states * gelu_tanh(branch_pre))
    mixer_out = low_back(matmul(mixed_low, recur_out.T))
    residual = inputs + mixer_out
    normed2 = low(rms_norm(residual, second_gain))
    gate_val = low_back(matmul(normed2, feed_in[:, 0, :]))
    up_val = low_back(matmul(normed2, feed_in[:, 1, :]))
    hidden = low(gelu_tanh(gate_val) * up_val)
    return residual + matmul(hidden, feed_out.T)

def reference(tokens, cotangent, start_state, start_window, first_gain, recur_in, conv_taps, conv_bias, decay_gate, input_gate, decay_bias, input_bias, decay_logit, recur_out, second_gain, feed_in, feed_out):
    params = (first_gain, recur_in.astype(jnp.float32), conv_taps, conv_bias, decay_gate.astype(jnp.float32), input_gate.astype(jnp.float32), decay_bias, input_bias, decay_logit, recur_out.astype(jnp.float32), second_gain, feed_in.astype(jnp.float32), feed_out.astype(jnp.float32))

    def one_segment(carried, pieces):
        inputs, upstream, state_now, window_now = pieces
        result, pull_back = jax.vjp(segment, inputs.astype(jnp.float32), state_now, window_now, params)
        input_grad, state_grad, window_grad, param_grads = pull_back(upstream.astype(jnp.float32))
        carried = jax.tree.map(lambda first_part, second_part: first_part + second_part, carried, param_grads)
        return (carried, (result.astype(jnp.bfloat16), input_grad.astype(jnp.bfloat16), state_grad, window_grad))
    zero_grads = jax.tree.map(jnp.zeros_like, params)
    totals, (output, input_grad, state_grad, window_grad) = lax.scan(one_segment, zero_grads, (tokens, cotangent, start_state, start_window))
    first_gain_grad, recur_in_grad, conv_taps_grad, conv_bias_grad, decay_gate_grad, input_gate_grad, decay_bias_grad, input_bias_grad, decay_logit_grad, recur_out_grad, second_gain_grad, feed_in_grad, feed_out_grad = totals
    return (output, input_grad, state_grad, window_grad, first_gain_grad, recur_in_grad, conv_taps_grad, conv_bias_grad, decay_gate_grad, input_gate_grad, decay_bias_grad, input_bias_grad, decay_logit_grad, recur_out_grad, second_gain_grad, feed_in_grad, feed_out_grad)
```

```python
import jax
import jax.numpy as jnp
from jax import lax
from jax.experimental import pallas as pl
from jax.experimental.pallas import tpu as pltpu
from jax.sharding import PartitionSpec as P

EPSILON = 1e-06
RATE_SCALE = 8.0
LANES = 128
CHUNK = 64
BF = jnp.bfloat16
F32 = jnp.float32


def rms_norm(values, scale_gain):
    factor = lax.rsqrt(jnp.mean(values * values, axis=-1, keepdims=True) + EPSILON)
    return values * factor * scale_gain


def gelu_tanh(values):
    return jax.nn.gelu(values, approximate=True)


def gelu_back(values, grads):
    return jax.vjp(gelu_tanh, values)[1](grads)[0]


def contract_last(left, right):
    return lax.dot_general(left, right, (((1,), (1,)), ((), ())), preferred_element_type=F32)


def contract_first(left, right):
    return lax.dot_general(left, right, (((0,), (0,)), ((), ())), preferred_element_type=F32)


def contract(left, right):
    return jnp.dot(left, right, preferred_element_type=F32)


def conv_apply(padded, taps, offset):
    edge_rows = taps.shape[0] - 1
    length = padded.shape[-2] - edge_rows
    summed = padded[..., edge_rows:, :] * taps[0] + offset
    for back_step in range(1, taps.shape[0]):
        first = edge_rows - back_step
        summed = summed + padded[..., first : first + length, :] * taps[back_step]
    return summed


def swap(value, bit):
    return lax.ppermute(value, "seq", [(i, i ^ bit) for i in range(lax.axis_size("seq"))])


def gather_seq(value):
    half = value.shape[0] // 2
    one = swap(value, 1)
    two = swap(value, 2)
    three = jnp.concatenate([swap(one[:half], 2), swap(two[half:], 1)], axis=0)
    return value, one, two, three


def scatter_seq(blocks):
    half = blocks[0].shape[0] // 2
    low = [block.astype(BF) for block in blocks]
    from_one = swap(jnp.concatenate([low[3][:half], low[1][:half]], axis=0), 1).astype(F32)
    from_two = swap(jnp.concatenate([low[3][half:], low[2][half:]], axis=0), 2).astype(F32)
    pass_two = (blocks[2][:half] + from_one[:half]).astype(BF)
    pass_one = (blocks[1][half:] + from_two[:half]).astype(BF)
    last_two = swap(pass_two, 2).astype(F32)
    last_one = swap(pass_one, 1).astype(F32)
    top = blocks[0][:half] + from_one[half:] + last_two
    bottom = blocks[0][half:] + from_two[half:] + last_one
    return jnp.concatenate([top, bottom], axis=0)


def in_order(blocks, place):
    rows = blocks[0].shape[0]
    whole = jnp.zeros((rows * len(blocks),) + blocks[0].shape[1:], blocks[0].dtype)
    for step, block in enumerate(blocks):
        whole = lax.dynamic_update_slice_in_dim(whole, block, (place ^ step) * rows, 0)
    return whole


def neg_expm1(values):
    total = 1.0 + values * (1.0 / 9.0)
    for order in range(8, 1, -1):
        total = 1.0 + values * (1.0 / order) * total
    return jnp.where(values > -0.7, -values * total, 1.0 - jnp.exp(values))


def scan_kernel(
    blk_ref, low_ref, wd_ref, wi_ref, par_ref, conv_ref, branch_ref,
    states_ref, decay_ref, rate_ref, open_ref, mixed_ref,
):
    length = conv_ref.shape[0]
    par = par_ref[...]
    soft = par[2:3]
    row = lax.broadcasted_iota(jnp.int32, (CHUNK // 8, 8, LANES), 1)

    def body(step, carry):
        rows = pl.ds(pl.multiple_of(step * CHUNK, CHUNK), CHUNK)
        low = low_ref[rows, :]
        rate = jax.nn.sigmoid(contract(low, wd_ref[0]) + par[0:1])
        opened = jax.nn.sigmoid(contract(low, wi_ref[0]) + par[1:2])
        log_decay = -RATE_SCALE * rate * soft
        decay = jnp.exp(log_decay)
        drive = jnp.sqrt(neg_expm1(2.0 * log_decay)) * opened * conv_ref[rows, :]
        rate_ref[rows, :] = rate
        open_ref[rows, :] = opened
        decay_ref[rows, :] = decay
        prod = decay.reshape(CHUNK // 8, 8, LANES)
        total = drive.reshape(CHUNK // 8, 8, LANES)
        for shift in (1, 2, 4):
            inside = row >= shift
            moved = jnp.where(inside, pltpu.roll(total, shift, 1), 0.0)
            total = total + prod * moved
            prod = prod * jnp.where(inside, pltpu.roll(prod, shift, 1), 1.0)
        pieces = []
        for group in range(CHUNK // 8):
            piece = total[group] + prod[group] * carry
            carry = piece[7:8]
            pieces.append(piece)
        states = jnp.concatenate(pieces, axis=0)
        states_ref[rows, :] = states
        mixed_ref[rows, :] = (states * gelu_tanh(branch_ref[rows, :])).astype(BF)
        return carry

    lax.fori_loop(0, length // CHUNK, body, par[3:4])


def scan_forward(blk, conv_ext, decay_w, input_w, params, conv_out, branch_pre):
    length, width = conv_out.shape
    tiles = width // LANES
    tile = pl.BlockSpec((length, LANES), lambda i, blk: (0, i))
    weight = pl.BlockSpec((1, decay_w.shape[1], LANES), lambda i, blk: (i, 0, 0))
    whole = jax.ShapeDtypeStruct((length, width), F32)
    return pl.pallas_call(
        scan_kernel,
        grid_spec=pltpu.PrefetchScalarGridSpec(
            num_scalar_prefetch=1,
            grid=(tiles,),
            in_specs=[
                pl.BlockSpec((length, decay_w.shape[1]), lambda i, blk: (0, blk[i])),
                weight,
                weight,
                pl.BlockSpec((8, LANES), lambda i, blk: (0, i)),
                tile,
                tile,
            ],
            out_specs=[tile] * 5,
        ),
        out_shape=[whole, whole, whole, whole, jax.ShapeDtypeStruct((length, width), BF)],
        compiler_params=pltpu.CompilerParams(vmem_limit_bytes=32 * 2**20),
        cost_estimate=pl.CostEstimate(
            flops=4 * length * width * 256, bytes_accessed=length * width * 28, transcendentals=0
        ),
        name="scan_forward",
    )(blk, conv_ext, decay_w, input_w, params, conv_out, branch_pre)


def back_kernel(
    par_ref, mixed_ref, branch_ref, states_ref, decay_ref, rate_ref, open_ref, conv_ref,
    branch_out, gate_out, input_out, direct_out, sums_out,
):
    length = conv_ref.shape[0]
    groups = CHUNK // 8
    par = par_ref[...]
    soft = par[2:3]
    row = lax.broadcasted_iota(jnp.int32, (groups, 8, LANES), 1)
    flat_row = lax.broadcasted_iota(jnp.int32, (CHUNK, LANES), 0)
    steps = length // CHUNK

    def body(turn, carried):
        carry, gate_sum, input_sum, logit_sum = carried
        step = steps - 1 - turn
        first = pl.multiple_of(step * CHUNK, CHUNK)
        rows = pl.ds(first, CHUNK)
        mixed_grad = mixed_ref[rows, :]
        branch = branch_ref[rows, :]
        states = states_ref[rows, :]
        decay = decay_ref[rows, :]
        branch_act, pull = jax.vjp(gelu_tanh, branch)
        branch_out[rows, :] = pull(mixed_grad * states)[0].astype(BF)
        state_grad = mixed_grad * branch_act
        prod = decay.reshape(groups, 8, LANES)
        total = (decay * state_grad).reshape(groups, 8, LANES)
        for shift in (1, 2, 4):
            inside = row < 8 - shift
            moved = jnp.where(inside, pltpu.roll(total, 8 - shift, 1), 0.0)
            total = total + prod * moved
            prod = prod * jnp.where(inside, pltpu.roll(prod, 8 - shift, 1), 1.0)
        pieces = [None] * groups
        after = carry
        for group in reversed(range(groups)):
            piece = total[group] + prod[group] * after
            after = piece[0:1]
            pieces[group] = piece
        passed = jnp.concatenate(pieces, axis=0)
        shifted = jnp.where(flat_row == CHUNK - 1, carry, pltpu.roll(passed, CHUNK - 1, 0))
        adjoint = state_grad + shifted
        before = states_ref[pl.ds(pl.multiple_of(jnp.maximum(first - 8, 0), 8), 8), :][7:8]
        before = jnp.where(step == 0, par[3:4], before)
        previous = jnp.where(flat_row == 0, before, pltpu.roll(states, 1, 0))
        rate = rate_ref[rows, :]
        opened = open_ref[rows, :]
        conv = conv_ref[rows, :]
        log_decay = -RATE_SCALE * rate * soft
        scale = jnp.sqrt(neg_expm1(2.0 * log_decay))
        opened_conv = opened * conv
        log_grad = decay * (adjoint * previous - adjoint * opened_conv * (decay / scale))
        scaled = adjoint * scale
        direct_out[rows, :] = scaled * opened
        input_grad = (scaled * conv * opened * (1.0 - opened)).astype(BF)
        rate_grad = log_grad * rate
        gate_grad = (rate_grad * (1.0 - rate) * (-RATE_SCALE * soft)).astype(BF)
        gate_out[rows, :] = gate_grad
        input_out[rows, :] = input_grad

        def folded(value):
            return jnp.sum(value.astype(F32).reshape(groups, 8, LANES), axis=0)

        return (
            after,
            gate_sum + folded(gate_grad),
            input_sum + folded(input_grad),
            logit_sum + folded(rate_grad),
        )

    zero = jnp.zeros((8, LANES), F32)
    after, gate_sum, input_sum, logit_sum = lax.fori_loop(
        0, steps, body, (jnp.zeros((1, LANES), F32), zero, zero, zero)
    )
    sums_out[...] = jnp.concatenate(
        [
            jnp.sum(gate_sum, axis=0, keepdims=True),
            jnp.sum(input_sum, axis=0, keepdims=True),
            jnp.sum(logit_sum, axis=0, keepdims=True) * (-RATE_SCALE * par[4:5]),
            after,
            jnp.zeros((4, LANES), F32),
        ],
        axis=0,
    )


def scan_backward(params, mixed_grad, branch_pre, states, decays, rate, opened, conv_out):
    length, width = conv_out.shape
    tiles = width // LANES
    tile = pl.BlockSpec((length, LANES), lambda i: (0, i))
    small = pl.BlockSpec((8, LANES), lambda i: (0, i))
    low = jax.ShapeDtypeStruct((length, width), BF)
    return pl.pallas_call(
        back_kernel,
        grid=(tiles,),
        in_specs=[small] + [tile] * 7,
        out_specs=[tile] * 4 + [small],
        out_shape=[
            low,
            low,
            low,
            jax.ShapeDtypeStruct((length, width), F32),
            jax.ShapeDtypeStruct((8, width), F32),
        ],
        compiler_params=pltpu.CompilerParams(vmem_limit_bytes=32 * 2**20),
        cost_estimate=pl.CostEstimate(
            flops=100 * length * width, bytes_accessed=length * width * 38, transcendentals=0
        ),
        name="scan_backward",
    )(params, mixed_grad, branch_pre, states, decays, rate, opened, conv_out)


def shards(
    tokens,
    cotangent,
    start_state,
    start_window,
    first_gain,
    recur_in,
    conv_taps,
    conv_bias,
    decay_gate,
    input_gate,
    decay_bias,
    input_bias,
    decay_logit,
    recur_out,
    second_gain,
    feed_in,
    feed_out,
):
    segments, length, model_width = tokens.shape
    recur_width = conv_taps.shape[1]
    head_count, block_size = decay_gate.shape[:2]
    edge_rows = conv_taps.shape[0] - 1
    seq_parts = lax.axis_size("seq")
    place = lax.axis_index("seq")
    own_rows, _, recur_part = recur_in.shape
    feed_part = feed_in.shape[2]
    first_channel = place * recur_part
    first_block = first_channel // block_size
    block_count = -(-recur_part // block_size)
    strip = block_count * block_size - recur_part
    odd = place % 2 == 1

    def own(value):
        return lax.dynamic_slice_in_dim(value, first_channel, recur_part, value.ndim - 1)

    def spread(value):
        sent = jnp.where(odd, value[:, :strip], value[:, recur_part - strip :])
        arrived = swap(sent, 1)
        return jnp.where(
            odd,
            jnp.concatenate([arrived, value], axis=1),
            jnp.concatenate([value, arrived], axis=1),
        )

    def gather_seg(value):
        return lax.all_gather(value, "seg", axis=0, tiled=True)

    def scatter_seg(value):
        return lax.psum_scatter(value.astype(BF), "seg", scatter_dimension=0, tiled=True).astype(F32)

    full_rin = gather_seg(recur_in.reshape(own_rows, 2 * recur_part))
    full_rout = gather_seg(recur_out)
    full_fin = gather_seg(feed_in.reshape(own_rows, 2 * feed_part))
    full_fout = gather_seg(feed_out)

    inputs = tokens.astype(F32).reshape(length, model_width)
    upstream = cotangent.reshape(length, model_width)
    low1 = rms_norm(inputs, first_gain).astype(BF)
    all_low1 = in_order(gather_seq(low1), place)
    all_cot = jnp.concatenate(gather_seq(upstream), axis=0)

    taps = own(conv_taps)
    logit = own(decay_logit[None])
    params = jnp.concatenate(
        [
            own(decay_bias[None]),
            own(input_bias[None]),
            jax.nn.softplus(logit),
            own(start_state),
            jax.nn.sigmoid(logit),
            jnp.zeros((3, recur_part), F32),
        ],
        axis=0,
    )
    window = own(start_window)[0]
    decay_blocks = lax.dynamic_slice_in_dim(decay_gate, first_block, block_count, 0)
    input_blocks = lax.dynamic_slice_in_dim(input_gate, first_block, block_count, 0)
    tiles = recur_part // LANES
    halves = block_size // LANES
    first_tile = jnp.where(odd, strip // LANES, 0)

    def tiled(blocks):
        parts = blocks.reshape(block_count, block_size, halves, LANES).transpose(0, 2, 1, 3)
        parts = parts.reshape(block_count * halves, block_size, LANES)
        return lax.dynamic_slice_in_dim(parts, first_tile, tiles, 0)

    tile_block = ((first_tile + jnp.arange(tiles)) // halves).astype(jnp.int32)

    projected = contract(all_low1, full_rin)
    branch_pre = projected[:, :recur_part]
    padded = jnp.concatenate([window, projected[:, recur_part:]], axis=0)
    conv_out = conv_apply(padded, taps, own(conv_bias[None]))
    conv_ext = spread(conv_out.astype(BF))
    states, decays, rate, opened, mixed_low = scan_forward(
        tile_block, conv_ext, tiled(decay_blocks), tiled(input_blocks), params, conv_out, branch_pre
    )

    def for_places(left, right):
        return [
            contract_last(
                lax.dynamic_slice_in_dim(left, (place ^ step) * length, length, 0), right
            )
            for step in range(seq_parts)
        ]

    residual = inputs + scatter_seq(for_places(mixed_low, full_rout))

    low2 = rms_norm(residual, second_gain).astype(BF)
    all_low2 = jnp.concatenate(gather_seq(low2), axis=0)
    gate_up = contract(all_low2, full_fin)
    gate_val = gate_up[:, :feed_part]
    up_val = gate_up[:, feed_part:]
    gate_act = gelu_tanh(gate_val)
    hidden = (gate_act * up_val).astype(BF)
    hidden_grad = contract(all_cot, full_fout)
    gate_grad = gelu_back(gate_val, hidden_grad * up_val).astype(BF)
    up_grad = (hidden_grad * gate_act).astype(BF)
    gate_up_grad = jnp.concatenate([gate_grad, up_grad], axis=1)

    def rows_split(value):
        return [value[step * length : (step + 1) * length] for step in range(seq_parts)]

    normed2_grad = scatter_seq(rows_split(contract_last(gate_up_grad, full_fin)))
    mlp_out = scatter_seq(rows_split(contract_last(hidden, full_fout)))
    output = (residual + mlp_out).astype(BF).reshape(tokens.shape)
    feed_in_grad = scatter_seg(contract_first(all_low2, gate_up_grad))
    feed_out_grad = scatter_seg(contract_first(all_cot, hidden))

    residual_norm_grad, second_gain_grad = jax.vjp(rms_norm, residual, second_gain)[1](normed2_grad)
    residual_grad = upstream.astype(F32) + residual_norm_grad

    mixer_grad = in_order(gather_seq(residual_grad.astype(BF)), place)
    mixed_grad = contract(mixer_grad, full_rout)
    branch_grad, gate_low_grad, input_low_grad, conv_direct, sums = scan_backward(
        params, mixed_grad, branch_pre, states, decays, rate, opened, conv_out
    )
    gates_ext = spread(jnp.concatenate([gate_low_grad, input_low_grad], axis=0))
    all_rows = seq_parts * length

    def blocked(value):
        return value.reshape(value.shape[0], block_count, block_size)

    gate_ext, input_ext = (blocked(gates_ext[:all_rows]), blocked(gates_ext[all_rows:]))
    back_ext = (
        jnp.einsum("nhc,hbc->nhb", gate_ext, decay_blocks, preferred_element_type=F32)
        + jnp.einsum("nhc,hbc->nhb", input_ext, input_blocks, preferred_element_type=F32)
    ).reshape(all_rows, block_count * block_size)

    def own_of(ext):
        return jnp.where(odd, ext[:, strip:], ext[:, :recur_part])

    conv_back = conv_direct + own_of(back_ext)
    low_ext = blocked(conv_ext)
    gate_grads = [
        own_of(
            jnp.einsum("nhb,nhc->bhc", low_ext, ext, preferred_element_type=F32).reshape(
                block_size, block_count * block_size
            )
        )
        for ext in (gate_ext, input_ext)
    ]
    conv_pull = jax.vjp(conv_apply, padded, taps, own(conv_bias[None]))[1]
    padded_grad, taps_grad, conv_bias_grad = conv_pull(conv_back)
    conv_in_grad = padded_grad[edge_rows:].astype(BF)
    proj_grad = jnp.concatenate([branch_grad, conv_in_grad], axis=1)
    normed1_grad = scatter_seq(for_places(proj_grad, full_rin))
    input_norm_grad, first_gain_grad = jax.vjp(rms_norm, inputs, first_gain)[1](normed1_grad)
    input_grad = (residual_grad + input_norm_grad).astype(BF).reshape(tokens.shape)

    recur_in_grad = scatter_seg(contract_first(all_low1, proj_grad))
    recur_out_grad = scatter_seg(contract_first(mixer_grad, mixed_low))

    small = lax.psum(
        jnp.concatenate(gate_grads + [taps_grad, conv_bias_grad, sums[:3]], axis=0), "seg"
    )
    small = jnp.concatenate([small, sums[3:4], padded_grad[:edge_rows]], axis=0)
    small = lax.all_gather(small, "seq", axis=1, tiled=True)

    def take(first, count):
        return small[first : first + count]

    def as_blocks(value):
        return value.reshape(block_size, head_count, block_size).transpose(1, 0, 2)

    gains = lax.psum(jnp.stack([first_gain_grad, second_gain_grad]), ("seq", "seg"))
    at = 2 * block_size
    kernel_taps = conv_taps.shape[0]
    return (
        output,
        input_grad,
        take(at + kernel_taps + 4, 1),
        take(at + kernel_taps + 5, edge_rows)[None],
        gains[0],
        recur_in_grad.reshape(own_rows, 2, recur_part),
        take(at, kernel_taps),
        small[at + kernel_taps],
        as_blocks(take(0, block_size)),
        as_blocks(take(block_size, block_size)),
        small[at + kernel_taps + 1],
        small[at + kernel_taps + 2],
        small[at + kernel_taps + 3],
        recur_out_grad,
        gains[1],
        feed_in_grad.reshape(own_rows, 2, feed_part),
        feed_out_grad,
    )


def solution(mesh):
    placed = (
        P("seg", "seq", None),
        P("seg", "seq", None),
        P("seg", None),
        P("seg", None, None),
        P(),
        P("seg", None, "seq"),
        P(),
        P(),
        P(),
        P(),
        P(),
        P(),
        P(),
        P("seg", "seq"),
        P(),
        P("seg", None, "seq"),
        P("seg", "seq"),
    )
    return jax.shard_map(
        shards,
        mesh=mesh,
        in_specs=placed,
        out_specs=(
            P("seg", "seq", None),
            P("seg", "seq", None),
            P("seg", None),
            P("seg", None, None),
            P(),
            P("seg", None, "seq"),
            P(),
            P(),
            P(),
            P(),
            P(),
            P(),
            P(),
            P("seg", "seq"),
            P(),
            P("seg", None, "seq"),
            P("seg", "seq"),
        ),
        check_vma=False,
    )
```

```python
import jax
import jax.numpy as jnp
from jax import lax
from jax.experimental import pallas as pl
from jax.experimental.pallas import tpu as pltpu
from jax.sharding import PartitionSpec as P

EPSILON = 1e-06
RATE_SCALE = 8.0
LANES = 128
CHUNK = 64
BF = jnp.bfloat16
F32 = jnp.float32
ORDER = [(3, 0), (1, 0), (3, 1), (2, 1), (0, 0), (0, 1), (2, 0), (1, 1)]


def rms_norm(values, scale_gain):
    factor = lax.rsqrt(jnp.mean(values * values, axis=-1, keepdims=True) + EPSILON)
    return values * factor * scale_gain


def gelu_tanh(values):
    return jax.nn.gelu(values, approximate=True)


def gelu_back(values, grads):
    return jax.vjp(gelu_tanh, values)[1](grads)[0]


def contract_last(left, right):
    return lax.dot_general(left, right, (((1,), (1,)), ((), ())), preferred_element_type=F32)


def contract_first(left, right):
    return lax.dot_general(left, right, (((0,), (0,)), ((), ())), preferred_element_type=F32)


def contract(left, right):
    return jnp.dot(left, right, preferred_element_type=F32)


def conv_apply(padded, taps, offset):
    edge_rows = taps.shape[0] - 1
    length = padded.shape[-2] - edge_rows
    summed = padded[..., edge_rows:, :] * taps[0] + offset
    for back_step in range(1, taps.shape[0]):
        first = edge_rows - back_step
        summed = summed + padded[..., first : first + length, :] * taps[back_step]
    return summed


def swap(value, bit):
    return lax.ppermute(value, "seq", [(i, i ^ bit) for i in range(lax.axis_size("seq"))])


def gather_halves(value):
    half = value.shape[0] // 2
    one = swap(value, 1)
    two = swap(value, 2)
    return value, one, two, swap(one[:half], 2), swap(two[half:], 1)


def gather_seq(value):
    own, one, two, *three = gather_halves(value)
    return own, one, two, jnp.concatenate(three, axis=0)


def assemble_kernel(rows_ref, core_ref, own_ref, one_ref, two_ref, top_ref, bottom_ref, whole_ref, mine_ref, other_ref):
    half = top_ref.shape[0]
    blocks = {
        (0, 0): own_ref[:half], (0, 1): own_ref[half:], (1, 0): one_ref[:half], (1, 1): one_ref[half:],
        (2, 0): two_ref[:half], (2, 1): two_ref[half:], (3, 0): top_ref[...], (3, 1): bottom_ref[...],
    }
    for k, which in enumerate(ORDER):
        whole_ref[pl.ds(pl.multiple_of(rows_ref[k], half), half), :] = blocks[which]

    @pl.when(pl.program_id(1) == 0)
    def _():
        mine_ref[...] = whole_ref[...].T

    @pl.when(pl.program_id(1) == 1)
    def _():
        other_ref[...] = whole_ref[...].T


def assemble(rows, core, blocks, chips, name):
    length, width = 4 * blocks[0].shape[0], blocks[0].shape[1]
    part = width // (2 * chips)
    if part % LANES:
        return assemble_plain(rows, core, blocks, chips)

    def column(i, j, rows, core):
        return (0, 2 * i + (core[0] ^ j))

    def turned():
        return pl.BlockSpec((part, length), lambda i, j, *_: (i, 0))

    return pl.pallas_call(
        assemble_kernel,
        grid_spec=pltpu.PrefetchScalarGridSpec(
            num_scalar_prefetch=2,
            grid=(chips, 2),
            in_specs=[pl.BlockSpec((value.shape[0], part), column) for value in blocks],
            out_specs=[pl.BlockSpec((length, part), column), turned(), turned()],
        ),
        out_shape=[
            jax.ShapeDtypeStruct((length, width), BF),
            jax.ShapeDtypeStruct((width // 2, length), BF),
            jax.ShapeDtypeStruct((width // 2, length), BF),
        ],
        compiler_params=pltpu.CompilerParams(vmem_limit_bytes=32 * 2**20),
        cost_estimate=pl.CostEstimate(flops=0, bytes_accessed=6 * length * width, transcendentals=0),
        name=name,
    )(rows, core, *blocks)


def assemble_plain(rows, core, blocks, chips):
    own, one, two, top, bottom = blocks
    half = top.shape[0]
    halves = {
        (0, 0): own[:half], (0, 1): own[half:], (1, 0): one[:half], (1, 1): one[half:],
        (2, 0): two[:half], (2, 1): two[half:], (3, 0): top, (3, 1): bottom,
    }
    length, width = 8 * half, own.shape[1]
    whole = jnp.zeros((length, width), BF)
    for k, which in enumerate(ORDER):
        whole = lax.dynamic_update_slice_in_dim(whole, halves[which], rows[k], 0)
    turned = whole.T.reshape(chips, 2, width // (2 * chips), length)
    mine, other = (
        lax.dynamic_index_in_dim(turned, which, 1, False).reshape(width // 2, length)
        for which in (core[0], 1 - core[0])
    )
    return whole, mine, other


def scatter_halves(send_one, send_two, keep):
    half = send_one.shape[0] // 2
    from_one = swap(send_one, 1)
    from_two = swap(send_two, 2)
    pass_two = (keep[2 * half : 3 * half] + from_one[:half].astype(F32)).astype(BF)
    pass_one = (keep[3 * half :] + from_two[:half].astype(F32)).astype(BF)
    last_two = swap(pass_two, 2)
    last_one = swap(pass_one, 1)
    near = jnp.concatenate([from_one[half:], from_two[half:]], axis=0).astype(F32)
    far = jnp.concatenate([last_two, last_one], axis=0).astype(F32)
    return keep[: 2 * half] + near + far


def arranged_rows(place, half):
    return jnp.stack([((place ^ step) * 2 + part) * half for step, part in ORDER]).astype(jnp.int32)


def project_kernel(rows_ref, left_ref, right_ref, one_ref, two_ref, keep_ref, order_ref):
    half = left_ref.shape[0] // 8

    @pl.when(pl.program_id(0) == 0)
    def _():
        for k in range(8):
            first = pl.multiple_of(rows_ref[k], half)
            order_ref[k * half : (k + 1) * half, :] = left_ref[pl.ds(first, half), :]

    terms = contract_last(order_ref[...], right_ref[...])
    one_ref[...] = terms[: 2 * half].astype(BF)
    two_ref[...] = terms[2 * half : 4 * half].astype(BF)
    keep_ref[...] = terms[4 * half :]


def project(rows, left, right, column, name):
    length, depth = left.shape
    width = right.shape[0]
    tile = 512
    part = length // 4
    return pl.pallas_call(
        project_kernel,
        grid_spec=pltpu.PrefetchScalarGridSpec(
            num_scalar_prefetch=1,
            grid=(width // tile,),
            in_specs=[
                pl.BlockSpec((length, depth), lambda i, rows: (0, 0), pipeline_mode=pl.Buffered(1)),
                pl.BlockSpec((tile, depth), lambda i, rows: (i, column)),
            ],
            out_specs=[
                pl.BlockSpec((part, tile), lambda i, rows: (0, i)),
                pl.BlockSpec((part, tile), lambda i, rows: (0, i)),
                pl.BlockSpec((2 * part, tile), lambda i, rows: (0, i)),
                pl.BlockSpec((length, depth), lambda i, rows: (0, 0)),
            ],
        ),
        out_shape=[
            jax.ShapeDtypeStruct((part, width), BF),
            jax.ShapeDtypeStruct((part, width), BF),
            jax.ShapeDtypeStruct((2 * part, width), F32),
            jax.ShapeDtypeStruct((length, depth), BF),
        ],
        compiler_params=pltpu.CompilerParams(vmem_limit_bytes=40 * 2**20),
        cost_estimate=pl.CostEstimate(
            flops=2 * length * depth * width,
            bytes_accessed=2 * width * depth + 8 * length * width,
            transcendentals=0,
        ),
        name=name,
    )(rows, left, right)


def swap_core(value):
    return lax.ppermute(value, "seg", [(i, i ^ 1) for i in range(lax.axis_size("seg"))])


def along(value, sources, step):
    pairs = [(2 * i + core, 2 * (i + step) + core) for i in sources for core in range(2)]
    return lax.ppermute(value, "seg", pairs)


def short_chain():
    return lax.axis_size("seg") == 8


def gather_chain(block):
    if not short_chain():
        return lax.all_gather(block, "seg", axis=0, tiled=True)
    place, core = lax.axis_index("seg") // 2, lax.axis_index("seg") % 2
    up, down = [block], [block]
    for hop in range(1, 4):
        up.append(along(up[-1], range(hop - 1, 3), 1))
        down.append(along(down[-1], range(1, 5 - hop), -1))
    held = [
        block,
        jnp.where(place <= 2, down[1], up[3]),
        jnp.where(place >= 2, up[2], down[2]),
        jnp.where(place >= 1, up[1], down[3]),
    ]
    rows = block.shape[0]
    whole = jnp.zeros((8 * rows,) + block.shape[1:], block.dtype)
    for step, value in enumerate(held):
        first = ((place + step) % 4) * 2
        whole = lax.dynamic_update_slice_in_dim(whole, value, (first + core) * rows, 0)
        other = swap_core(value)
        whole = lax.dynamic_update_slice_in_dim(whole, other, (first + 1 - core) * rows, 0)
    return whole


def scatter_chain(value, stages=(None,) * 3):
    if not short_chain():
        summed = lax.psum_scatter(value.astype(BF), "seg", scatter_dimension=0, tiled=True)
        return summed.astype(F32)
    place, core = lax.axis_index("seg") // 2, lax.axis_index("seg") % 2
    rows = value.shape[0] // 8
    value = value.astype(BF).reshape(4, 2, rows, value.shape[1])

    def of_core(which):
        return lax.dynamic_index_in_dim(value, which, 1, False)

    paired = of_core(core).astype(F32) + swap_core(of_core(1 - core)).astype(F32)
    paired = paired.astype(BF)

    def block(index):
        return lax.dynamic_index_in_dim(paired, jnp.clip(index, 0, 3), 0, False)

    up = down = None
    for hop in range(1, 4):
        rising, falling = block(4 - hop + place), block(place - 4 + hop)
        stage = stages[hop - 1]
        if stage is not None and hop == 1:
            rising, falling = after(rising, stage), after(falling, stage)
        if stage is not None and hop > 1:
            up, down = after(up, stage), after(down, stage)
        if hop > 1:
            rising = (rising.astype(F32) + up.astype(F32)).astype(BF)
            falling = (falling.astype(F32) + down.astype(F32)).astype(BF)
        up = along(rising, range(hop), 1)
        down = along(falling, range(4 - hop, 4), -1)
    return block(place).astype(F32) + up.astype(F32) + down.astype(F32)


def sum_small(value):
    core = lax.axis_index("seg") % 2
    mine = lax.dynamic_index_in_dim(value, core, 0, False)
    if not short_chain():
        return lax.dynamic_index_in_dim(lax.psum(value, "seg"), core, 0, False)
    total = mine.astype(F32) + swap_core(lax.dynamic_index_in_dim(value, 1 - core, 0, False)).astype(F32)
    for bit in (2, 4):
        low = total.astype(BF)
        other = lax.ppermute(low, "seg", [(i, i ^ bit) for i in range(8)])
        total = low.astype(F32) + other.astype(F32)
    return total.astype(BF)


def sum_all(value):
    if not short_chain():
        return lax.psum(value, ("seq", "seg"))
    for axis, bits in (("seg", (1, 2, 4)), ("seq", (1, 2))):
        for bit in bits:
            pairs = [(i, i ^ bit) for i in range(lax.axis_size(axis))]
            value = value + lax.ppermute(value, axis, pairs)
    return value


def after(value, earlier):
    return lax.optimization_barrier((value, earlier))[0]


def neg_expm1(values):
    total = 1.0 + values * (1.0 / 9.0)
    for order in range(8, 1, -1):
        total = 1.0 + values * (1.0 / order) * total
    return jnp.where(values > -0.7, -values * total, 1.0 - jnp.exp(values))


def scan_kernel(
    blk_ref, low_ref, wd_ref, wi_ref, par_ref, conv_ref, branch_ref,
    states_ref, decay_ref, rate_ref, open_ref, mixed_ref,
):
    length = conv_ref.shape[0]
    par = par_ref[...]
    soft = par[2:3]
    row = lax.broadcasted_iota(jnp.int32, (CHUNK // 8, 8, LANES), 1)

    def body(step, carry):
        rows = pl.ds(pl.multiple_of(step * CHUNK, CHUNK), CHUNK)
        low = low_ref[rows, :]
        rate = jax.nn.sigmoid(contract(low, wd_ref[0]) + par[0:1])
        opened = jax.nn.sigmoid(contract(low, wi_ref[0]) + par[1:2])
        log_decay = -RATE_SCALE * rate * soft
        decay = jnp.exp(log_decay)
        drive = jnp.sqrt(neg_expm1(2.0 * log_decay)) * opened * conv_ref[rows, :]
        rate_ref[rows, :] = rate
        open_ref[rows, :] = opened
        decay_ref[rows, :] = decay
        prod = decay.reshape(CHUNK // 8, 8, LANES)
        total = drive.reshape(CHUNK // 8, 8, LANES)
        for shift in (1, 2, 4):
            inside = row >= shift
            moved = jnp.where(inside, pltpu.roll(total, shift, 1), 0.0)
            total = total + prod * moved
            prod = prod * jnp.where(inside, pltpu.roll(prod, shift, 1), 1.0)
        pieces = []
        for group in range(CHUNK // 8):
            piece = total[group] + prod[group] * carry
            carry = piece[7:8]
            pieces.append(piece)
        states = jnp.concatenate(pieces, axis=0)
        states_ref[rows, :] = states
        mixed_ref[rows, :] = (states * gelu_tanh(branch_ref[rows, :])).astype(BF)
        return carry

    lax.fori_loop(0, length // CHUNK, body, par[3:4])


def scan_forward(blk, conv_ext, decay_w, input_w, params, conv_out, projected):
    length, width = conv_out.shape
    tiles = width // LANES
    tile = pl.BlockSpec((length, LANES), lambda i, blk: (0, i))
    weight = pl.BlockSpec((1, decay_w.shape[1], LANES), lambda i, blk: (i, 0, 0))
    whole = jax.ShapeDtypeStruct((length, width), F32)
    return pl.pallas_call(
        scan_kernel,
        grid_spec=pltpu.PrefetchScalarGridSpec(
            num_scalar_prefetch=1,
            grid=(tiles,),
            in_specs=[
                pl.BlockSpec((length, decay_w.shape[1]), lambda i, blk: (0, blk[i])),
                weight,
                weight,
                pl.BlockSpec((8, LANES), lambda i, blk: (0, i)),
                tile,
                tile,
            ],
            out_specs=[tile] * 5,
        ),
        out_shape=[whole, whole, whole, whole, jax.ShapeDtypeStruct((length, width), BF)],
        compiler_params=pltpu.CompilerParams(vmem_limit_bytes=32 * 2**20),
        cost_estimate=pl.CostEstimate(
            flops=4 * length * width * 256, bytes_accessed=length * width * 28, transcendentals=0
        ),
        name="scan_forward",
    )(blk, conv_ext, decay_w, input_w, params, conv_out, projected)


def back_kernel(
    rows_ref, strip_ref, par_ref, mixer_ref, out_w_ref, branch_ref, states_ref, decay_ref, rate_ref, open_ref, conv_ref,
    proj_out, gate_out, input_out, direct_out, sums_out, strips_out, mixed_ref,
):
    length = conv_ref.shape[0]
    groups = CHUNK // 8
    par = par_ref[...]
    soft = par[2:3]
    row = lax.broadcasted_iota(jnp.int32, (groups, 8, LANES), 1)
    flat_row = lax.broadcasted_iota(jnp.int32, (CHUNK, LANES), 0)
    steps = length // CHUNK
    half = length // 8
    mixed = contract(mixer_ref[...], out_w_ref[...])
    for k in range(8):
        mixed_ref[pl.ds(pl.multiple_of(rows_ref[k], half), half), :] = mixed[k * half : (k + 1) * half]

    def body(turn, carried):
        carry, gate_sum, input_sum, logit_sum = carried
        step = steps - 1 - turn
        first = pl.multiple_of(step * CHUNK, CHUNK)
        rows = pl.ds(first, CHUNK)
        mixed_grad = mixed_ref[rows, :]
        branch = branch_ref[rows, :]
        states = states_ref[rows, :]
        decay = decay_ref[rows, :]
        branch_act, pull = jax.vjp(gelu_tanh, branch)
        proj_out[rows, :] = pull(mixed_grad * states)[0].astype(BF)
        state_grad = mixed_grad * branch_act
        prod = decay.reshape(groups, 8, LANES)
        total = (decay * state_grad).reshape(groups, 8, LANES)
        for shift in (1, 2, 4):
            inside = row < 8 - shift
            moved = jnp.where(inside, pltpu.roll(total, 8 - shift, 1), 0.0)
            total = total + prod * moved
            prod = prod * jnp.where(inside, pltpu.roll(prod, 8 - shift, 1), 1.0)
        pieces = [None] * groups
        after = carry
        for group in reversed(range(groups)):
            piece = total[group] + prod[group] * after
            after = piece[0:1]
            pieces[group] = piece
        passed = jnp.concatenate(pieces, axis=0)
        shifted = jnp.where(flat_row == CHUNK - 1, carry, pltpu.roll(passed, CHUNK - 1, 0))
        adjoint = state_grad + shifted
        before = states_ref[pl.ds(pl.multiple_of(jnp.maximum(first - 8, 0), 8), 8), :][7:8]
        before = jnp.where(step == 0, par[3:4], before)
        previous = jnp.where(flat_row == 0, before, pltpu.roll(states, 1, 0))
        rate = rate_ref[rows, :]
        opened = open_ref[rows, :]
        conv = conv_ref[rows, :]
        log_decay = -RATE_SCALE * rate * soft
        scale = jnp.sqrt(neg_expm1(2.0 * log_decay))
        opened_conv = opened * conv
        log_grad = decay * (adjoint * previous - adjoint * opened_conv * (decay / scale))
        scaled = adjoint * scale
        direct_out[rows, :] = scaled * opened
        input_grad = (scaled * conv * opened * (1.0 - opened)).astype(BF)
        rate_grad = log_grad * rate
        gate_grad = (rate_grad * (1.0 - rate) * (-RATE_SCALE * soft)).astype(BF)
        gate_out[rows, :] = gate_grad
        input_out[rows, :] = input_grad

        def folded(value):
            return jnp.sum(value.astype(F32).reshape(groups, 8, LANES), axis=0)

        return (
            after,
            gate_sum + folded(gate_grad),
            input_sum + folded(input_grad),
            logit_sum + folded(rate_grad),
        )

    zero = jnp.zeros((8, LANES), F32)
    after, gate_sum, input_sum, logit_sum = lax.fori_loop(
        0, steps, body, (jnp.zeros((1, LANES), F32), zero, zero, zero)
    )
    sums_out[...] = jnp.concatenate(
        [
            jnp.sum(gate_sum, axis=0, keepdims=True),
            jnp.sum(input_sum, axis=0, keepdims=True),
            jnp.sum(logit_sum, axis=0, keepdims=True) * (-RATE_SCALE * par[4:5]),
            after,
            jnp.zeros((4, LANES), F32),
        ],
        axis=0,
    )

    @pl.when(pl.program_id(0) == strip_ref[0])
    def _():
        strips_out[0] = gate_out[...]
        strips_out[1] = input_out[...]


def scan_backward(rows, strip_tile, params, mixer_grad, recur, projected, states, decays, rate, opened, conv_out):
    length, width = conv_out.shape
    tiles = width // LANES
    out_tile = recur.shape[1] // LANES - tiles
    tile = pl.BlockSpec((length, LANES), lambda i, *_: (0, i))
    small = pl.BlockSpec((8, LANES), lambda i, *_: (0, i))
    low = jax.ShapeDtypeStruct((length, width), BF)
    return pl.pallas_call(
        back_kernel,
        grid_spec=pltpu.PrefetchScalarGridSpec(
            num_scalar_prefetch=2,
            grid=(tiles,),
            in_specs=[
                small,
                pl.BlockSpec(mixer_grad.shape, lambda i, *_: (0, 0), pipeline_mode=pl.Buffered(1)),
                pl.BlockSpec((recur.shape[0], LANES), lambda i, *_: (0, out_tile + i)),
            ]
            + [tile] * 6,
            out_specs=[tile] * 4 + [small, pl.BlockSpec((2, length, LANES), lambda i, *_: (0, 0, 0))],
            scratch_shapes=[pltpu.VMEM((length, LANES), F32)],
        ),
        out_shape=[
            jax.ShapeDtypeStruct((length, 2 * width), BF),
            low,
            low,
            jax.ShapeDtypeStruct((length, width), F32),
            jax.ShapeDtypeStruct((8, width), F32),
            jax.ShapeDtypeStruct((2, length, LANES), BF),
        ],
        compiler_params=pltpu.CompilerParams(vmem_limit_bytes=40 * 2**20),
        cost_estimate=pl.CostEstimate(
            flops=2 * length * width * recur.shape[0], bytes_accessed=length * width * 44, transcendentals=0
        ),
        name="scan_backward",
    )(rows, strip_tile, params, mixer_grad, recur, projected, states, decays, rate, opened, conv_out)


def gates_kernel(
    blk_ref, near_ref, edge_ref, par_ref, sums_ref, gate_ref, gate_near, input_ref, input_near, strips_ref,
    wd_ref, wi_ref, direct_ref, low_t_ref, conv_in_ref, proj_in, proj_out, small_out, single_out,
):
    length = direct_ref.shape[0]
    block = low_t_ref.shape[0]
    edge = edge_ref[pl.program_id(0)] == 1
    gate, opened = gate_ref[...], input_ref[...]
    gate_both = jnp.concatenate([gate, jnp.where(edge, strips_ref[0], gate_near[...])], axis=1)
    input_both = jnp.concatenate([opened, jnp.where(edge, strips_ref[1], input_near[...])], axis=1)
    conv_grad = direct_ref[...] + contract_last(gate_both, wd_ref[0]) + contract_last(input_both, wi_ref[0])
    row = lax.broadcasted_iota(jnp.int32, (length, LANES), 0)
    par = par_ref[...]
    conv_in = conv_in_ref[...]
    conv_in_grad = par[0:1] * conv_grad
    tap_sums = [jnp.sum(conv_grad * conv_in, axis=0, keepdims=True)]
    for k in range(1, 4):
        moved = jnp.where(row < length - k, pltpu.roll(conv_grad, length - k, 0), 0.0)
        conv_in_grad = conv_in_grad + par[k : k + 1] * moved
        total = jnp.sum(moved * conv_in, axis=0, keepdims=True)
        for t in range(k):
            total = total + conv_grad[t : t + 1] * par[7 + t - k : 8 + t - k]
        tap_sums.append(total)
    proj_out[...] = conv_in_grad.astype(BF)
    window = []
    for s in range(3):
        total = par[3 - s : 4 - s] * conv_grad[0:1]
        for k in range(4 - s, 4):
            total = total + par[k : k + 1] * conv_grad[s - 3 + k : s - 2 + k]
        window.append(total)
    sums = sums_ref[...]
    zero = jnp.zeros((8, LANES), F32)
    vectors = jnp.concatenate(
        tap_sums + [jnp.sum(conv_grad, axis=0, keepdims=True), sums[0:3], zero], axis=0
    ).astype(BF)
    low_t = low_t_ref[...]
    small_out[0, :block, :] = contract(low_t, gate).astype(BF)
    small_out[1, :block, :] = contract(low_t, opened).astype(BF)
    small_out[0, block:, :] = vectors
    small_out[1, block:, :] = vectors
    single_out[...] = jnp.concatenate([sums[3:4]] + window + [zero, zero[:4]], axis=0).astype(BF)


def gates_backward(blk, near, edge, params, sums, gate, opened, strips, decay_w, input_w, direct, low_t, projected, proj):
    length, width = direct.shape
    tiles = width // LANES
    block = decay_w.shape[2]
    tile = pl.BlockSpec((length, LANES), lambda i, *_: (0, i))
    beside = pl.BlockSpec((length, LANES), lambda i, blk, near, edge: (0, near[i]))
    small = pl.BlockSpec((8, LANES), lambda i, *_: (0, i))
    weight = pl.BlockSpec((1, LANES, block), lambda i, *_: (i, 0, 0))
    second = pl.BlockSpec((length, LANES), lambda i, *_: (0, tiles + i))
    return pl.pallas_call(
        gates_kernel,
        grid_spec=pltpu.PrefetchScalarGridSpec(
            num_scalar_prefetch=3,
            grid=(tiles,),
            in_specs=[
                small,
                small,
                tile,
                beside,
                tile,
                beside,
                pl.BlockSpec(strips.shape, lambda i, *_: (0, 0, 0)),
                weight,
                weight,
                tile,
                pl.BlockSpec((block, length), lambda i, blk, near, edge: (blk[i], 0)),
                second,
                pl.BlockSpec(memory_space=pl.ANY),
            ],
            out_specs=[
                second,
                pl.BlockSpec((2, block + 16, LANES), lambda i, *_: (0, 0, i)),
                pl.BlockSpec((16, LANES), lambda i, *_: (0, i)),
            ],
        ),
        out_shape=[
            jax.ShapeDtypeStruct(proj.shape, BF),
            jax.ShapeDtypeStruct((2, block + 16, width), BF),
            jax.ShapeDtypeStruct((16, width), BF),
        ],
        input_output_aliases={15: 0},
        compiler_params=pltpu.CompilerParams(vmem_limit_bytes=32 * 2**20),
        cost_estimate=pl.CostEstimate(
            flops=8 * length * width * block, bytes_accessed=length * width * 20, transcendentals=0
        ),
        name="gates_backward",
    )(blk, near, edge, params, sums, gate, gate, opened, opened, strips, decay_w, input_w, direct, low_t, projected, proj)


def mlp_data(tile, low_ref, cot_ref, weight_ref):
    gate_up = contract(low_ref[...], weight_ref[:, : 2 * tile])
    hidden_grad = contract(cot_ref[...], weight_ref[:, 2 * tile :])
    gate_val, up_val = gate_up[:, :tile], gate_up[:, tile:]
    gate_act, pull = jax.vjp(gelu_tanh, gate_val)
    hidden = (gate_act * up_val).astype(BF)
    gate_grad = pull(hidden_grad * up_val)[0].astype(BF)
    up_grad = (hidden_grad * gate_act).astype(BF)
    return jnp.concatenate([gate_grad, up_grad], axis=1), hidden


def add_term(total_ref, term):
    @pl.when(pl.program_id(0) == 0)
    def _():
        total_ref[...] = term

    @pl.when(pl.program_id(0) > 0)
    def _():
        total_ref[...] += term


def give_halves(total_ref, before_ref, one_ref, two_ref, keep_ref):
    @pl.when(pl.program_id(0) == pl.num_programs(0) - 1)
    def _():
        part = total_ref.shape[0] // 4
        one_ref[...] = (total_ref[:part] + before_ref[:part]).astype(BF)
        two_ref[...] = (total_ref[part : 2 * part] + before_ref[part : 2 * part]).astype(BF)
        keep_ref[...] = total_ref[2 * part :] + before_ref[2 * part :]


def mlp_first_kernel(tile, low_ref, cot_ref, weight_ref, units_ref, back_ref, out_ref):
    both, hidden = mlp_data(tile, low_ref, cot_ref, weight_ref)
    units_ref[:, : 2 * tile] = both
    units_ref[:, 2 * tile :] = hidden
    add_term(back_ref, contract_last(both, weight_ref[:, : 2 * tile]))
    add_term(out_ref, contract_last(hidden, weight_ref[:, 2 * tile :]))


def mlp_last_kernel(tile, low_ref, cot_ref, weight_ref, before_ref, units_ref, one_ref, two_ref, keep_ref, back_ref):
    both, hidden = mlp_data(tile, low_ref, cot_ref, weight_ref)
    units_ref[:, : 2 * tile] = both
    units_ref[:, 2 * tile :] = hidden
    add_term(back_ref, contract_last(both, weight_ref[:, : 2 * tile]))
    give_halves(back_ref, before_ref, one_ref, two_ref, keep_ref)


def mlp_out_kernel(tile, weight_ref, units_ref, before_ref, one_ref, two_ref, keep_ref, out_ref):
    add_term(out_ref, contract_last(units_ref[:, 2 * tile :], weight_ref[:, 2 * tile :]))
    give_halves(out_ref, before_ref, one_ref, two_ref, keep_ref)


def mlp_grad_kernel(tile, low_ref, low_other, cot_ref, cot_other, units_ref, units_other, grad_ref):
    cut = 2 * tile
    grad_ref[:, :cut] = (
        contract(low_ref[...], units_ref[:, :cut]) + contract(low_other[...], units_other[:, :cut])
    ).astype(BF)
    grad_ref[:, cut:] = (
        contract(cot_ref[...], units_ref[:, cut:]) + contract(cot_other[...], units_other[:, cut:])
    ).astype(BF)


def recur_grad_kernel(low_ref, low_other, mixer_ref, mixer_other, proj_ref, proj_other, mixed_ref, mixed_other, grad_ref):
    step = pl.program_id(0)

    @pl.when(step < 2)
    def _():
        grad_ref[...] = (
            contract(low_ref[...], proj_ref[...]) + contract(low_other[...], proj_other[...])
        ).astype(BF)

    @pl.when(step == 2)
    def _():
        grad_ref[...] = (
            contract(mixer_ref[...], mixed_ref[...]) + contract(mixer_other[...], mixed_other[...])
        ).astype(BF)


def recur_grad(low_t, mixer_t, proj, mixed):
    depth, length = low_t[0].shape
    width = mixed[0].shape[1]
    fixed = pl.BlockSpec((depth, length), lambda i: (0, 0), pipeline_mode=pl.Buffered(1))
    moving = pl.BlockSpec((length, width), lambda i: (0, jnp.minimum(i, 1)))
    whole = pl.BlockSpec((length, width), lambda i: (0, 0))
    return pl.pallas_call(
        recur_grad_kernel,
        grid=(3,),
        in_specs=[fixed] * 4 + [moving] * 2 + [whole] * 2,
        out_specs=pl.BlockSpec((depth, width), lambda i: (0, i)),
        out_shape=jax.ShapeDtypeStruct((depth, 3 * width), BF),
        compiler_params=pltpu.CompilerParams(vmem_limit_bytes=40 * 2**20),
        cost_estimate=pl.CostEstimate(
            flops=12 * depth * length * width, bytes_accessed=6 * depth * width + 8 * depth * length, transcendentals=0
        ),
        name="recur_grad",
    )(*low_t, *mixer_t, *proj, *mixed)


def mlp_call(kernel, tile, products, rows, width, columns, fixed_in, moving_in, fixed_out, moving_out, scratch, name):
    def fixed(shape, single):
        return pl.BlockSpec(shape, lambda i: (0, 0), pipeline_mode=pl.Buffered(1) if single else None)

    def moving(shape):
        return pl.BlockSpec((shape[0], 3 * tile), lambda i: (0, i))

    return pl.pallas_call(
        lambda *refs: kernel(tile, *refs),
        grid=(columns // (3 * tile),),
        in_specs=[
            fixed(value.shape, True) if kind == "fixed" else moving(value.shape)
            for kind, value in fixed_in + moving_in
        ],
        out_specs=[moving(shape) for shape, _ in moving_out] + [fixed(shape, False) for shape, _ in fixed_out],
        out_shape=[jax.ShapeDtypeStruct(shape, kind) for shape, kind in moving_out + fixed_out],
        scratch_shapes=[pltpu.VMEM(shape, kind) for shape, kind in scratch],
        compiler_params=pltpu.CompilerParams(vmem_limit_bytes=60 * 2**20),
        cost_estimate=pl.CostEstimate(
            flops=2 * products * rows * width * columns // 3,
            bytes_accessed=4 * width * columns + 16 * rows * width,
            transcendentals=0,
        ),
        name=name,
    )(*[value for _, value in fixed_in + moving_in])


def half_shapes(rows, width):
    part = rows // 4
    return [((part, width), BF), ((part, width), BF), ((2 * part, width), F32)]


def mlp_first(tile, low2, cot, weight):
    (rows, width), columns = low2.shape, weight.shape[1]
    ins = [("fixed", low2), ("fixed", cot), ("moving", weight)]
    return mlp_call(
        mlp_first_kernel, tile, 6, rows, width, columns, ins, [],
        [((rows, width), F32)] * 2, [((rows, columns), BF)], [], "mlp_first",
    )


def mlp_last(tile, low2, cot, weight, before):
    (rows, width), columns = low2.shape, weight.shape[1]
    ins = [("fixed", low2), ("fixed", cot), ("moving", weight), ("fixed", before)]
    return mlp_call(
        mlp_last_kernel, tile, 5, rows, width, columns, ins, [],
        half_shapes(rows, width), [((rows, columns), BF)], [((rows, width), F32)], "mlp_last",
    )


def mlp_out_last(tile, weight, units, before):
    (width, columns), rows = weight.shape, units.shape[0]
    ins = [("moving", weight), ("moving", units), ("fixed", before)]
    return mlp_call(
        mlp_out_kernel, tile, 1, rows, width, columns, ins, [],
        half_shapes(rows, width), [], [((rows, width), F32)], "mlp_out",
    )


def mlp_grad(tile, low_t, cot_t, units):
    (depth, rows), columns = low_t[0].shape, units[0].shape[1]
    ins = [("fixed", value) for value in (*low_t, *cot_t)] + [("moving", value) for value in units]
    return mlp_call(
        mlp_grad_kernel, tile, 3, rows, 2 * depth, columns, ins, [],
        [], [((depth, columns), BF)], [], "mlp_grad",
    )[0]


def shards(
    tokens,
    cotangent,
    start_state,
    start_window,
    first_gain,
    recur_in,
    conv_taps,
    conv_bias,
    decay_gate,
    input_gate,
    decay_bias,
    input_bias,
    decay_logit,
    recur_out,
    second_gain,
    feed_in,
    feed_out,
):
    segments, length, model_width = tokens.shape
    recur_width = conv_taps.shape[1]
    head_count, block_size = decay_gate.shape[:2]
    edge_rows = conv_taps.shape[0] - 1
    seq_parts = lax.axis_size("seq")
    place = lax.axis_index("seq")
    own_rows, _, recur_part = recur_in.shape
    feed_part = feed_in.shape[2]
    first_channel = place * recur_part
    first_block = first_channel // block_size
    block_count = -(-recur_part // block_size)
    strip = block_count * block_size - recur_part
    odd = place % 2 == 1

    def own(value):
        return lax.dynamic_slice_in_dim(value, first_channel, recur_part, value.ndim - 1)

    def strip_of(value):
        return jnp.where(odd, value[:, :strip], value[:, recur_part - strip :])

    def gather_seg(value):
        return lax.all_gather(value, "seg", axis=0, tiled=True)

    seg_parts = lax.axis_size("seg")
    core = lax.axis_index("seg") % 2

    def scatter_rows(value):
        groups = [list(range(c, seg_parts, 2)) for c in range(2)]
        return lax.psum_scatter(value, "seg", scatter_dimension=0, tiled=True, axis_index_groups=groups)

    def gathered(value, rows, name):
        whole, mine, other = assemble(rows, core[None].astype(jnp.int32), gather_halves(value), seg_parts // 2, name)
        return whole, (mine, swap_core(other))

    def of_both(value):
        return value, swap_core(value)

    unit = 2 * LANES
    first_part = 2 * feed_part // 3 // unit * unit
    cuts = [(0, first_part), (first_part, feed_part)]

    def feed_columns(first, count):
        return [feed_in[:, 0, first : first + count], feed_in[:, 1, first : first + count], feed_out[:, first : first + count]]

    feeds = [
        jnp.concatenate([c for first in range(a, b, unit) for c in feed_columns(first, unit)], axis=1)
        for a, b in cuts
    ]
    recur = gather_seg(jnp.concatenate([recur_in[:, 0], recur_in[:, 1], recur_out], axis=1))
    feed_first = gather_seg(feeds[0])
    feed_last = gather_seg(feeds[1])

    inputs = tokens.astype(F32).reshape(length, model_width)
    upstream = cotangent.reshape(length, model_width)
    low1 = rms_norm(inputs, first_gain).astype(BF)
    rows = arranged_rows(place, length // 2)
    straight = jnp.arange(8, dtype=jnp.int32) * (length // 2)
    all_low1, low1_rows = gathered(low1, rows, "gather_low1")
    all_cot, cot_rows = gathered(upstream, straight, "gather_cot")

    taps = own(conv_taps)
    logit = own(decay_logit[None])
    params = jnp.concatenate(
        [
            own(decay_bias[None]),
            own(input_bias[None]),
            jax.nn.softplus(logit),
            own(start_state),
            jax.nn.sigmoid(logit),
            jnp.zeros((3, recur_part), F32),
        ],
        axis=0,
    )
    window = own(start_window)[0]
    conv_params = jnp.concatenate([taps, window, jnp.zeros((1, recur_part), F32)], axis=0)
    tiles = recur_part // LANES
    halves = block_size // LANES
    first_tile = jnp.where(odd, strip // LANES, 0)
    tile_place = first_tile + jnp.arange(tiles)
    tile_block = (tile_place // halves).astype(jnp.int32)
    near = (tile_place ^ 1) - first_tile
    edge = ((near < 0) | (near >= tiles)).astype(jnp.int32)
    near = jnp.clip(near, 0, tiles - 1).astype(jnp.int32)
    strip_tile = jnp.where(odd, 0, tiles - 1).astype(jnp.int32)[None]

    def gate_tiles(blocks):
        blocks = lax.dynamic_slice_in_dim(blocks, first_block, block_count, 0)
        columns = blocks.reshape(block_count, block_size, halves, LANES).transpose(0, 2, 1, 3)
        columns = columns.reshape(block_count * halves, block_size, LANES)
        lines = blocks.reshape(block_count * halves, LANES, block_size)
        turned = jnp.concatenate([lines[:, :, LANES:], lines[:, :, :LANES]], axis=2)
        swapped = (jnp.arange(block_count * halves) % 2 == 1)[:, None, None]
        lines = jnp.where(swapped, turned, lines)
        return (
            lax.dynamic_slice_in_dim(columns, first_tile, tiles, 0),
            lax.dynamic_slice_in_dim(lines, first_tile, tiles, 0),
        )

    decay_columns, decay_lines = gate_tiles(decay_gate)
    input_columns, input_lines = gate_tiles(input_gate)

    projected = contract(all_low1, recur[:, : 2 * recur_part])
    padded = jnp.concatenate([window, projected[:, recur_part:]], axis=0)
    conv_out = conv_apply(padded, taps, own(conv_bias[None]))
    conv_low = conv_out.astype(BF)
    arrived = swap(strip_of(conv_low), 1)
    conv_ext = jnp.where(
        odd,
        jnp.concatenate([arrived, conv_low], axis=1),
        jnp.concatenate([conv_low, arrived], axis=1),
    )
    states, decays, rate, opened, mixed_low = scan_forward(
        tile_block, conv_ext, decay_columns, input_columns, params, conv_out, projected
    )
    *pieces, mixed_low = project(rows, mixed_low, recur, 2, "mixer_out")
    residual = inputs + scatter_halves(*pieces)

    low2 = rms_norm(residual, second_gain).astype(BF)
    all_low2, low2_rows = gathered(low2, straight, "gather_low2")
    units, back_first, out_first = mlp_first(unit, all_low2, all_cot, feed_first)
    grad_first = scatter_rows(mlp_grad(unit, low2_rows, cot_rows, of_both(units)))
    units, *pieces = mlp_last(unit, all_low2, all_cot, feed_last, back_first)
    normed2_grad = scatter_halves(*pieces)
    mlp_out = scatter_halves(*mlp_out_last(unit, feed_last, units, out_first))
    units_last = units
    output = (residual + mlp_out).astype(BF).reshape(tokens.shape)
    residual_norm_grad, second_gain_grad = jax.vjp(rms_norm, residual, second_gain)[1](normed2_grad)
    residual_grad = upstream.astype(F32) + residual_norm_grad

    mixer_grad, mixer_rows = gathered(residual_grad.astype(BF), straight, "gather_mixer")
    proj_grad, gate_low_grad, input_low_grad, conv_direct, sums, strips = scan_backward(
        rows, strip_tile, params, mixer_grad, recur, projected, states, decays, rate, opened, conv_out
    )
    proj_grad, small, single = gates_backward(
        tile_block, near, edge, conv_params, sums, gate_low_grad, input_low_grad, swap(strips, 1),
        decay_lines, input_lines, conv_direct, conv_ext.T, projected, proj_grad,
    )
    *pieces, _ = project(rows, proj_grad, recur, 0, "normed1_grad")
    grad_last = mlp_grad(unit, low2_rows, cot_rows, of_both(after(units_last, sums)))
    grad_last = scatter_rows(after(grad_last, (grad_first, pieces[2])))
    normed1_grad = scatter_halves(*pieces)
    input_norm_grad, first_gain_grad = jax.vjp(rms_norm, inputs, first_gain)[1](normed1_grad)
    input_grad = (residual_grad + input_norm_grad).astype(BF).reshape(tokens.shape)

    recur_term = recur_grad(low1_rows, mixer_rows, of_both(proj_grad), of_both(mixed_low))
    recur_sum = scatter_rows(after(recur_term, (grad_last, normed1_grad)))

    def columns_of(which):
        return jnp.concatenate(
            [
                part[:, first : first + unit]
                for part in (grad_first, grad_last)
                for first in range(which * unit, part.shape[1], 3 * unit)
            ],
            axis=1,
        ).astype(F32)

    feed_in_grad = jnp.stack([columns_of(0), columns_of(1)], axis=1)
    feed_out_grad = columns_of(2)
    recur_sum = after(recur_sum, (feed_in_grad, feed_out_grad)).astype(F32)
    recur_in_grad, recur_out_grad = recur_sum[:, : 2 * recur_part], recur_sum[:, 2 * recur_part :]

    mine = gather_seq(jnp.concatenate([sum_small(small), single], axis=0))
    swapped = [jnp.where(odd, mine[i ^ 1], mine[i]) for i in range(4)]
    mine = jnp.concatenate([jnp.where(place >= 2, swapped[i ^ 2], swapped[i]) for i in range(4)], axis=1)
    vectors = mine[block_size:].astype(F32)
    other = swap_core(mine[:block_size])

    def as_blocks(which):
        value = jnp.where(core == which, mine[:block_size], other).astype(F32)
        return value.reshape(block_size, head_count, block_size).transpose(1, 0, 2)

    gains = sum_all(jnp.stack([first_gain_grad, second_gain_grad]))
    kernel_taps = conv_taps.shape[0]
    return (
        output,
        input_grad,
        vectors[16:17],
        vectors[17 : 17 + edge_rows][None],
        gains[0],
        recur_in_grad.reshape(own_rows, 2, recur_part),
        vectors[:kernel_taps],
        vectors[kernel_taps],
        as_blocks(0),
        as_blocks(1),
        vectors[kernel_taps + 1],
        vectors[kernel_taps + 2],
        vectors[kernel_taps + 3],
        recur_out_grad,
        gains[1],
        feed_in_grad,
        feed_out_grad,
    )


def solution(mesh):
    placed = (
        P("seg", "seq", None),
        P("seg", "seq", None),
        P("seg", None),
        P("seg", None, None),
        P(),
        P("seg", None, "seq"),
        P(),
        P(),
        P(),
        P(),
        P(),
        P(),
        P(),
        P("seg", "seq"),
        P(),
        P("seg", None, "seq"),
        P("seg", "seq"),
    )
    return jax.shard_map(
        shards,
        mesh=mesh,
        in_specs=placed,
        out_specs=(
            P("seg", "seq", None),
            P("seg", "seq", None),
            P("seg", None),
            P("seg", None, None),
            P(),
            P("seg", None, "seq"),
            P(),
            P(),
            P(),
            P(),
            P(),
            P(),
            P(),
            P("seg", "seq"),
            P(),
            P("seg", None, "seq"),
            P("seg", "seq"),
        ),
        check_vma=False,
    )
```

```python
import jax
import jax.numpy as jnp
from jax import lax
from jax.experimental import pallas as pl
from jax.experimental.pallas import tpu as pltpu
from jax.sharding import PartitionSpec as P

EPSILON = 1e-06
RATE_SCALE = 8.0
LANES = 128
CHUNK = 64
BF = jnp.bfloat16
F32 = jnp.float32
ORDER = [(3, 0), (1, 0), (3, 1), (2, 1), (0, 0), (0, 1), (2, 0), (1, 1)]


def rms_norm(values, scale_gain):
    factor = lax.rsqrt(jnp.mean(values * values, axis=-1, keepdims=True) + EPSILON)
    return values * factor * scale_gain


def gelu_tanh(values):
    return jax.nn.gelu(values, approximate=True)


def gelu_back(values, grads):
    return jax.vjp(gelu_tanh, values)[1](grads)[0]


def contract_last(left, right):
    return lax.dot_general(left, right, (((1,), (1,)), ((), ())), preferred_element_type=F32)


def contract_first(left, right):
    return lax.dot_general(left, right, (((0,), (0,)), ((), ())), preferred_element_type=F32)


def contract(left, right):
    return jnp.dot(left, right, preferred_element_type=F32)


def conv_apply(padded, taps, offset):
    edge_rows = taps.shape[0] - 1
    length = padded.shape[-2] - edge_rows
    summed = padded[..., edge_rows:, :] * taps[0] + offset
    for back_step in range(1, taps.shape[0]):
        first = edge_rows - back_step
        summed = summed + padded[..., first : first + length, :] * taps[back_step]
    return summed


def swap(value, bit):
    return lax.ppermute(value, "seq", [(i, i ^ bit) for i in range(lax.axis_size("seq"))])


def gather_halves(value):
    half = value.shape[0] // 2
    one = swap(value, 1)
    two = swap(value, 2)
    return value, one, two, swap(one[:half], 2), swap(two[half:], 1)


def gather_seq(value):
    own, one, two, *three = gather_halves(value)
    return own, one, two, jnp.concatenate(three, axis=0)


def assemble_kernel(rows_ref, core_ref, own_ref, one_ref, two_ref, top_ref, bottom_ref, whole_ref, mine_ref, other_ref):
    half = top_ref.shape[0]
    blocks = {
        (0, 0): own_ref[:half], (0, 1): own_ref[half:], (1, 0): one_ref[:half], (1, 1): one_ref[half:],
        (2, 0): two_ref[:half], (2, 1): two_ref[half:], (3, 0): top_ref[...], (3, 1): bottom_ref[...],
    }
    for k, which in enumerate(ORDER):
        whole_ref[pl.ds(pl.multiple_of(rows_ref[k], half), half), :] = blocks[which]

    @pl.when(pl.program_id(1) == 0)
    def _():
        mine_ref[...] = whole_ref[...].T

    @pl.when(pl.program_id(1) == 1)
    def _():
        other_ref[...] = whole_ref[...].T


def assemble(rows, core, blocks, chips, name):
    length, width = 4 * blocks[0].shape[0], blocks[0].shape[1]
    part = width // (2 * chips)
    if part % LANES:
        return assemble_plain(rows, core, blocks, chips)

    def column(i, j, rows, core):
        return (0, 2 * i + (core[0] ^ j))

    def turned():
        return pl.BlockSpec((part, length), lambda i, j, *_: (i, 0))

    return pl.pallas_call(
        assemble_kernel,
        grid_spec=pltpu.PrefetchScalarGridSpec(
            num_scalar_prefetch=2,
            grid=(chips, 2),
            in_specs=[pl.BlockSpec((value.shape[0], part), column) for value in blocks],
            out_specs=[pl.BlockSpec((length, part), column), turned(), turned()],
        ),
        out_shape=[
            jax.ShapeDtypeStruct((length, width), BF),
            jax.ShapeDtypeStruct((width // 2, length), BF),
            jax.ShapeDtypeStruct((width // 2, length), BF),
        ],
        compiler_params=pltpu.CompilerParams(vmem_limit_bytes=32 * 2**20),
        cost_estimate=pl.CostEstimate(flops=0, bytes_accessed=6 * length * width, transcendentals=0),
        name=name,
    )(rows, core, *blocks)


def assemble_plain(rows, core, blocks, chips):
    own, one, two, top, bottom = blocks
    half = top.shape[0]
    halves = {
        (0, 0): own[:half], (0, 1): own[half:], (1, 0): one[:half], (1, 1): one[half:],
        (2, 0): two[:half], (2, 1): two[half:], (3, 0): top, (3, 1): bottom,
    }
    length, width = 8 * half, own.shape[1]
    whole = jnp.zeros((length, width), BF)
    for k, which in enumerate(ORDER):
        whole = lax.dynamic_update_slice_in_dim(whole, halves[which], rows[k], 0)
    turned = whole.T.reshape(chips, 2, width // (2 * chips), length)
    mine, other = (
        lax.dynamic_index_in_dim(turned, which, 1, False).reshape(width // 2, length)
        for which in (core[0], 1 - core[0])
    )
    return whole, mine, other


def scatter_halves(send_one, send_two, keep):
    half = send_one.shape[0] // 2
    from_one = swap(send_one, 1)
    from_two = swap(send_two, 2)
    pass_two = (keep[2 * half : 3 * half] + from_one[:half].astype(F32)).astype(BF)
    pass_one = (keep[3 * half :] + from_two[:half].astype(F32)).astype(BF)
    last_two = swap(pass_two, 2)
    last_one = swap(pass_one, 1)
    near = jnp.concatenate([from_one[half:], from_two[half:]], axis=0).astype(F32)
    far = jnp.concatenate([last_two, last_one], axis=0).astype(F32)
    return keep[: 2 * half] + near + far


def arranged_rows(place, half):
    return jnp.stack([((place ^ step) * 2 + part) * half for step, part in ORDER]).astype(jnp.int32)


def project_kernel(rows_ref, left_ref, right_ref, one_ref, two_ref, keep_ref, order_ref):
    half = left_ref.shape[0] // 8

    @pl.when(pl.program_id(0) == 0)
    def _():
        for k in range(8):
            first = pl.multiple_of(rows_ref[k], half)
            order_ref[k * half : (k + 1) * half, :] = left_ref[pl.ds(first, half), :]

    terms = contract_last(order_ref[...], right_ref[...])
    one_ref[...] = terms[: 2 * half].astype(BF)
    two_ref[...] = terms[2 * half : 4 * half].astype(BF)
    keep_ref[...] = terms[4 * half :]


def project(rows, left, right, column, name):
    length, depth = left.shape
    width = right.shape[0]
    tile = 512
    part = length // 4
    return pl.pallas_call(
        project_kernel,
        grid_spec=pltpu.PrefetchScalarGridSpec(
            num_scalar_prefetch=1,
            grid=(width // tile,),
            in_specs=[
                pl.BlockSpec((length, depth), lambda i, rows: (0, 0), pipeline_mode=pl.Buffered(1)),
                pl.BlockSpec((tile, depth), lambda i, rows: (i, column)),
            ],
            out_specs=[
                pl.BlockSpec((part, tile), lambda i, rows: (0, i)),
                pl.BlockSpec((part, tile), lambda i, rows: (0, i)),
                pl.BlockSpec((2 * part, tile), lambda i, rows: (0, i)),
                pl.BlockSpec((length, depth), lambda i, rows: (0, 0)),
            ],
        ),
        out_shape=[
            jax.ShapeDtypeStruct((part, width), BF),
            jax.ShapeDtypeStruct((part, width), BF),
            jax.ShapeDtypeStruct((2 * part, width), F32),
            jax.ShapeDtypeStruct((length, depth), BF),
        ],
        compiler_params=pltpu.CompilerParams(vmem_limit_bytes=40 * 2**20),
        cost_estimate=pl.CostEstimate(
            flops=2 * length * depth * width,
            bytes_accessed=2 * width * depth + 8 * length * width,
            transcendentals=0,
        ),
        name=name,
    )(rows, left, right)


def swap_core(value):
    return lax.ppermute(value, "seg", [(i, i ^ 1) for i in range(lax.axis_size("seg"))])


def along(value, sources, step):
    pairs = [(2 * i + core, 2 * (i + step) + core) for i in sources for core in range(2)]
    return lax.ppermute(value, "seg", pairs)


def short_chain():
    return lax.axis_size("seg") == 8


def sum_small(value, middle):
    core = lax.axis_index("seg") % 2
    mine = lax.dynamic_index_in_dim(value, core, 0, False)
    if not short_chain():
        return lax.dynamic_index_in_dim(lax.psum(value, "seg"), core, 0, False)
    total = mine.astype(F32) + swap_core(lax.dynamic_index_in_dim(value, 1 - core, 0, False)).astype(F32)
    for bit in (2, 4):
        low = total.astype(BF)
        other = lax.ppermute(low, "seg", [(i, i ^ bit) for i in range(8)])
        total = low.astype(F32) + after(other, middle).astype(F32)
    return total.astype(BF)


def sum_all(value):
    if not short_chain():
        return lax.psum(value, ("seq", "seg"))
    for axis, bits in (("seg", (1, 2, 4)), ("seq", (1, 2))):
        for bit in bits:
            pairs = [(i, i ^ bit) for i in range(lax.axis_size(axis))]
            value = value + lax.ppermute(value, axis, pairs)
    return value


def after(value, earlier):
    return lax.optimization_barrier((value, earlier))[0]


def neg_expm1(values):
    total = 1.0 + values * (1.0 / 9.0)
    for order in range(8, 1, -1):
        total = 1.0 + values * (1.0 / order) * total
    return jnp.where(values > -0.7, -values * total, 1.0 - jnp.exp(values))


def scan_kernel(
    blk_ref, low_ref, wd_ref, wi_ref, par_ref, conv_ref, branch_ref,
    states_ref, decay_ref, rate_ref, open_ref, mixed_ref,
):
    length = conv_ref.shape[0]
    par = par_ref[...]
    soft = par[2:3]
    row = lax.broadcasted_iota(jnp.int32, (CHUNK // 8, 8, LANES), 1)

    def body(step, carry):
        rows = pl.ds(pl.multiple_of(step * CHUNK, CHUNK), CHUNK)
        low = low_ref[rows, :]
        rate = jax.nn.sigmoid(contract(low, wd_ref[0]) + par[0:1])
        opened = jax.nn.sigmoid(contract(low, wi_ref[0]) + par[1:2])
        log_decay = -RATE_SCALE * rate * soft
        decay = jnp.exp(log_decay)
        drive = jnp.sqrt(neg_expm1(2.0 * log_decay)) * opened * conv_ref[rows, :]
        rate_ref[rows, :] = rate
        open_ref[rows, :] = opened
        decay_ref[rows, :] = decay
        prod = decay.reshape(CHUNK // 8, 8, LANES)
        total = drive.reshape(CHUNK // 8, 8, LANES)
        for shift in (1, 2, 4):
            inside = row >= shift
            moved = jnp.where(inside, pltpu.roll(total, shift, 1), 0.0)
            total = total + prod * moved
            prod = prod * jnp.where(inside, pltpu.roll(prod, shift, 1), 1.0)
        pieces = []
        for group in range(CHUNK // 8):
            piece = total[group] + prod[group] * carry
            carry = piece[7:8]
            pieces.append(piece)
        states = jnp.concatenate(pieces, axis=0)
        states_ref[rows, :] = states
        mixed_ref[rows, :] = (states * gelu_tanh(branch_ref[rows, :])).astype(BF)
        return carry

    lax.fori_loop(0, length // CHUNK, body, par[3:4])


def scan_forward(blk, conv_ext, decay_w, input_w, params, conv_out, projected):
    length, width = conv_out.shape
    tiles = width // LANES
    tile = pl.BlockSpec((length, LANES), lambda i, blk: (0, i))
    weight = pl.BlockSpec((1, decay_w.shape[1], LANES), lambda i, blk: (i, 0, 0))
    whole = jax.ShapeDtypeStruct((length, width), F32)
    return pl.pallas_call(
        scan_kernel,
        grid_spec=pltpu.PrefetchScalarGridSpec(
            num_scalar_prefetch=1,
            grid=(tiles,),
            in_specs=[
                pl.BlockSpec((length, decay_w.shape[1]), lambda i, blk: (0, blk[i])),
                weight,
                weight,
                pl.BlockSpec((8, LANES), lambda i, blk: (0, i)),
                tile,
                tile,
            ],
            out_specs=[tile] * 5,
        ),
        out_shape=[whole, whole, whole, whole, jax.ShapeDtypeStruct((length, width), BF)],
        compiler_params=pltpu.CompilerParams(vmem_limit_bytes=32 * 2**20),
        cost_estimate=pl.CostEstimate(
            flops=4 * length * width * 256, bytes_accessed=length * width * 28, transcendentals=0
        ),
        name="scan_forward",
    )(blk, conv_ext, decay_w, input_w, params, conv_out, projected)


def back_kernel(
    rows_ref, strip_ref, par_ref, mixer_ref, out_w_ref, branch_ref, states_ref, decay_ref, rate_ref, open_ref, conv_ref,
    proj_out, gate_out, input_out, direct_out, sums_out, strips_out, mixed_ref,
):
    length = conv_ref.shape[0]
    groups = CHUNK // 8
    par = par_ref[...]
    soft = par[2:3]
    row = lax.broadcasted_iota(jnp.int32, (groups, 8, LANES), 1)
    flat_row = lax.broadcasted_iota(jnp.int32, (CHUNK, LANES), 0)
    steps = length // CHUNK
    half = length // 8
    mixed = contract(mixer_ref[...], out_w_ref[...])
    for k in range(8):
        mixed_ref[pl.ds(pl.multiple_of(rows_ref[k], half), half), :] = mixed[k * half : (k + 1) * half]

    def body(turn, carried):
        carry, gate_sum, input_sum, logit_sum = carried
        step = steps - 1 - turn
        first = pl.multiple_of(step * CHUNK, CHUNK)
        rows = pl.ds(first, CHUNK)
        mixed_grad = mixed_ref[rows, :]
        branch = branch_ref[rows, :]
        states = states_ref[rows, :]
        decay = decay_ref[rows, :]
        branch_act, pull = jax.vjp(gelu_tanh, branch)
        proj_out[rows, :] = pull(mixed_grad * states)[0].astype(BF)
        state_grad = mixed_grad * branch_act
        prod = decay.reshape(groups, 8, LANES)
        total = (decay * state_grad).reshape(groups, 8, LANES)
        for shift in (1, 2, 4):
            inside = row < 8 - shift
            moved = jnp.where(inside, pltpu.roll(total, 8 - shift, 1), 0.0)
            total = total + prod * moved
            prod = prod * jnp.where(inside, pltpu.roll(prod, 8 - shift, 1), 1.0)
        pieces = [None] * groups
        after = carry
        for group in reversed(range(groups)):
            piece = total[group] + prod[group] * after
            after = piece[0:1]
            pieces[group] = piece
        passed = jnp.concatenate(pieces, axis=0)
        shifted = jnp.where(flat_row == CHUNK - 1, carry, pltpu.roll(passed, CHUNK - 1, 0))
        adjoint = state_grad + shifted
        before = states_ref[pl.ds(pl.multiple_of(jnp.maximum(first - 8, 0), 8), 8), :][7:8]
        before = jnp.where(step == 0, par[3:4], before)
        previous = jnp.where(flat_row == 0, before, pltpu.roll(states, 1, 0))
        rate = rate_ref[rows, :]
        opened = open_ref[rows, :]
        conv = conv_ref[rows, :]
        log_decay = -RATE_SCALE * rate * soft
        scale = jnp.sqrt(neg_expm1(2.0 * log_decay))
        opened_conv = opened * conv
        log_grad = decay * (adjoint * previous - adjoint * opened_conv * (decay / scale))
        scaled = adjoint * scale
        direct_out[rows, :] = scaled * opened
        input_grad = (scaled * conv * opened * (1.0 - opened)).astype(BF)
        rate_grad = log_grad * rate
        gate_grad = (rate_grad * (1.0 - rate) * (-RATE_SCALE * soft)).astype(BF)
        gate_out[rows, :] = gate_grad
        input_out[rows, :] = input_grad

        def folded(value):
            return jnp.sum(value.astype(F32).reshape(groups, 8, LANES), axis=0)

        return (
            after,
            gate_sum + folded(gate_grad),
            input_sum + folded(input_grad),
            logit_sum + folded(rate_grad),
        )

    zero = jnp.zeros((8, LANES), F32)
    after, gate_sum, input_sum, logit_sum = lax.fori_loop(
        0, steps, body, (jnp.zeros((1, LANES), F32), zero, zero, zero)
    )
    sums_out[...] = jnp.concatenate(
        [
            jnp.sum(gate_sum, axis=0, keepdims=True),
            jnp.sum(input_sum, axis=0, keepdims=True),
            jnp.sum(logit_sum, axis=0, keepdims=True) * (-RATE_SCALE * par[4:5]),
            after,
            jnp.zeros((4, LANES), F32),
        ],
        axis=0,
    )

    @pl.when(pl.program_id(0) == strip_ref[0])
    def _():
        strips_out[0] = gate_out[...]
        strips_out[1] = input_out[...]


def scan_backward(rows, strip_tile, params, mixer_grad, recur, projected, states, decays, rate, opened, conv_out):
    length, width = conv_out.shape
    tiles = width // LANES
    out_tile = recur.shape[1] // LANES - tiles
    tile = pl.BlockSpec((length, LANES), lambda i, *_: (0, i))
    small = pl.BlockSpec((8, LANES), lambda i, *_: (0, i))
    low = jax.ShapeDtypeStruct((length, width), BF)
    return pl.pallas_call(
        back_kernel,
        grid_spec=pltpu.PrefetchScalarGridSpec(
            num_scalar_prefetch=2,
            grid=(tiles,),
            in_specs=[
                small,
                pl.BlockSpec(mixer_grad.shape, lambda i, *_: (0, 0), pipeline_mode=pl.Buffered(1)),
                pl.BlockSpec((recur.shape[0], LANES), lambda i, *_: (0, out_tile + i)),
            ]
            + [tile] * 6,
            out_specs=[tile] * 4 + [small, pl.BlockSpec((2, length, LANES), lambda i, *_: (0, 0, 0))],
            scratch_shapes=[pltpu.VMEM((length, LANES), F32)],
        ),
        out_shape=[
            jax.ShapeDtypeStruct((length, 2 * width), BF),
            low,
            low,
            jax.ShapeDtypeStruct((length, width), F32),
            jax.ShapeDtypeStruct((8, width), F32),
            jax.ShapeDtypeStruct((2, length, LANES), BF),
        ],
        compiler_params=pltpu.CompilerParams(vmem_limit_bytes=40 * 2**20),
        cost_estimate=pl.CostEstimate(
            flops=2 * length * width * recur.shape[0], bytes_accessed=length * width * 44, transcendentals=0
        ),
        name="scan_backward",
    )(rows, strip_tile, params, mixer_grad, recur, projected, states, decays, rate, opened, conv_out)


def gates_kernel(
    blk_ref, near_ref, edge_ref, par_ref, sums_ref, gate_ref, gate_near, input_ref, input_near, strips_ref,
    wd_ref, wi_ref, direct_ref, low_t_ref, conv_in_ref, proj_in, proj_out, small_out, single_out,
):
    length = direct_ref.shape[0]
    block = low_t_ref.shape[0]
    edge = edge_ref[pl.program_id(0)] == 1
    gate, opened = gate_ref[...], input_ref[...]
    gate_both = jnp.concatenate([gate, jnp.where(edge, strips_ref[0], gate_near[...])], axis=1)
    input_both = jnp.concatenate([opened, jnp.where(edge, strips_ref[1], input_near[...])], axis=1)
    conv_grad = direct_ref[...] + contract_last(gate_both, wd_ref[0]) + contract_last(input_both, wi_ref[0])
    row = lax.broadcasted_iota(jnp.int32, (length, LANES), 0)
    par = par_ref[...]
    conv_in = conv_in_ref[...]
    conv_in_grad = par[0:1] * conv_grad
    tap_sums = [jnp.sum(conv_grad * conv_in, axis=0, keepdims=True)]
    for k in range(1, 4):
        moved = jnp.where(row < length - k, pltpu.roll(conv_grad, length - k, 0), 0.0)
        conv_in_grad = conv_in_grad + par[k : k + 1] * moved
        total = jnp.sum(moved * conv_in, axis=0, keepdims=True)
        for t in range(k):
            total = total + conv_grad[t : t + 1] * par[7 + t - k : 8 + t - k]
        tap_sums.append(total)
    proj_out[...] = conv_in_grad.astype(BF)
    window = []
    for s in range(3):
        total = par[3 - s : 4 - s] * conv_grad[0:1]
        for k in range(4 - s, 4):
            total = total + par[k : k + 1] * conv_grad[s - 3 + k : s - 2 + k]
        window.append(total)
    sums = sums_ref[...]
    zero = jnp.zeros((8, LANES), F32)
    vectors = jnp.concatenate(
        tap_sums + [jnp.sum(conv_grad, axis=0, keepdims=True), sums[0:3], zero], axis=0
    ).astype(BF)
    low_t = low_t_ref[...]
    small_out[0, :block, :] = contract(low_t, gate).astype(BF)
    small_out[1, :block, :] = contract(low_t, opened).astype(BF)
    small_out[0, block:, :] = vectors
    small_out[1, block:, :] = vectors
    single_out[...] = jnp.concatenate([sums[3:4]] + window + [zero, zero[:4]], axis=0).astype(BF)


def gates_backward(blk, near, edge, params, sums, gate, opened, strips, decay_w, input_w, direct, low_t, projected, proj):
    length, width = direct.shape
    tiles = width // LANES
    block = decay_w.shape[2]
    tile = pl.BlockSpec((length, LANES), lambda i, *_: (0, i))
    beside = pl.BlockSpec((length, LANES), lambda i, blk, near, edge: (0, near[i]))
    small = pl.BlockSpec((8, LANES), lambda i, *_: (0, i))
    weight = pl.BlockSpec((1, LANES, block), lambda i, *_: (i, 0, 0))
    second = pl.BlockSpec((length, LANES), lambda i, *_: (0, tiles + i))
    return pl.pallas_call(
        gates_kernel,
        grid_spec=pltpu.PrefetchScalarGridSpec(
            num_scalar_prefetch=3,
            grid=(tiles,),
            in_specs=[
                small,
                small,
                tile,
                beside,
                tile,
                beside,
                pl.BlockSpec(strips.shape, lambda i, *_: (0, 0, 0)),
                weight,
                weight,
                tile,
                pl.BlockSpec((block, length), lambda i, blk, near, edge: (blk[i], 0)),
                second,
                pl.BlockSpec(memory_space=pl.ANY),
            ],
            out_specs=[
                second,
                pl.BlockSpec((2, block + 16, LANES), lambda i, *_: (0, 0, i)),
                pl.BlockSpec((16, LANES), lambda i, *_: (0, i)),
            ],
        ),
        out_shape=[
            jax.ShapeDtypeStruct(proj.shape, BF),
            jax.ShapeDtypeStruct((2, block + 16, width), BF),
            jax.ShapeDtypeStruct((16, width), BF),
        ],
        input_output_aliases={15: 0},
        compiler_params=pltpu.CompilerParams(vmem_limit_bytes=32 * 2**20),
        cost_estimate=pl.CostEstimate(
            flops=8 * length * width * block, bytes_accessed=length * width * 20, transcendentals=0
        ),
        name="gates_backward",
    )(blk, near, edge, params, sums, gate, gate, opened, opened, strips, decay_w, input_w, direct, low_t, projected, proj)


def mlp_data(tile, low_ref, cot_ref, weight_ref):
    gate_up = contract(low_ref[...], weight_ref[:, : 2 * tile])
    hidden_grad = contract(cot_ref[...], weight_ref[:, 2 * tile :])
    gate_val, up_val = gate_up[:, :tile], gate_up[:, tile:]
    gate_act, pull = jax.vjp(gelu_tanh, gate_val)
    hidden = (gate_act * up_val).astype(BF)
    gate_grad = pull(hidden_grad * up_val)[0].astype(BF)
    up_grad = (hidden_grad * gate_act).astype(BF)
    return jnp.concatenate([gate_grad, up_grad], axis=1), hidden


def add_term(total_ref, term):
    @pl.when(pl.program_id(0) == 0)
    def _():
        total_ref[...] = term

    @pl.when(pl.program_id(0) > 0)
    def _():
        total_ref[...] += term


def give_halves(total_ref, before_ref, one_ref, two_ref, keep_ref):
    @pl.when(pl.program_id(0) == pl.num_programs(0) - 1)
    def _():
        part = total_ref.shape[0] // 4
        one_ref[...] = (total_ref[:part] + before_ref[:part]).astype(BF)
        two_ref[...] = (total_ref[part : 2 * part] + before_ref[part : 2 * part]).astype(BF)
        keep_ref[...] = total_ref[2 * part :] + before_ref[2 * part :]


def mlp_first_kernel(tile, low_ref, cot_ref, weight_ref, units_ref, back_ref, out_ref):
    both, hidden = mlp_data(tile, low_ref, cot_ref, weight_ref)
    units_ref[:, : 2 * tile] = both
    units_ref[:, 2 * tile :] = hidden
    add_term(back_ref, contract_last(both, weight_ref[:, : 2 * tile]))
    add_term(out_ref, contract_last(hidden, weight_ref[:, 2 * tile :]))


def mlp_last_kernel(tile, low_ref, cot_ref, weight_ref, before_ref, units_ref, one_ref, two_ref, keep_ref, back_ref):
    both, hidden = mlp_data(tile, low_ref, cot_ref, weight_ref)
    units_ref[:, : 2 * tile] = both
    units_ref[:, 2 * tile :] = hidden
    add_term(back_ref, contract_last(both, weight_ref[:, : 2 * tile]))
    give_halves(back_ref, before_ref, one_ref, two_ref, keep_ref)


def mlp_out_kernel(tile, weight_ref, units_ref, before_ref, one_ref, two_ref, keep_ref, out_ref):
    add_term(out_ref, contract_last(units_ref[:, 2 * tile :], weight_ref[:, 2 * tile :]))
    give_halves(out_ref, before_ref, one_ref, two_ref, keep_ref)


def mlp_grad_kernel(tile, low_ref, low_other, cot_ref, cot_other, units_ref, units_other, grad_ref):
    cut = 2 * tile
    grad_ref[:, :cut] = (
        contract(low_ref[...], units_ref[:, :cut]) + contract(low_other[...], units_other[:, :cut])
    ).astype(BF)
    grad_ref[:, cut:] = (
        contract(cot_ref[...], units_ref[:, cut:]) + contract(cot_other[...], units_other[:, cut:])
    ).astype(BF)


def recur_grad_kernel(
    low_ref, low_other, mixer_ref, mixer_other, proj_ref, proj_other, mixed_ref, mixed_other, held_ref, grad_ref
):
    step = pl.program_id(0)

    @pl.when(step < 2)
    def _():
        grad_ref[...] = (
            contract(low_ref[...], proj_ref[...]) + contract(low_other[...], proj_other[...])
        ).astype(BF)

    @pl.when(step == 2)
    def _():
        grad_ref[...] = (
            contract(mixer_ref[...], mixed_ref[...]) + contract(mixer_other[...], mixed_other[...])
        ).astype(BF)


def recur_grad(low_t, mixer_t, proj, mixed, held):
    depth, length = low_t[0].shape
    width = mixed[0].shape[1]
    fixed = pl.BlockSpec((depth, length), lambda i: (0, 0), pipeline_mode=pl.Buffered(1))
    moving = pl.BlockSpec((length, width), lambda i: (0, jnp.minimum(i, 1)))
    whole = pl.BlockSpec((length, width), lambda i: (0, 0))
    return pl.pallas_call(
        recur_grad_kernel,
        grid=(3,),
        in_specs=[fixed] * 4 + [moving] * 2 + [whole] * 2 + [pl.BlockSpec(memory_space=pl.ANY)],
        out_specs=pl.BlockSpec((depth, width), lambda i: (0, i)),
        out_shape=jax.ShapeDtypeStruct(held.shape, BF),
        input_output_aliases={8: 0},
        compiler_params=pltpu.CompilerParams(vmem_limit_bytes=40 * 2**20),
        cost_estimate=pl.CostEstimate(
            flops=12 * depth * length * width, bytes_accessed=6 * depth * width + 8 * depth * length, transcendentals=0
        ),
        name="recur_grad",
    )(*low_t, *mixer_t, *proj, *mixed, held)


def mlp_grad_beside_kernel(
    tile, first, low_ref, low_other, cot_ref, cot_other, units_ref, units_other, held_ref, grad_ref, sem
):
    mlp_grad_kernel(tile, low_ref, low_other, cot_ref, cot_other, units_ref, units_other, grad_ref)
    columns = pl.ds(pl.multiple_of(first + pl.program_id(0) * 3 * tile, LANES), 3 * tile)
    copy = pltpu.make_async_copy(grad_ref, held_ref.at[:, columns], sem)
    copy.start()
    copy.wait()


def mlp_grad_beside(tile, low_t, cot_t, units, first):
    (depth, rows), columns = low_t[0].shape, units[0].shape[1]
    fixed = pl.BlockSpec((depth, rows), lambda i: (0, 0), pipeline_mode=pl.Buffered(1))
    moving = pl.BlockSpec((rows, 3 * tile), lambda i: (0, i))
    return pl.pallas_call(
        lambda *refs: mlp_grad_beside_kernel(tile, first, *refs),
        grid=(columns // (3 * tile),),
        in_specs=[fixed] * 4 + [moving] * 2,
        out_specs=pl.BlockSpec(memory_space=pl.ANY),
        out_shape=jax.ShapeDtypeStruct((depth, first + columns), BF),
        scratch_shapes=[pltpu.VMEM((depth, 3 * tile), BF), pltpu.SemaphoreType.DMA],
        compiler_params=pltpu.CompilerParams(vmem_limit_bytes=40 * 2**20),
        cost_estimate=pl.CostEstimate(
            flops=4 * rows * depth * columns, bytes_accessed=2 * depth * columns + 8 * rows * depth, transcendentals=0
        ),
        name="mlp_grad_last",
    )(*low_t, *cot_t, *units)


def unpack_kernel(tile, first, sums_ref, in_held, out_held, feed_in_ref, feed_out_ref, recur_in_ref, recur_out_ref):
    width = recur_out_ref.shape[1]
    for i in range(2):
        recur_in_ref[:, i, :] = sums_ref[:, i * width : (i + 1) * width].astype(F32)
    recur_out_ref[...] = sums_ref[:, 2 * width : 3 * width].astype(F32)
    for k in range(feed_out_ref.shape[1] // tile):
        at = slice(k * tile, (k + 1) * tile)
        start = first + 3 * tile * k
        for i in range(2):
            feed_in_ref[:, i, at] = sums_ref[:, start + i * tile : start + (i + 1) * tile].astype(F32)
        feed_out_ref[:, at] = sums_ref[:, start + 2 * tile : start + 3 * tile].astype(F32)


def unpack(tile, sums, feed_in, feed_out, recur_width, done):
    rows = sums.shape[0]
    units = feed_out.shape[1]
    part = units - done
    anywhere = pl.BlockSpec(memory_space=pl.ANY)
    return pl.pallas_call(
        lambda *refs: unpack_kernel(tile, 3 * recur_width, *refs),
        grid=(1,),
        in_specs=[pl.BlockSpec(sums.shape, lambda i: (0, 0)), anywhere, anywhere],
        out_specs=[
            pl.BlockSpec((rows, 2, part), lambda i: (0, 0, done // part)),
            pl.BlockSpec((rows, part), lambda i: (0, done // part)),
            pl.BlockSpec((rows, 2, recur_width), lambda i: (0, 0, 0)),
            pl.BlockSpec((rows, recur_width), lambda i: (0, 0)),
        ],
        out_shape=[
            jax.ShapeDtypeStruct(feed_in.shape, F32),
            jax.ShapeDtypeStruct(feed_out.shape, F32),
            jax.ShapeDtypeStruct((rows, 2, recur_width), F32),
            jax.ShapeDtypeStruct((rows, recur_width), F32),
        ],
        input_output_aliases={1: 0, 2: 1},
        compiler_params=pltpu.CompilerParams(vmem_limit_bytes=40 * 2**20),
        cost_estimate=pl.CostEstimate(flops=0, bytes_accessed=6 * rows * sums.shape[1], transcendentals=0),
        name="unpack",
    )(sums, feed_in, feed_out)


def mlp_call(kernel, tile, products, rows, width, columns, fixed_in, moving_in, fixed_out, moving_out, scratch, name):
    def fixed(shape, single):
        return pl.BlockSpec(shape, lambda i: (0, 0), pipeline_mode=pl.Buffered(1) if single else None)

    def moving(shape):
        return pl.BlockSpec((shape[0], 3 * tile), lambda i: (0, i))

    return pl.pallas_call(
        lambda *refs: kernel(tile, *refs),
        grid=(columns // (3 * tile),),
        in_specs=[
            fixed(value.shape, True) if kind == "fixed" else moving(value.shape)
            for kind, value in fixed_in + moving_in
        ],
        out_specs=[moving(shape) for shape, _ in moving_out] + [fixed(shape, False) for shape, _ in fixed_out],
        out_shape=[jax.ShapeDtypeStruct(shape, kind) for shape, kind in moving_out + fixed_out],
        scratch_shapes=[pltpu.VMEM(shape, kind) for shape, kind in scratch],
        compiler_params=pltpu.CompilerParams(vmem_limit_bytes=60 * 2**20),
        cost_estimate=pl.CostEstimate(
            flops=2 * products * rows * width * columns // 3,
            bytes_accessed=4 * width * columns + 16 * rows * width,
            transcendentals=0,
        ),
        name=name,
    )(*[value for _, value in fixed_in + moving_in])


def half_shapes(rows, width):
    part = rows // 4
    return [((part, width), BF), ((part, width), BF), ((2 * part, width), F32)]


def mlp_first(tile, low2, cot, weight):
    (rows, width), columns = low2.shape, weight.shape[1]
    ins = [("fixed", low2), ("fixed", cot), ("moving", weight)]
    return mlp_call(
        mlp_first_kernel, tile, 6, rows, width, columns, ins, [],
        [((rows, width), F32)] * 2, [((rows, columns), BF)], [], "mlp_first",
    )


def mlp_last(tile, low2, cot, weight, before):
    (rows, width), columns = low2.shape, weight.shape[1]
    ins = [("fixed", low2), ("fixed", cot), ("moving", weight), ("fixed", before)]
    return mlp_call(
        mlp_last_kernel, tile, 5, rows, width, columns, ins, [],
        half_shapes(rows, width), [((rows, columns), BF)], [((rows, width), F32)], "mlp_last",
    )


def mlp_out_last(tile, weight, units, before):
    (width, columns), rows = weight.shape, units.shape[0]
    ins = [("moving", weight), ("moving", units), ("fixed", before)]
    return mlp_call(
        mlp_out_kernel, tile, 1, rows, width, columns, ins, [],
        half_shapes(rows, width), [], [((rows, width), F32)], "mlp_out",
    )


def mlp_grad(tile, low_t, cot_t, units):
    (depth, rows), columns = low_t[0].shape, units[0].shape[1]
    ins = [("fixed", value) for value in (*low_t, *cot_t)] + [("moving", value) for value in units]
    return mlp_call(
        mlp_grad_kernel, tile, 3, rows, 2 * depth, columns, ins, [],
        [], [((depth, columns), BF)], [], "mlp_grad",
    )[0]


def shards(
    tokens,
    cotangent,
    start_state,
    start_window,
    first_gain,
    recur_in,
    conv_taps,
    conv_bias,
    decay_gate,
    input_gate,
    decay_bias,
    input_bias,
    decay_logit,
    recur_out,
    second_gain,
    feed_in,
    feed_out,
):
    segments, length, model_width = tokens.shape
    recur_width = conv_taps.shape[1]
    head_count, block_size = decay_gate.shape[:2]
    edge_rows = conv_taps.shape[0] - 1
    seq_parts = lax.axis_size("seq")
    place = lax.axis_index("seq")
    own_rows, _, recur_part = recur_in.shape
    feed_part = feed_in.shape[2]
    first_channel = place * recur_part
    first_block = first_channel // block_size
    block_count = -(-recur_part // block_size)
    strip = block_count * block_size - recur_part
    odd = place % 2 == 1

    def own(value):
        return lax.dynamic_slice_in_dim(value, first_channel, recur_part, value.ndim - 1)

    def strip_of(value):
        return jnp.where(odd, value[:, :strip], value[:, recur_part - strip :])

    def gather_seg(value):
        return lax.all_gather(value, "seg", axis=0, tiled=True)

    seg_parts = lax.axis_size("seg")
    core = lax.axis_index("seg") % 2

    def scatter_rows(value):
        groups = [list(range(c, seg_parts, 2)) for c in range(2)]
        return lax.psum_scatter(value, "seg", scatter_dimension=0, tiled=True, axis_index_groups=groups)

    def gathered(blocks, rows, name):
        whole, mine, other = assemble(rows, core[None].astype(jnp.int32), blocks, seg_parts // 2, name)
        return whole, (mine, swap_core(other))

    def of_both(value):
        return value, swap_core(value)

    unit = 2 * LANES
    first_part = 2 * feed_part // 3 // unit * unit
    cuts = [(0, first_part), (first_part, feed_part)]

    def feed_columns(first, count):
        return [feed_in[:, 0, first : first + count], feed_in[:, 1, first : first + count], feed_out[:, first : first + count]]

    feeds = [
        jnp.concatenate([c for first in range(a, b, unit) for c in feed_columns(first, unit)], axis=1)
        for a, b in cuts
    ]
    recur = gather_seg(jnp.concatenate([recur_in[:, 0], recur_in[:, 1], recur_out], axis=1))
    feed_first = gather_seg(feeds[0])
    feed_last = gather_seg(feeds[1])

    inputs = tokens.astype(F32).reshape(length, model_width)
    upstream = cotangent.reshape(length, model_width)
    low1 = rms_norm(inputs, first_gain).astype(BF)
    rows = arranged_rows(place, length // 2)
    straight = jnp.arange(8, dtype=jnp.int32) * (length // 2)
    all_low1, low1_rows = gathered(gather_halves(low1), rows, "gather_low1")
    all_cot, cot_rows = gathered(gather_halves(upstream), straight, "gather_cot")

    taps = own(conv_taps)
    logit = own(decay_logit[None])
    params = jnp.concatenate(
        [
            own(decay_bias[None]),
            own(input_bias[None]),
            jax.nn.softplus(logit),
            own(start_state),
            jax.nn.sigmoid(logit),
            jnp.zeros((3, recur_part), F32),
        ],
        axis=0,
    )
    window = own(start_window)[0]
    conv_params = jnp.concatenate([taps, window, jnp.zeros((1, recur_part), F32)], axis=0)
    tiles = recur_part // LANES
    halves = block_size // LANES
    first_tile = jnp.where(odd, strip // LANES, 0)
    tile_place = first_tile + jnp.arange(tiles)
    tile_block = (tile_place // halves).astype(jnp.int32)
    near = (tile_place ^ 1) - first_tile
    edge = ((near < 0) | (near >= tiles)).astype(jnp.int32)
    near = jnp.clip(near, 0, tiles - 1).astype(jnp.int32)
    strip_tile = jnp.where(odd, 0, tiles - 1).astype(jnp.int32)[None]

    def gate_tiles(blocks):
        blocks = lax.dynamic_slice_in_dim(blocks, first_block, block_count, 0)
        columns = blocks.reshape(block_count, block_size, halves, LANES).transpose(0, 2, 1, 3)
        columns = columns.reshape(block_count * halves, block_size, LANES)
        lines = blocks.reshape(block_count * halves, LANES, block_size)
        turned = jnp.concatenate([lines[:, :, LANES:], lines[:, :, :LANES]], axis=2)
        swapped = (jnp.arange(block_count * halves) % 2 == 1)[:, None, None]
        lines = jnp.where(swapped, turned, lines)
        return (
            lax.dynamic_slice_in_dim(columns, first_tile, tiles, 0),
            lax.dynamic_slice_in_dim(lines, first_tile, tiles, 0),
        )

    decay_columns, decay_lines = gate_tiles(decay_gate)
    input_columns, input_lines = gate_tiles(input_gate)

    projected = contract(all_low1, recur[:, : 2 * recur_part])
    padded = jnp.concatenate([window, projected[:, recur_part:]], axis=0)
    conv_out = conv_apply(padded, taps, own(conv_bias[None]))
    conv_low = conv_out.astype(BF)
    arrived = swap(strip_of(conv_low), 1)
    conv_ext = jnp.where(
        odd,
        jnp.concatenate([arrived, conv_low], axis=1),
        jnp.concatenate([conv_low, arrived], axis=1),
    )
    states, decays, rate, opened, mixed_low = scan_forward(
        tile_block, conv_ext, decay_columns, input_columns, params, conv_out, projected
    )
    *pieces, mixed_low = project(rows, mixed_low, recur, 2, "mixer_out")
    residual = inputs + scatter_halves(*pieces)

    low2 = rms_norm(residual, second_gain).astype(BF)
    all_low2, low2_rows = gathered(gather_halves(low2), straight, "gather_low2")
    units, back_first, out_first = mlp_first(unit, all_low2, all_cot, feed_first)
    grad_first = scatter_rows(mlp_grad(unit, low2_rows, cot_rows, of_both(units)))
    units, *pieces = mlp_last(unit, all_low2, all_cot, feed_last, back_first)
    normed2_grad = scatter_halves(*pieces)
    units_last = units
    residual_norm_grad, second_gain_grad = jax.vjp(rms_norm, residual, second_gain)[1](normed2_grad)
    residual_grad = upstream.astype(F32) + residual_norm_grad

    mixer_blocks = gather_halves(residual_grad.astype(BF))
    held = mlp_grad_beside(unit, low2_rows, cot_rows, of_both(units_last), 3 * recur_part)
    mixer_grad, mixer_rows = gathered(after(mixer_blocks, held), straight, "gather_mixer")
    proj_grad, gate_low_grad, input_low_grad, conv_direct, sums, strips = scan_backward(
        rows, strip_tile, params, mixer_grad, recur, projected, states, decays, rate, opened, conv_out
    )
    proj_grad, small, single = gates_backward(
        tile_block, near, edge, conv_params, sums, gate_low_grad, input_low_grad, swap(strips, 1),
        decay_lines, input_lines, conv_direct, conv_ext.T, projected, proj_grad,
    )
    mlp_term = scatter_halves(*mlp_out_last(unit, feed_last, after(units_last, proj_grad), out_first))
    output = (residual + mlp_term).astype(BF).reshape(tokens.shape)
    grad_last_term = recur_grad(low1_rows, mixer_rows, of_both(proj_grad), of_both(mixed_low), held)
    *pieces, _ = project(rows, after(proj_grad, grad_last_term), recur, 0, "normed1_grad")
    normed1_grad = scatter_halves(*pieces)
    input_norm_grad, first_gain_grad = jax.vjp(rms_norm, inputs, first_gain)[1](normed1_grad)
    input_grad = (residual_grad + input_norm_grad).astype(BF).reshape(tokens.shape)

    grad_last = scatter_rows(after(grad_last_term, grad_first))

    def columns_of(value, which, start):
        return jnp.concatenate(
            [value[:, at : at + unit] for at in range(start + which * unit, value.shape[1], 3 * unit)], axis=1
        ).astype(F32)

    def feed_grads(value, start):
        return jnp.stack([columns_of(value, i, start) for i in range(2)], axis=1), columns_of(value, 2, start)

    feed_in_first, feed_out_first = feed_grads(grad_first, 0)
    feed_in_grad = jnp.pad(feed_in_first, ((0, 0), (0, 0), (0, feed_part - first_part)))
    feed_out_grad = jnp.pad(feed_out_first, ((0, 0), (0, feed_part - first_part)))
    grad_last = after(grad_last, (feed_in_grad, feed_out_grad))
    feed_in_grad, feed_out_grad, recur_in_grad, recur_out_grad = unpack(
        unit, grad_last, feed_in_grad, feed_out_grad, recur_part, first_part
    )

    mine = gather_seq(jnp.concatenate([sum_small(small, grad_last_term), single], axis=0))
    swapped = [jnp.where(odd, mine[i ^ 1], mine[i]) for i in range(4)]
    mine = jnp.concatenate([jnp.where(place >= 2, swapped[i ^ 2], swapped[i]) for i in range(4)], axis=1)
    vectors = mine[block_size:].astype(F32)
    other = swap_core(mine[:block_size])

    def as_blocks(which):
        value = jnp.where(core == which, mine[:block_size], other).astype(F32)
        return value.reshape(block_size, head_count, block_size).transpose(1, 0, 2)

    gains = sum_all(jnp.stack([first_gain_grad, second_gain_grad]))
    kernel_taps = conv_taps.shape[0]
    return (
        output,
        input_grad,
        vectors[16:17],
        vectors[17 : 17 + edge_rows][None],
        gains[0],
        recur_in_grad,
        vectors[:kernel_taps],
        vectors[kernel_taps],
        as_blocks(0),
        as_blocks(1),
        vectors[kernel_taps + 1],
        vectors[kernel_taps + 2],
        vectors[kernel_taps + 3],
        recur_out_grad,
        gains[1],
        feed_in_grad,
        feed_out_grad,
    )


def solution(mesh):
    placed = (
        P("seg", "seq", None),
        P("seg", "seq", None),
        P("seg", None),
        P("seg", None, None),
        P(),
        P("seg", None, "seq"),
        P(),
        P(),
        P(),
        P(),
        P(),
        P(),
        P(),
        P("seg", "seq"),
        P(),
        P("seg", None, "seq"),
        P("seg", "seq"),
    )
    return jax.shard_map(
        shards,
        mesh=mesh,
        in_specs=placed,
        out_specs=(
            P("seg", "seq", None),
            P("seg", "seq", None),
            P("seg", None),
            P("seg", None, None),
            P(),
            P("seg", None, "seq"),
            P(),
            P(),
            P(),
            P(),
            P(),
            P(),
            P(),
            P("seg", "seq"),
            P(),
            P("seg", None, "seq"),
            P("seg", "seq"),
        ),
        check_vma=False,
    )
```

```python
import jax
import jax.numpy as jnp
from jax import lax
from jax.experimental import pallas as pl
from jax.experimental.pallas import tpu as pltpu
from jax.sharding import PartitionSpec as P

EPSILON = 1e-06
RATE_SCALE = 8.0
LANES = 128
CHUNK = 64
BF = jnp.bfloat16
F32 = jnp.float32
ORDER = [(3, 0), (1, 0), (3, 1), (2, 1), (0, 0), (0, 1), (2, 0), (1, 1)]


def rms_norm(values, scale_gain):
    factor = lax.rsqrt(jnp.mean(values * values, axis=-1, keepdims=True) + EPSILON)
    return values * factor * scale_gain


def gelu_tanh(values):
    return jax.nn.gelu(values, approximate=True)


def gelu_back(values, grads):
    return jax.vjp(gelu_tanh, values)[1](grads)[0]


def contract_last(left, right):
    return lax.dot_general(left, right, (((1,), (1,)), ((), ())), preferred_element_type=F32)


def contract_first(left, right):
    return lax.dot_general(left, right, (((0,), (0,)), ((), ())), preferred_element_type=F32)


def contract(left, right):
    return jnp.dot(left, right, preferred_element_type=F32)


def conv_apply(padded, taps, offset):
    edge_rows = taps.shape[0] - 1
    length = padded.shape[-2] - edge_rows
    summed = padded[..., edge_rows:, :] * taps[0] + offset
    for back_step in range(1, taps.shape[0]):
        first = edge_rows - back_step
        summed = summed + padded[..., first : first + length, :] * taps[back_step]
    return summed


def swap(value, bit):
    return lax.ppermute(value, "seq", [(i, i ^ bit) for i in range(lax.axis_size("seq"))])


def gather_halves(value):
    half = value.shape[0] // 2
    one = swap(value, 1)
    two = swap(value, 2)
    return value, one, two, swap(one[:half], 2), swap(two[half:], 1)


def gather_seq(value):
    own, one, two, *three = gather_halves(value)
    return own, one, two, jnp.concatenate(three, axis=0)


def assemble_kernel(rows_ref, core_ref, own_ref, one_ref, two_ref, top_ref, bottom_ref, whole_ref, mine_ref, other_ref):
    half = top_ref.shape[0]
    blocks = {
        (0, 0): own_ref[:half], (0, 1): own_ref[half:], (1, 0): one_ref[:half], (1, 1): one_ref[half:],
        (2, 0): two_ref[:half], (2, 1): two_ref[half:], (3, 0): top_ref[...], (3, 1): bottom_ref[...],
    }
    for k, which in enumerate(ORDER):
        whole_ref[pl.ds(pl.multiple_of(rows_ref[k], half), half), :] = blocks[which]

    @pl.when(pl.program_id(1) == 0)
    def _():
        mine_ref[...] = whole_ref[...].T

    @pl.when(pl.program_id(1) == 1)
    def _():
        other_ref[...] = whole_ref[...].T


def assemble(rows, core, blocks, chips, name):
    length, width = 4 * blocks[0].shape[0], blocks[0].shape[1]
    part = width // (2 * chips)
    if part % LANES:
        return assemble_plain(rows, core, blocks, chips)

    def column(i, j, rows, core):
        return (0, 2 * i + (core[0] ^ j))

    def turned():
        return pl.BlockSpec((part, length), lambda i, j, *_: (i, 0))

    return pl.pallas_call(
        assemble_kernel,
        grid_spec=pltpu.PrefetchScalarGridSpec(
            num_scalar_prefetch=2,
            grid=(chips, 2),
            in_specs=[pl.BlockSpec((value.shape[0], part), column) for value in blocks],
            out_specs=[pl.BlockSpec((length, part), column), turned(), turned()],
        ),
        out_shape=[
            jax.ShapeDtypeStruct((length, width), BF),
            jax.ShapeDtypeStruct((width // 2, length), BF),
            jax.ShapeDtypeStruct((width // 2, length), BF),
        ],
        compiler_params=pltpu.CompilerParams(vmem_limit_bytes=32 * 2**20),
        cost_estimate=pl.CostEstimate(flops=0, bytes_accessed=6 * length * width, transcendentals=0),
        name=name,
    )(rows, core, *blocks)


def assemble_plain(rows, core, blocks, chips):
    own, one, two, top, bottom = blocks
    half = top.shape[0]
    halves = {
        (0, 0): own[:half], (0, 1): own[half:], (1, 0): one[:half], (1, 1): one[half:],
        (2, 0): two[:half], (2, 1): two[half:], (3, 0): top, (3, 1): bottom,
    }
    length, width = 8 * half, own.shape[1]
    whole = jnp.zeros((length, width), BF)
    for k, which in enumerate(ORDER):
        whole = lax.dynamic_update_slice_in_dim(whole, halves[which], rows[k], 0)
    turned = whole.T.reshape(chips, 2, width // (2 * chips), length)
    mine, other = (
        lax.dynamic_index_in_dim(turned, which, 1, False).reshape(width // 2, length)
        for which in (core[0], 1 - core[0])
    )
    return whole, mine, other


def scatter_halves(send_one, send_two, keep):
    half = send_one.shape[0] // 2
    from_one = swap(send_one, 1)
    from_two = swap(send_two, 2)
    pass_two = (keep[2 * half : 3 * half] + from_one[:half].astype(F32)).astype(BF)
    pass_one = (keep[3 * half :] + from_two[:half].astype(F32)).astype(BF)
    last_two = swap(pass_two, 2)
    last_one = swap(pass_one, 1)
    near = jnp.concatenate([from_one[half:], from_two[half:]], axis=0).astype(F32)
    far = jnp.concatenate([last_two, last_one], axis=0).astype(F32)
    return keep[: 2 * half] + near + far


def arranged_rows(place, half):
    return jnp.stack([((place ^ step) * 2 + part) * half for step, part in ORDER]).astype(jnp.int32)


def project_kernel(rows_ref, left_ref, right_ref, one_ref, two_ref, keep_ref, order_ref):
    half = left_ref.shape[0] // 8

    @pl.when(pl.program_id(0) == 0)
    def _():
        for k in range(8):
            first = pl.multiple_of(rows_ref[k], half)
            order_ref[k * half : (k + 1) * half, :] = left_ref[pl.ds(first, half), :]

    terms = contract_last(order_ref[...], right_ref[...])
    one_ref[...] = terms[: 2 * half].astype(BF)
    two_ref[...] = terms[2 * half : 4 * half].astype(BF)
    keep_ref[...] = terms[4 * half :]


def project(rows, left, right, column, name):
    length, depth = left.shape
    width = right.shape[0]
    tile = 512
    part = length // 4
    return pl.pallas_call(
        project_kernel,
        grid_spec=pltpu.PrefetchScalarGridSpec(
            num_scalar_prefetch=1,
            grid=(width // tile,),
            in_specs=[
                pl.BlockSpec((length, depth), lambda i, rows: (0, 0), pipeline_mode=pl.Buffered(1)),
                pl.BlockSpec((tile, depth), lambda i, rows: (i, column)),
            ],
            out_specs=[
                pl.BlockSpec((part, tile), lambda i, rows: (0, i)),
                pl.BlockSpec((part, tile), lambda i, rows: (0, i)),
                pl.BlockSpec((2 * part, tile), lambda i, rows: (0, i)),
                pl.BlockSpec((length, depth), lambda i, rows: (0, 0)),
            ],
        ),
        out_shape=[
            jax.ShapeDtypeStruct((part, width), BF),
            jax.ShapeDtypeStruct((part, width), BF),
            jax.ShapeDtypeStruct((2 * part, width), F32),
            jax.ShapeDtypeStruct((length, depth), BF),
        ],
        compiler_params=pltpu.CompilerParams(vmem_limit_bytes=40 * 2**20),
        cost_estimate=pl.CostEstimate(
            flops=2 * length * depth * width,
            bytes_accessed=2 * width * depth + 8 * length * width,
            transcendentals=0,
        ),
        name=name,
    )(rows, left, right)


def swap_core(value):
    return lax.ppermute(value, "seg", [(i, i ^ 1) for i in range(lax.axis_size("seg"))])


def along(value, sources, step):
    pairs = [(2 * i + core, 2 * (i + step) + core) for i in sources for core in range(2)]
    return lax.ppermute(value, "seg", pairs)


def short_chain():
    return lax.axis_size("seg") == 8


def sum_small(value, middle):
    core = lax.axis_index("seg") % 2
    mine = lax.dynamic_index_in_dim(value, core, 0, False)
    if not short_chain():
        return lax.dynamic_index_in_dim(lax.psum(value, "seg"), core, 0, False)
    total = mine.astype(F32) + swap_core(lax.dynamic_index_in_dim(value, 1 - core, 0, False)).astype(F32)
    rows = value.shape[1]
    cut = rows // 32 * 16
    chip = lax.axis_index("seg") // 2 % 2
    low = total.astype(BF)

    def half(which):
        return lax.dynamic_slice_in_dim(low, which * cut, rows - cut, 0)

    def exchange(value, bit):
        return lax.ppermute(value, "seg", [(i, i ^ bit) for i in range(8)])

    part = (half(chip).astype(F32) + after(exchange(half(1 - chip), 2), middle).astype(F32)).astype(BF)
    part = (part.astype(F32) + exchange(part, 4).astype(F32)).astype(BF)
    other = exchange(part, 2)
    shared = rows - 2 * cut
    return jnp.where(
        chip == 0,
        jnp.concatenate([part, other[shared:]], axis=0),
        jnp.concatenate([other, part[shared:]], axis=0),
    )


def sum_all(value):
    if not short_chain():
        return lax.psum(value, ("seq", "seg"))
    for axis, bits in (("seg", (1, 2, 4)), ("seq", (1, 2))):
        for bit in bits:
            pairs = [(i, i ^ bit) for i in range(lax.axis_size(axis))]
            value = value + lax.ppermute(value, axis, pairs)
    return value


def after(value, earlier):
    return lax.optimization_barrier((value, earlier))[0]


def neg_expm1(values):
    total = 1.0 + values * (1.0 / 9.0)
    for order in range(8, 1, -1):
        total = 1.0 + values * (1.0 / order) * total
    return jnp.where(values > -0.7, -values * total, 1.0 - jnp.exp(values))


def scan_kernel(
    blk_ref, low_ref, wd_ref, wi_ref, par_ref, conv_ref, branch_ref,
    states_ref, decay_ref, rate_ref, open_ref, mixed_ref,
):
    length = conv_ref.shape[0]
    par = par_ref[...]
    soft = par[2:3]
    row = lax.broadcasted_iota(jnp.int32, (CHUNK // 8, 8, LANES), 1)

    def body(step, carry):
        rows = pl.ds(pl.multiple_of(step * CHUNK, CHUNK), CHUNK)
        low = low_ref[rows, :]
        rate = jax.nn.sigmoid(contract(low, wd_ref[0]) + par[0:1])
        opened = jax.nn.sigmoid(contract(low, wi_ref[0]) + par[1:2])
        log_decay = -RATE_SCALE * rate * soft
        decay = jnp.exp(log_decay)
        drive = jnp.sqrt(neg_expm1(2.0 * log_decay)) * opened * conv_ref[rows, :]
        rate_ref[rows, :] = rate
        open_ref[rows, :] = opened
        decay_ref[rows, :] = decay
        prod = decay.reshape(CHUNK // 8, 8, LANES)
        total = drive.reshape(CHUNK // 8, 8, LANES)
        for shift in (1, 2, 4):
            inside = row >= shift
            moved = jnp.where(inside, pltpu.roll(total, shift, 1), 0.0)
            total = total + prod * moved
            prod = prod * jnp.where(inside, pltpu.roll(prod, shift, 1), 1.0)
        pieces = []
        for group in range(CHUNK // 8):
            piece = total[group] + prod[group] * carry
            carry = piece[7:8]
            pieces.append(piece)
        states = jnp.concatenate(pieces, axis=0)
        states_ref[rows, :] = states
        mixed_ref[rows, :] = (states * gelu_tanh(branch_ref[rows, :])).astype(BF)
        return carry

    lax.fori_loop(0, length // CHUNK, body, par[3:4])


def scan_forward(blk, conv_ext, decay_w, input_w, params, conv_out, projected):
    length, width = conv_out.shape
    tiles = width // LANES
    tile = pl.BlockSpec((length, LANES), lambda i, blk: (0, i))
    weight = pl.BlockSpec((1, decay_w.shape[1], LANES), lambda i, blk: (i, 0, 0))
    whole = jax.ShapeDtypeStruct((length, width), F32)
    return pl.pallas_call(
        scan_kernel,
        grid_spec=pltpu.PrefetchScalarGridSpec(
            num_scalar_prefetch=1,
            grid=(tiles,),
            in_specs=[
                pl.BlockSpec((length, decay_w.shape[1]), lambda i, blk: (0, blk[i])),
                weight,
                weight,
                pl.BlockSpec((8, LANES), lambda i, blk: (0, i)),
                tile,
                tile,
            ],
            out_specs=[tile] * 5,
        ),
        out_shape=[whole, whole, whole, whole, jax.ShapeDtypeStruct((length, width), BF)],
        compiler_params=pltpu.CompilerParams(vmem_limit_bytes=32 * 2**20),
        cost_estimate=pl.CostEstimate(
            flops=4 * length * width * 256, bytes_accessed=length * width * 28, transcendentals=0
        ),
        name="scan_forward",
    )(blk, conv_ext, decay_w, input_w, params, conv_out, projected)


def back_kernel(
    rows_ref, strip_ref, par_ref, mixed_in, branch_ref, states_ref, decay_ref, rate_ref, open_ref, conv_ref,
    proj_out, gate_out, input_out, direct_out, sums_out, strips_out, mixed_ref,
):
    length = conv_ref.shape[0]
    groups = CHUNK // 8
    par = par_ref[...]
    soft = par[2:3]
    row = lax.broadcasted_iota(jnp.int32, (groups, 8, LANES), 1)
    flat_row = lax.broadcasted_iota(jnp.int32, (CHUNK, LANES), 0)
    steps = length // CHUNK
    half = length // 8
    for k in range(8):
        mixed_ref[pl.ds(pl.multiple_of(rows_ref[k], half), half), :] = mixed_in[k * half : (k + 1) * half, :]

    def body(turn, carried):
        carry, gate_sum, input_sum, logit_sum = carried
        step = steps - 1 - turn
        first = pl.multiple_of(step * CHUNK, CHUNK)
        rows = pl.ds(first, CHUNK)
        mixed_grad = mixed_ref[rows, :]
        branch = branch_ref[rows, :]
        states = states_ref[rows, :]
        decay = decay_ref[rows, :]
        branch_act, pull = jax.vjp(gelu_tanh, branch)
        proj_out[rows, :] = pull(mixed_grad * states)[0].astype(BF)
        state_grad = mixed_grad * branch_act
        prod = decay.reshape(groups, 8, LANES)
        total = (decay * state_grad).reshape(groups, 8, LANES)
        for shift in (1, 2, 4):
            inside = row < 8 - shift
            moved = jnp.where(inside, pltpu.roll(total, 8 - shift, 1), 0.0)
            total = total + prod * moved
            prod = prod * jnp.where(inside, pltpu.roll(prod, 8 - shift, 1), 1.0)
        pieces = [None] * groups
        after = carry
        for group in reversed(range(groups)):
            piece = total[group] + prod[group] * after
            after = piece[0:1]
            pieces[group] = piece
        passed = jnp.concatenate(pieces, axis=0)
        shifted = jnp.where(flat_row == CHUNK - 1, carry, pltpu.roll(passed, CHUNK - 1, 0))
        adjoint = state_grad + shifted
        before = states_ref[pl.ds(pl.multiple_of(jnp.maximum(first - 8, 0), 8), 8), :][7:8]
        before = jnp.where(step == 0, par[3:4], before)
        previous = jnp.where(flat_row == 0, before, pltpu.roll(states, 1, 0))
        rate = rate_ref[rows, :]
        opened = open_ref[rows, :]
        conv = conv_ref[rows, :]
        log_decay = -RATE_SCALE * rate * soft
        scale = jnp.sqrt(neg_expm1(2.0 * log_decay))
        opened_conv = opened * conv
        log_grad = decay * (adjoint * previous - adjoint * opened_conv * (decay / scale))
        scaled = adjoint * scale
        direct_out[rows, :] = scaled * opened
        input_grad = (scaled * conv * opened * (1.0 - opened)).astype(BF)
        rate_grad = log_grad * rate
        gate_grad = (rate_grad * (1.0 - rate) * (-RATE_SCALE * soft)).astype(BF)
        gate_out[rows, :] = gate_grad
        input_out[rows, :] = input_grad

        def folded(value):
            return jnp.sum(value.astype(F32).reshape(groups, 8, LANES), axis=0)

        return (
            after,
            gate_sum + folded(gate_grad),
            input_sum + folded(input_grad),
            logit_sum + folded(rate_grad),
        )

    zero = jnp.zeros((8, LANES), F32)
    after, gate_sum, input_sum, logit_sum = lax.fori_loop(
        0, steps, body, (jnp.zeros((1, LANES), F32), zero, zero, zero)
    )
    sums_out[...] = jnp.concatenate(
        [
            jnp.sum(gate_sum, axis=0, keepdims=True),
            jnp.sum(input_sum, axis=0, keepdims=True),
            jnp.sum(logit_sum, axis=0, keepdims=True) * (-RATE_SCALE * par[4:5]),
            after,
            jnp.zeros((4, LANES), F32),
        ],
        axis=0,
    )

    @pl.when(pl.program_id(0) == strip_ref[0])
    def _():
        strips_out[0] = gate_out[...]
        strips_out[1] = input_out[...]


def scan_backward(rows, strip_tile, params, mixed_grad, projected, states, decays, rate, opened, conv_out):
    length, width = conv_out.shape
    tiles = width // LANES
    tile = pl.BlockSpec((length, LANES), lambda i, *_: (0, i))
    small = pl.BlockSpec((8, LANES), lambda i, *_: (0, i))
    low = jax.ShapeDtypeStruct((length, width), BF)
    return pl.pallas_call(
        back_kernel,
        grid_spec=pltpu.PrefetchScalarGridSpec(
            num_scalar_prefetch=2,
            grid=(tiles,),
            in_specs=[
                small,
            ]
            + [tile] * 7,
            out_specs=[tile] * 4 + [small, pl.BlockSpec((2, length, LANES), lambda i, *_: (0, 0, 0))],
            scratch_shapes=[pltpu.VMEM((length, LANES), F32)],
        ),
        out_shape=[
            jax.ShapeDtypeStruct((length, 2 * width), BF),
            low,
            low,
            jax.ShapeDtypeStruct((length, width), F32),
            jax.ShapeDtypeStruct((8, width), F32),
            jax.ShapeDtypeStruct((2, length, LANES), BF),
        ],
        compiler_params=pltpu.CompilerParams(vmem_limit_bytes=40 * 2**20),
        cost_estimate=pl.CostEstimate(
            flops=100 * length * width, bytes_accessed=length * width * 44, transcendentals=0
        ),
        name="scan_backward",
    )(rows, strip_tile, params, mixed_grad, projected, states, decays, rate, opened, conv_out)


def gates_kernel(
    blk_ref, near_ref, edge_ref, par_ref, sums_ref, gate_ref, gate_near, input_ref, input_near, strips_ref,
    wd_ref, wi_ref, direct_ref, low_t_ref, conv_in_ref, proj_in, proj_out, small_out, single_out,
):
    length = direct_ref.shape[0]
    block = low_t_ref.shape[0]
    edge = edge_ref[pl.program_id(0)] == 1
    gate, opened = gate_ref[...], input_ref[...]
    gate_both = jnp.concatenate([gate, jnp.where(edge, strips_ref[0], gate_near[...])], axis=1)
    input_both = jnp.concatenate([opened, jnp.where(edge, strips_ref[1], input_near[...])], axis=1)
    conv_grad = direct_ref[...] + contract_last(gate_both, wd_ref[0]) + contract_last(input_both, wi_ref[0])
    row = lax.broadcasted_iota(jnp.int32, (length, LANES), 0)
    par = par_ref[...]
    conv_in = conv_in_ref[...]
    conv_in_grad = par[0:1] * conv_grad
    tap_sums = [jnp.sum(conv_grad * conv_in, axis=0, keepdims=True)]
    for k in range(1, 4):
        moved = jnp.where(row < length - k, pltpu.roll(conv_grad, length - k, 0), 0.0)
        conv_in_grad = conv_in_grad + par[k : k + 1] * moved
        total = jnp.sum(moved * conv_in, axis=0, keepdims=True)
        for t in range(k):
            total = total + conv_grad[t : t + 1] * par[7 + t - k : 8 + t - k]
        tap_sums.append(total)
    proj_out[...] = conv_in_grad.astype(BF)
    window = []
    for s in range(3):
        total = par[3 - s : 4 - s] * conv_grad[0:1]
        for k in range(4 - s, 4):
            total = total + par[k : k + 1] * conv_grad[s - 3 + k : s - 2 + k]
        window.append(total)
    sums = sums_ref[...]
    zero = jnp.zeros((8, LANES), F32)
    vectors = jnp.concatenate(
        tap_sums + [jnp.sum(conv_grad, axis=0, keepdims=True), sums[0:3], zero], axis=0
    ).astype(BF)
    low_t = low_t_ref[...]
    small_out[0, :block, :] = contract(low_t, gate).astype(BF)
    small_out[1, :block, :] = contract(low_t, opened).astype(BF)
    small_out[0, block:, :] = vectors
    small_out[1, block:, :] = vectors
    single_out[...] = jnp.concatenate([sums[3:4]] + window + [zero, zero[:4]], axis=0).astype(BF)


def gates_backward(blk, near, edge, params, sums, gate, opened, strips, decay_w, input_w, direct, low_t, projected, proj):
    length, width = direct.shape
    tiles = width // LANES
    block = decay_w.shape[2]
    tile = pl.BlockSpec((length, LANES), lambda i, *_: (0, i))
    beside = pl.BlockSpec((length, LANES), lambda i, blk, near, edge: (0, near[i]))
    small = pl.BlockSpec((8, LANES), lambda i, *_: (0, i))
    weight = pl.BlockSpec((1, LANES, block), lambda i, *_: (i, 0, 0))
    second = pl.BlockSpec((length, LANES), lambda i, *_: (0, tiles + i))
    return pl.pallas_call(
        gates_kernel,
        grid_spec=pltpu.PrefetchScalarGridSpec(
            num_scalar_prefetch=3,
            grid=(tiles,),
            in_specs=[
                small,
                small,
                tile,
                beside,
                tile,
                beside,
                pl.BlockSpec(strips.shape, lambda i, *_: (0, 0, 0)),
                weight,
                weight,
                tile,
                pl.BlockSpec((block, length), lambda i, blk, near, edge: (blk[i], 0)),
                second,
                pl.BlockSpec(memory_space=pl.ANY),
            ],
            out_specs=[
                second,
                pl.BlockSpec((2, block + 16, LANES), lambda i, *_: (0, 0, i)),
                pl.BlockSpec((16, LANES), lambda i, *_: (0, i)),
            ],
        ),
        out_shape=[
            jax.ShapeDtypeStruct(proj.shape, BF),
            jax.ShapeDtypeStruct((2, block + 16, width), BF),
            jax.ShapeDtypeStruct((16, width), BF),
        ],
        input_output_aliases={15: 0},
        compiler_params=pltpu.CompilerParams(vmem_limit_bytes=32 * 2**20),
        cost_estimate=pl.CostEstimate(
            flops=8 * length * width * block, bytes_accessed=length * width * 20, transcendentals=0
        ),
        name="gates_backward",
    )(blk, near, edge, params, sums, gate, gate, opened, opened, strips, decay_w, input_w, direct, low_t, projected, proj)


def mlp_data(tile, low_ref, cot_ref, weight_ref):
    gate_up = contract(low_ref[...], weight_ref[:, : 2 * tile])
    hidden_grad = contract(cot_ref[...], weight_ref[:, 2 * tile :])
    gate_val, up_val = gate_up[:, :tile], gate_up[:, tile:]
    gate_act, pull = jax.vjp(gelu_tanh, gate_val)
    hidden = (gate_act * up_val).astype(BF)
    gate_grad = pull(hidden_grad * up_val)[0].astype(BF)
    up_grad = (hidden_grad * gate_act).astype(BF)
    return jnp.concatenate([gate_grad, up_grad], axis=1), hidden


def add_term(total_ref, term):
    @pl.when(pl.program_id(0) == 0)
    def _():
        total_ref[...] = term

    @pl.when(pl.program_id(0) > 0)
    def _():
        total_ref[...] += term


def give_halves(total_ref, before_ref, one_ref, two_ref, keep_ref):
    @pl.when(pl.program_id(0) == pl.num_programs(0) - 1)
    def _():
        part = total_ref.shape[0] // 4
        one_ref[...] = (total_ref[:part] + before_ref[:part]).astype(BF)
        two_ref[...] = (total_ref[part : 2 * part] + before_ref[part : 2 * part]).astype(BF)
        keep_ref[...] = total_ref[2 * part :] + before_ref[2 * part :]


def mlp_first_kernel(tile, low_ref, cot_ref, weight_ref, units_ref, back_ref, out_ref):
    both, hidden = mlp_data(tile, low_ref, cot_ref, weight_ref)
    units_ref[:, : 2 * tile] = both
    units_ref[:, 2 * tile :] = hidden
    add_term(back_ref, contract_last(both, weight_ref[:, : 2 * tile]))
    add_term(out_ref, contract_last(hidden, weight_ref[:, 2 * tile :]))


def mlp_last_kernel(tile, low_ref, cot_ref, weight_ref, before_ref, units_ref, one_ref, two_ref, keep_ref, back_ref):
    both, hidden = mlp_data(tile, low_ref, cot_ref, weight_ref)
    units_ref[:, : 2 * tile] = both
    units_ref[:, 2 * tile :] = hidden
    add_term(back_ref, contract_last(both, weight_ref[:, : 2 * tile]))
    give_halves(back_ref, before_ref, one_ref, two_ref, keep_ref)


def mlp_out_kernel(tile, weight_ref, units_ref, before_ref, one_ref, two_ref, keep_ref, out_ref):
    add_term(out_ref, contract_last(units_ref[:, 2 * tile :], weight_ref[:, 2 * tile :]))
    give_halves(out_ref, before_ref, one_ref, two_ref, keep_ref)


def mlp_grad_kernel(tile, low_ref, low_other, cot_ref, cot_other, units_ref, units_other, grad_ref):
    cut = 2 * tile
    grad_ref[:, :cut] = (
        contract(low_ref[...], units_ref[:, :cut]) + contract(low_other[...], units_other[:, :cut])
    ).astype(BF)
    grad_ref[:, cut:] = (
        contract(cot_ref[...], units_ref[:, cut:]) + contract(cot_other[...], units_other[:, cut:])
    ).astype(BF)


def recur_grad_kernel(
    low_ref, low_other, mixer_ref, mixer_other, proj_ref, proj_other, mixed_ref, mixed_other, held_ref, grad_ref
):
    step = pl.program_id(0)

    @pl.when(step < 2)
    def _():
        grad_ref[...] = (
            contract(low_ref[...], proj_ref[...]) + contract(low_other[...], proj_other[...])
        ).astype(BF)

    @pl.when(step == 2)
    def _():
        grad_ref[...] = (
            contract(mixer_ref[...], mixed_ref[...]) + contract(mixer_other[...], mixed_other[...])
        ).astype(BF)


def recur_grad(low_t, mixer_t, proj, mixed, held):
    depth, length = low_t[0].shape
    width = mixed[0].shape[1]
    fixed = pl.BlockSpec((depth, length), lambda i: (0, 0), pipeline_mode=pl.Buffered(1))
    moving = pl.BlockSpec((length, width), lambda i: (0, jnp.minimum(i, 1)))
    whole = pl.BlockSpec((length, width), lambda i: (0, 0))
    return pl.pallas_call(
        recur_grad_kernel,
        grid=(3,),
        in_specs=[fixed] * 4 + [moving] * 2 + [whole] * 2 + [pl.BlockSpec(memory_space=pl.ANY)],
        out_specs=pl.BlockSpec((depth, width), lambda i: (0, i)),
        out_shape=jax.ShapeDtypeStruct(held.shape, BF),
        input_output_aliases={8: 0},
        compiler_params=pltpu.CompilerParams(vmem_limit_bytes=40 * 2**20),
        cost_estimate=pl.CostEstimate(
            flops=12 * depth * length * width, bytes_accessed=6 * depth * width + 8 * depth * length, transcendentals=0
        ),
        name="recur_grad",
    )(*low_t, *mixer_t, *proj, *mixed, held)


def mlp_grad_beside_kernel(
    tile, first, low_ref, low_other, cot_ref, cot_other, units_ref, units_other, held_ref, grad_ref, sem
):
    mlp_grad_kernel(tile, low_ref, low_other, cot_ref, cot_other, units_ref, units_other, grad_ref)
    columns = pl.ds(pl.multiple_of(first + pl.program_id(0) * 3 * tile, LANES), 3 * tile)
    copy = pltpu.make_async_copy(grad_ref, held_ref.at[:, columns], sem)
    copy.start()
    copy.wait()


def mlp_grad_beside(tile, low_t, cot_t, units, first):
    (depth, rows), columns = low_t[0].shape, units[0].shape[1]
    fixed = pl.BlockSpec((depth, rows), lambda i: (0, 0), pipeline_mode=pl.Buffered(1))
    moving = pl.BlockSpec((rows, 3 * tile), lambda i: (0, i))
    return pl.pallas_call(
        lambda *refs: mlp_grad_beside_kernel(tile, first, *refs),
        grid=(columns // (3 * tile),),
        in_specs=[fixed] * 4 + [moving] * 2,
        out_specs=pl.BlockSpec(memory_space=pl.ANY),
        out_shape=jax.ShapeDtypeStruct((depth, first + columns), BF),
        scratch_shapes=[pltpu.VMEM((depth, 3 * tile), BF), pltpu.SemaphoreType.DMA],
        compiler_params=pltpu.CompilerParams(vmem_limit_bytes=40 * 2**20),
        cost_estimate=pl.CostEstimate(
            flops=4 * rows * depth * columns, bytes_accessed=2 * depth * columns + 8 * rows * depth, transcendentals=0
        ),
        name="mlp_grad_last",
    )(*low_t, *cot_t, *units)


def unpack_kernel(tile, first, sums_ref, in_held, out_held, feed_in_ref, feed_out_ref, recur_in_ref, recur_out_ref):
    width = recur_out_ref.shape[1]
    for i in range(2):
        recur_in_ref[:, i, :] = sums_ref[:, i * width : (i + 1) * width].astype(F32)
    recur_out_ref[...] = sums_ref[:, 2 * width : 3 * width].astype(F32)
    for k in range(feed_out_ref.shape[1] // tile):
        at = slice(k * tile, (k + 1) * tile)
        start = first + 3 * tile * k
        for i in range(2):
            feed_in_ref[:, i, at] = sums_ref[:, start + i * tile : start + (i + 1) * tile].astype(F32)
        feed_out_ref[:, at] = sums_ref[:, start + 2 * tile : start + 3 * tile].astype(F32)


def unpack(tile, sums, feed_in, feed_out, recur_width, done):
    rows = sums.shape[0]
    units = feed_out.shape[1]
    part = units - done
    anywhere = pl.BlockSpec(memory_space=pl.ANY)
    return pl.pallas_call(
        lambda *refs: unpack_kernel(tile, 3 * recur_width, *refs),
        grid=(1,),
        in_specs=[pl.BlockSpec(sums.shape, lambda i: (0, 0)), anywhere, anywhere],
        out_specs=[
            pl.BlockSpec((rows, 2, part), lambda i: (0, 0, done // part)),
            pl.BlockSpec((rows, part), lambda i: (0, done // part)),
            pl.BlockSpec((rows, 2, recur_width), lambda i: (0, 0, 0)),
            pl.BlockSpec((rows, recur_width), lambda i: (0, 0)),
        ],
        out_shape=[
            jax.ShapeDtypeStruct(feed_in.shape, F32),
            jax.ShapeDtypeStruct(feed_out.shape, F32),
            jax.ShapeDtypeStruct((rows, 2, recur_width), F32),
            jax.ShapeDtypeStruct((rows, recur_width), F32),
        ],
        input_output_aliases={1: 0, 2: 1},
        compiler_params=pltpu.CompilerParams(vmem_limit_bytes=40 * 2**20),
        cost_estimate=pl.CostEstimate(flops=0, bytes_accessed=6 * rows * sums.shape[1], transcendentals=0),
        name="unpack",
    )(sums, feed_in, feed_out)


def mlp_call(kernel, tile, products, rows, width, columns, fixed_in, moving_in, fixed_out, moving_out, scratch, name):
    def fixed(shape, single):
        return pl.BlockSpec(shape, lambda i: (0, 0), pipeline_mode=pl.Buffered(1) if single else None)

    def moving(shape):
        return pl.BlockSpec((shape[0], 3 * tile), lambda i: (0, i))

    return pl.pallas_call(
        lambda *refs: kernel(tile, *refs),
        grid=(columns // (3 * tile),),
        in_specs=[
            fixed(value.shape, True) if kind == "fixed" else moving(value.shape)
            for kind, value in fixed_in + moving_in
        ],
        out_specs=[moving(shape) for shape, _ in moving_out] + [fixed(shape, False) for shape, _ in fixed_out],
        out_shape=[jax.ShapeDtypeStruct(shape, kind) for shape, kind in moving_out + fixed_out],
        scratch_shapes=[pltpu.VMEM(shape, kind) for shape, kind in scratch],
        compiler_params=pltpu.CompilerParams(vmem_limit_bytes=60 * 2**20),
        cost_estimate=pl.CostEstimate(
            flops=2 * products * rows * width * columns // 3,
            bytes_accessed=4 * width * columns + 16 * rows * width,
            transcendentals=0,
        ),
        name=name,
    )(*[value for _, value in fixed_in + moving_in])


def half_shapes(rows, width):
    part = rows // 4
    return [((part, width), BF), ((part, width), BF), ((2 * part, width), F32)]


def mlp_first(tile, low2, cot, weight):
    (rows, width), columns = low2.shape, weight.shape[1]
    ins = [("fixed", low2), ("fixed", cot), ("moving", weight)]
    return mlp_call(
        mlp_first_kernel, tile, 6, rows, width, columns, ins, [],
        [((rows, width), F32)] * 2, [((rows, columns), BF)], [], "mlp_first",
    )


def mlp_last(tile, low2, cot, weight, before):
    (rows, width), columns = low2.shape, weight.shape[1]
    ins = [("fixed", low2), ("fixed", cot), ("moving", weight), ("fixed", before)]
    return mlp_call(
        mlp_last_kernel, tile, 5, rows, width, columns, ins, [],
        half_shapes(rows, width), [((rows, columns), BF)], [((rows, width), F32)], "mlp_last",
    )


def mlp_out_last(tile, weight, units, before):
    (width, columns), rows = weight.shape, units.shape[0]
    ins = [("moving", weight), ("moving", units), ("fixed", before)]
    return mlp_call(
        mlp_out_kernel, tile, 1, rows, width, columns, ins, [],
        half_shapes(rows, width), [], [((rows, width), F32)], "mlp_out",
    )


def mlp_grad(tile, low_t, cot_t, units):
    (depth, rows), columns = low_t[0].shape, units[0].shape[1]
    ins = [("fixed", value) for value in (*low_t, *cot_t)] + [("moving", value) for value in units]
    return mlp_call(
        mlp_grad_kernel, tile, 3, rows, 2 * depth, columns, ins, [],
        [], [((depth, columns), BF)], [], "mlp_grad",
    )[0]


def shards(
    tokens,
    cotangent,
    start_state,
    start_window,
    first_gain,
    recur_in,
    conv_taps,
    conv_bias,
    decay_gate,
    input_gate,
    decay_bias,
    input_bias,
    decay_logit,
    recur_out,
    second_gain,
    feed_in,
    feed_out,
):
    segments, length, model_width = tokens.shape
    recur_width = conv_taps.shape[1]
    head_count, block_size = decay_gate.shape[:2]
    edge_rows = conv_taps.shape[0] - 1
    seq_parts = lax.axis_size("seq")
    place = lax.axis_index("seq")
    own_rows, _, recur_part = recur_in.shape
    feed_part = feed_in.shape[2]
    first_channel = place * recur_part
    first_block = first_channel // block_size
    block_count = -(-recur_part // block_size)
    strip = block_count * block_size - recur_part
    odd = place % 2 == 1

    def own(value):
        return lax.dynamic_slice_in_dim(value, first_channel, recur_part, value.ndim - 1)

    def strip_of(value):
        return jnp.where(odd, value[:, :strip], value[:, recur_part - strip :])

    def gather_seg(value):
        return lax.all_gather(value, "seg", axis=0, tiled=True)

    seg_parts = lax.axis_size("seg")
    core = lax.axis_index("seg") % 2

    def scatter_rows(value):
        groups = [list(range(c, seg_parts, 2)) for c in range(2)]
        return lax.psum_scatter(value, "seg", scatter_dimension=0, tiled=True, axis_index_groups=groups)

    def gathered(blocks, rows, name):
        whole, mine, other = assemble(rows, core[None].astype(jnp.int32), blocks, seg_parts // 2, name)
        return whole, (mine, swap_core(other))

    def of_both(value):
        return value, swap_core(value)

    unit = 2 * LANES
    first_part = 2 * feed_part // 3 // unit * unit
    cuts = [(0, first_part), (first_part, feed_part)]

    def feed_columns(first, count):
        return [feed_in[:, 0, first : first + count], feed_in[:, 1, first : first + count], feed_out[:, first : first + count]]

    feeds = [
        jnp.concatenate([c for first in range(a, b, unit) for c in feed_columns(first, unit)], axis=1)
        for a, b in cuts
    ]
    recur = gather_seg(jnp.concatenate([recur_in[:, 0], recur_in[:, 1], recur_out], axis=1))
    feed_first = gather_seg(feeds[0])
    feed_last = gather_seg(feeds[1])

    inputs = tokens.astype(F32).reshape(length, model_width)
    upstream = cotangent.reshape(length, model_width)
    low1 = rms_norm(inputs, first_gain).astype(BF)
    rows = arranged_rows(place, length // 2)
    straight = jnp.arange(8, dtype=jnp.int32) * (length // 2)
    all_low1, low1_rows = gathered(gather_halves(low1), rows, "gather_low1")
    all_cot, cot_rows = gathered(gather_halves(upstream), straight, "gather_cot")

    taps = own(conv_taps)
    logit = own(decay_logit[None])
    params = jnp.concatenate(
        [
            own(decay_bias[None]),
            own(input_bias[None]),
            jax.nn.softplus(logit),
            own(start_state),
            jax.nn.sigmoid(logit),
            jnp.zeros((3, recur_part), F32),
        ],
        axis=0,
    )
    window = own(start_window)[0]
    conv_params = jnp.concatenate([taps, window, jnp.zeros((1, recur_part), F32)], axis=0)
    tiles = recur_part // LANES
    halves = block_size // LANES
    first_tile = jnp.where(odd, strip // LANES, 0)
    tile_place = first_tile + jnp.arange(tiles)
    tile_block = (tile_place // halves).astype(jnp.int32)
    near = (tile_place ^ 1) - first_tile
    edge = ((near < 0) | (near >= tiles)).astype(jnp.int32)
    near = jnp.clip(near, 0, tiles - 1).astype(jnp.int32)
    strip_tile = jnp.where(odd, 0, tiles - 1).astype(jnp.int32)[None]

    def gate_tiles(blocks):
        blocks = lax.dynamic_slice_in_dim(blocks, first_block, block_count, 0)
        columns = blocks.reshape(block_count, block_size, halves, LANES).transpose(0, 2, 1, 3)
        columns = columns.reshape(block_count * halves, block_size, LANES)
        lines = blocks.reshape(block_count * halves, LANES, block_size)
        turned = jnp.concatenate([lines[:, :, LANES:], lines[:, :, :LANES]], axis=2)
        swapped = (jnp.arange(block_count * halves) % 2 == 1)[:, None, None]
        lines = jnp.where(swapped, turned, lines)
        return (
            lax.dynamic_slice_in_dim(columns, first_tile, tiles, 0),
            lax.dynamic_slice_in_dim(lines, first_tile, tiles, 0),
        )

    decay_columns, decay_lines = gate_tiles(decay_gate)
    input_columns, input_lines = gate_tiles(input_gate)

    projected = contract(all_low1, recur[:, : 2 * recur_part])
    padded = jnp.concatenate([window, projected[:, recur_part:]], axis=0)
    conv_out = conv_apply(padded, taps, own(conv_bias[None]))
    conv_low = conv_out.astype(BF)
    arrived = swap(strip_of(conv_low), 1)
    conv_ext = jnp.where(
        odd,
        jnp.concatenate([arrived, conv_low], axis=1),
        jnp.concatenate([conv_low, arrived], axis=1),
    )
    states, decays, rate, opened, mixed_low = scan_forward(
        tile_block, conv_ext, decay_columns, input_columns, params, conv_out, projected
    )
    *pieces, mixed_low = project(rows, mixed_low, recur, 2, "mixer_out")
    residual = inputs + scatter_halves(*pieces)

    low2 = rms_norm(residual, second_gain).astype(BF)
    all_low2, low2_rows = gathered(gather_halves(low2), straight, "gather_low2")
    units, back_first, out_first = mlp_first(unit, all_low2, all_cot, feed_first)
    grad_first = scatter_rows(mlp_grad(unit, low2_rows, cot_rows, of_both(units)))
    units, *pieces = mlp_last(unit, all_low2, all_cot, feed_last, back_first)
    normed2_grad = scatter_halves(*pieces)
    units_last = units
    residual_norm_grad, second_gain_grad = jax.vjp(rms_norm, residual, second_gain)[1](normed2_grad)
    residual_grad = upstream.astype(F32) + residual_norm_grad

    mixer_blocks = gather_halves(residual_grad.astype(BF))
    held = mlp_grad_beside(unit, low2_rows, cot_rows, of_both(units_last), 3 * recur_part)
    mixer_grad, mixer_rows = gathered(after(mixer_blocks, held), straight, "gather_mixer")
    proj_grad, gate_low_grad, input_low_grad, conv_direct, sums, strips = scan_backward(
        rows, strip_tile, params, contract(mixer_grad, recur[:, 2 * recur_part :]), projected, states, decays, rate,
        opened, conv_out,
    )
    proj_grad, small, single = gates_backward(
        tile_block, near, edge, conv_params, sums, gate_low_grad, input_low_grad, swap(strips, 1),
        decay_lines, input_lines, conv_direct, conv_ext.T, projected, proj_grad,
    )
    mlp_term = scatter_halves(*mlp_out_last(unit, feed_last, after(units_last, proj_grad), out_first))
    output = (residual + mlp_term).astype(BF).reshape(tokens.shape)
    grad_last_term = recur_grad(low1_rows, mixer_rows, of_both(proj_grad), of_both(mixed_low), held)
    *pieces, _ = project(rows, after(proj_grad, grad_last_term), recur, 0, "normed1_grad")
    normed1_grad = scatter_halves(*pieces)
    input_norm_grad, first_gain_grad = jax.vjp(rms_norm, inputs, first_gain)[1](normed1_grad)
    input_grad = (residual_grad + input_norm_grad).astype(BF).reshape(tokens.shape)

    grad_last = scatter_rows(after(grad_last_term, grad_first))

    def columns_of(value, which, start):
        return jnp.concatenate(
            [value[:, at : at + unit] for at in range(start + which * unit, value.shape[1], 3 * unit)], axis=1
        ).astype(F32)

    def feed_grads(value, start):
        return jnp.stack([columns_of(value, i, start) for i in range(2)], axis=1), columns_of(value, 2, start)

    feed_in_first, feed_out_first = feed_grads(grad_first, 0)
    feed_in_grad = jnp.pad(feed_in_first, ((0, 0), (0, 0), (0, feed_part - first_part)))
    feed_out_grad = jnp.pad(feed_out_first, ((0, 0), (0, feed_part - first_part)))
    grad_last = after(grad_last, (feed_in_grad, feed_out_grad))
    feed_in_grad, feed_out_grad, recur_in_grad, recur_out_grad = unpack(
        unit, grad_last, feed_in_grad, feed_out_grad, recur_part, first_part
    )

    mine = gather_seq(jnp.concatenate([sum_small(small, grad_last_term), single], axis=0))
    swapped = [jnp.where(odd, mine[i ^ 1], mine[i]) for i in range(4)]
    mine = jnp.concatenate([jnp.where(place >= 2, swapped[i ^ 2], swapped[i]) for i in range(4)], axis=1)
    vectors = mine[block_size:].astype(F32)
    other = swap_core(mine[:block_size])

    def as_blocks(which):
        value = jnp.where(core == which, mine[:block_size], other).astype(F32)
        return value.reshape(block_size, head_count, block_size).transpose(1, 0, 2)

    gains = sum_all(jnp.stack([first_gain_grad, second_gain_grad]))
    kernel_taps = conv_taps.shape[0]
    return (
        output,
        input_grad,
        vectors[16:17],
        vectors[17 : 17 + edge_rows][None],
        gains[0],
        recur_in_grad,
        vectors[:kernel_taps],
        vectors[kernel_taps],
        as_blocks(0),
        as_blocks(1),
        vectors[kernel_taps + 1],
        vectors[kernel_taps + 2],
        vectors[kernel_taps + 3],
        recur_out_grad,
        gains[1],
        feed_in_grad,
        feed_out_grad,
    )


def solution(mesh):
    placed = (
        P("seg", "seq", None),
        P("seg", "seq", None),
        P("seg", None),
        P("seg", None, None),
        P(),
        P("seg", None, "seq"),
        P(),
        P(),
        P(),
        P(),
        P(),
        P(),
        P(),
        P("seg", "seq"),
        P(),
        P("seg", None, "seq"),
        P("seg", "seq"),
    )
    return jax.shard_map(
        shards,
        mesh=mesh,
        in_specs=placed,
        out_specs=(
            P("seg", "seq", None),
            P("seg", "seq", None),
            P("seg", None),
            P("seg", None, None),
            P(),
            P("seg", None, "seq"),
            P(),
            P(),
            P(),
            P(),
            P(),
            P(),
            P(),
            P("seg", "seq"),
            P(),
            P("seg", None, "seq"),
            P("seg", "seq"),
        ),
        check_vma=False,
    )
```

```python
import jax
import jax.numpy as jnp
from jax import lax
from jax.experimental import pallas as pl
from jax.experimental.pallas import tpu as pltpu
from jax.sharding import PartitionSpec as P

EPSILON = 1e-06
RATE_SCALE = 8.0
LANES = 128
CHUNK = 64
BF = jnp.bfloat16
F32 = jnp.float32
ORDER = [(3, 0), (1, 0), (3, 1), (2, 1), (0, 0), (0, 1), (2, 0), (1, 1)]


def rms_norm(values, scale_gain):
    factor = lax.rsqrt(jnp.mean(values * values, axis=-1, keepdims=True) + EPSILON)
    return values * factor * scale_gain


def gelu_tanh(values):
    return jax.nn.gelu(values, approximate=True)


def gelu_back(values, grads):
    return jax.vjp(gelu_tanh, values)[1](grads)[0]


def contract_last(left, right):
    return lax.dot_general(left, right, (((1,), (1,)), ((), ())), preferred_element_type=F32)


def contract_first(left, right):
    return lax.dot_general(left, right, (((0,), (0,)), ((), ())), preferred_element_type=F32)


def contract(left, right):
    return jnp.dot(left, right, preferred_element_type=F32)


def conv_apply(padded, taps, offset):
    edge_rows = taps.shape[0] - 1
    length = padded.shape[-2] - edge_rows
    summed = padded[..., edge_rows:, :] * taps[0] + offset
    for back_step in range(1, taps.shape[0]):
        first = edge_rows - back_step
        summed = summed + padded[..., first : first + length, :] * taps[back_step]
    return summed


def swap(value, bit):
    return lax.ppermute(value, "seq", [(i, i ^ bit) for i in range(lax.axis_size("seq"))])


def gather_halves(value):
    half = value.shape[0] // 2
    one = swap(value, 1)
    two = swap(value, 2)
    return value, one, two, swap(one[:half], 2), swap(two[half:], 1)


def gather_seq(value):
    own, one, two, *three = gather_halves(value)
    return own, one, two, jnp.concatenate(three, axis=0)


def assemble_kernel(rows_ref, core_ref, own_ref, one_ref, two_ref, top_ref, bottom_ref, whole_ref, mine_ref, other_ref):
    half = top_ref.shape[0]
    blocks = {
        (0, 0): own_ref[:half], (0, 1): own_ref[half:], (1, 0): one_ref[:half], (1, 1): one_ref[half:],
        (2, 0): two_ref[:half], (2, 1): two_ref[half:], (3, 0): top_ref[...], (3, 1): bottom_ref[...],
    }
    for k, which in enumerate(ORDER):
        whole_ref[pl.ds(pl.multiple_of(rows_ref[k], half), half), :] = blocks[which]

    @pl.when(pl.program_id(1) == 0)
    def _():
        mine_ref[...] = whole_ref[...].T

    @pl.when(pl.program_id(1) == 1)
    def _():
        other_ref[...] = whole_ref[...].T


def assemble(rows, core, blocks, chips, name):
    length, width = 4 * blocks[0].shape[0], blocks[0].shape[1]
    part = width // (2 * chips)
    if part % LANES:
        return assemble_plain(rows, core, blocks, chips)

    def column(i, j, rows, core):
        return (0, 2 * i + (core[0] ^ j))

    def turned():
        return pl.BlockSpec((part, length), lambda i, j, *_: (i, 0))

    return pl.pallas_call(
        assemble_kernel,
        grid_spec=pltpu.PrefetchScalarGridSpec(
            num_scalar_prefetch=2,
            grid=(chips, 2),
            in_specs=[pl.BlockSpec((value.shape[0], part), column) for value in blocks],
            out_specs=[pl.BlockSpec((length, part), column), turned(), turned()],
        ),
        out_shape=[
            jax.ShapeDtypeStruct((length, width), BF),
            jax.ShapeDtypeStruct((width // 2, length), BF),
            jax.ShapeDtypeStruct((width // 2, length), BF),
        ],
        compiler_params=pltpu.CompilerParams(vmem_limit_bytes=32 * 2**20),
        cost_estimate=pl.CostEstimate(flops=0, bytes_accessed=6 * length * width, transcendentals=0),
        name=name,
    )(rows, core, *blocks)


def assemble_plain(rows, core, blocks, chips):
    own, one, two, top, bottom = blocks
    half = top.shape[0]
    halves = {
        (0, 0): own[:half], (0, 1): own[half:], (1, 0): one[:half], (1, 1): one[half:],
        (2, 0): two[:half], (2, 1): two[half:], (3, 0): top, (3, 1): bottom,
    }
    length, width = 8 * half, own.shape[1]
    whole = jnp.zeros((length, width), BF)
    for k, which in enumerate(ORDER):
        whole = lax.dynamic_update_slice_in_dim(whole, halves[which], rows[k], 0)
    turned = whole.T.reshape(chips, 2, width // (2 * chips), length)
    mine, other = (
        lax.dynamic_index_in_dim(turned, which, 1, False).reshape(width // 2, length)
        for which in (core[0], 1 - core[0])
    )
    return whole, mine, other


def scatter_halves(send_one, send_two, keep):
    half = send_one.shape[0] // 2
    from_one = swap(send_one, 1)
    from_two = swap(send_two, 2)
    pass_two = (keep[2 * half : 3 * half] + from_one[:half].astype(F32)).astype(BF)
    pass_one = (keep[3 * half :] + from_two[:half].astype(F32)).astype(BF)
    last_two = swap(pass_two, 2)
    last_one = swap(pass_one, 1)
    near = jnp.concatenate([from_one[half:], from_two[half:]], axis=0).astype(F32)
    far = jnp.concatenate([last_two, last_one], axis=0).astype(F32)
    return keep[: 2 * half] + near + far


def arranged_rows(place, half):
    return jnp.stack([((place ^ step) * 2 + part) * half for step, part in ORDER]).astype(jnp.int32)


def project_kernel(rows_ref, left_ref, right_ref, one_ref, two_ref, keep_ref, order_ref):
    half = left_ref.shape[0] // 8

    @pl.when(pl.program_id(0) == 0)
    def _():
        for k in range(8):
            first = pl.multiple_of(rows_ref[k], half)
            order_ref[k * half : (k + 1) * half, :] = left_ref[pl.ds(first, half), :]

    terms = contract_last(order_ref[...], right_ref[...])
    one_ref[...] = terms[: 2 * half].astype(BF)
    two_ref[...] = terms[2 * half : 4 * half].astype(BF)
    keep_ref[...] = terms[4 * half :]


def project(rows, left, right, column, name):
    length, depth = left.shape
    width = right.shape[0]
    tile = 512
    part = length // 4
    return pl.pallas_call(
        project_kernel,
        grid_spec=pltpu.PrefetchScalarGridSpec(
            num_scalar_prefetch=1,
            grid=(width // tile,),
            in_specs=[
                pl.BlockSpec((length, depth), lambda i, rows: (0, 0), pipeline_mode=pl.Buffered(1)),
                pl.BlockSpec((tile, depth), lambda i, rows: (i, column)),
            ],
            out_specs=[
                pl.BlockSpec((part, tile), lambda i, rows: (0, i)),
                pl.BlockSpec((part, tile), lambda i, rows: (0, i)),
                pl.BlockSpec((2 * part, tile), lambda i, rows: (0, i)),
                pl.BlockSpec((length, depth), lambda i, rows: (0, 0)),
            ],
        ),
        out_shape=[
            jax.ShapeDtypeStruct((part, width), BF),
            jax.ShapeDtypeStruct((part, width), BF),
            jax.ShapeDtypeStruct((2 * part, width), F32),
            jax.ShapeDtypeStruct((length, depth), BF),
        ],
        compiler_params=pltpu.CompilerParams(vmem_limit_bytes=40 * 2**20),
        cost_estimate=pl.CostEstimate(
            flops=2 * length * depth * width,
            bytes_accessed=2 * width * depth + 8 * length * width,
            transcendentals=0,
        ),
        name=name,
    )(rows, left, right)


def swap_core(value):
    return lax.ppermute(value, "seg", [(i, i ^ 1) for i in range(lax.axis_size("seg"))])


def along(value, sources, step):
    pairs = [(2 * i + core, 2 * (i + step) + core) for i in sources for core in range(2)]
    return lax.ppermute(value, "seg", pairs)


def short_chain():
    return lax.axis_size("seg") == 8


def sum_small(value, middle):
    core = lax.axis_index("seg") % 2
    mine = lax.dynamic_index_in_dim(value, core, 0, False)
    if not short_chain():
        return lax.dynamic_index_in_dim(lax.psum(value, "seg"), core, 0, False)
    total = mine.astype(F32) + swap_core(lax.dynamic_index_in_dim(value, 1 - core, 0, False)).astype(F32)
    rows = value.shape[1]
    cut = rows // 32 * 16
    chip = lax.axis_index("seg") // 2 % 2
    low = total.astype(BF)

    def half(which):
        return lax.dynamic_slice_in_dim(low, which * cut, rows - cut, 0)

    def exchange(value, bit):
        return lax.ppermute(value, "seg", [(i, i ^ bit) for i in range(8)])

    part = (half(chip).astype(F32) + after(exchange(half(1 - chip), 2), middle).astype(F32)).astype(BF)
    part = (part.astype(F32) + exchange(part, 4).astype(F32)).astype(BF)
    other = exchange(part, 2)
    shared = rows - 2 * cut
    return jnp.where(
        chip == 0,
        jnp.concatenate([part, other[shared:]], axis=0),
        jnp.concatenate([other, part[shared:]], axis=0),
    )


def sum_all(value):
    if not short_chain():
        return lax.psum(value, ("seq", "seg"))
    for axis, bits in (("seg", (1, 2, 4)), ("seq", (1, 2))):
        for bit in bits:
            pairs = [(i, i ^ bit) for i in range(lax.axis_size(axis))]
            value = value + lax.ppermute(value, axis, pairs)
    return value


def after(value, earlier):
    return lax.optimization_barrier((value, earlier))[0]


def neg_expm1(values):
    total = 1.0 + values * (1.0 / 9.0)
    for order in range(8, 1, -1):
        total = 1.0 + values * (1.0 / order) * total
    return jnp.where(values > -0.7, -values * total, 1.0 - jnp.exp(values))


def scan_kernel(
    blk_ref, low_ref, wd_ref, wi_ref, par_ref, conv_ref, branch_ref,
    states_ref, decay_ref, rate_ref, open_ref, mixed_ref,
):
    length = conv_ref.shape[0]
    par = par_ref[...]
    soft = par[2:3]
    row = lax.broadcasted_iota(jnp.int32, (CHUNK // 8, 8, LANES), 1)

    def body(step, carry):
        rows = pl.ds(pl.multiple_of(step * CHUNK, CHUNK), CHUNK)
        low = low_ref[rows, :]
        rate = jax.nn.sigmoid(contract(low, wd_ref[0]) + par[0:1])
        opened = jax.nn.sigmoid(contract(low, wi_ref[0]) + par[1:2])
        log_decay = -RATE_SCALE * rate * soft
        decay = jnp.exp(log_decay)
        drive = jnp.sqrt(neg_expm1(2.0 * log_decay)) * opened * conv_ref[rows, :]
        rate_ref[rows, :] = rate
        open_ref[rows, :] = opened
        decay_ref[rows, :] = decay
        prod = decay.reshape(CHUNK // 8, 8, LANES)
        total = drive.reshape(CHUNK // 8, 8, LANES)
        for shift in (1, 2, 4):
            inside = row >= shift
            moved = jnp.where(inside, pltpu.roll(total, shift, 1), 0.0)
            total = total + prod * moved
            prod = prod * jnp.where(inside, pltpu.roll(prod, shift, 1), 1.0)
        pieces = []
        for group in range(CHUNK // 8):
            piece = total[group] + prod[group] * carry
            carry = piece[7:8]
            pieces.append(piece)
        states = jnp.concatenate(pieces, axis=0)
        states_ref[rows, :] = states
        mixed_ref[rows, :] = (states * gelu_tanh(branch_ref[rows, :])).astype(BF)
        return carry

    lax.fori_loop(0, length // CHUNK, body, par[3:4])


def scan_forward(blk, conv_ext, decay_w, input_w, params, conv_out, projected):
    length, width = conv_out.shape
    tiles = width // LANES
    tile = pl.BlockSpec((length, LANES), lambda i, blk: (0, i))
    weight = pl.BlockSpec((1, decay_w.shape[1], LANES), lambda i, blk: (i, 0, 0))
    whole = jax.ShapeDtypeStruct((length, width), F32)
    return pl.pallas_call(
        scan_kernel,
        grid_spec=pltpu.PrefetchScalarGridSpec(
            num_scalar_prefetch=1,
            grid=(tiles,),
            in_specs=[
                pl.BlockSpec((length, decay_w.shape[1]), lambda i, blk: (0, blk[i])),
                weight,
                weight,
                pl.BlockSpec((8, LANES), lambda i, blk: (0, i)),
                tile,
                tile,
            ],
            out_specs=[tile] * 5,
        ),
        out_shape=[whole, whole, whole, whole, jax.ShapeDtypeStruct((length, width), BF)],
        compiler_params=pltpu.CompilerParams(vmem_limit_bytes=32 * 2**20),
        cost_estimate=pl.CostEstimate(
            flops=4 * length * width * 256, bytes_accessed=length * width * 28, transcendentals=0
        ),
        name="scan_forward",
    )(blk, conv_ext, decay_w, input_w, params, conv_out, projected)


def back_kernel(
    rows_ref, strip_ref, par_ref, mixed_in, branch_ref, states_ref, decay_ref, rate_ref, open_ref, conv_ref,
    proj_out, gate_out, input_out, direct_out, sums_out, strips_out, mixed_ref,
):
    length = conv_ref.shape[0]
    groups = CHUNK // 8
    par = par_ref[...]
    soft = par[2:3]
    row = lax.broadcasted_iota(jnp.int32, (groups, 8, LANES), 1)
    flat_row = lax.broadcasted_iota(jnp.int32, (CHUNK, LANES), 0)
    steps = length // CHUNK
    half = length // 8
    for k in range(8):
        mixed_ref[pl.ds(pl.multiple_of(rows_ref[k], half), half), :] = mixed_in[k * half : (k + 1) * half, :]

    def body(turn, carried):
        carry, gate_sum, input_sum, logit_sum = carried
        step = steps - 1 - turn
        first = pl.multiple_of(step * CHUNK, CHUNK)
        rows = pl.ds(first, CHUNK)
        mixed_grad = mixed_ref[rows, :]
        branch = branch_ref[rows, :]
        states = states_ref[rows, :]
        decay = decay_ref[rows, :]
        branch_act, pull = jax.vjp(gelu_tanh, branch)
        proj_out[rows, :] = pull(mixed_grad * states)[0].astype(BF)
        state_grad = mixed_grad * branch_act
        prod = decay.reshape(groups, 8, LANES)
        total = (decay * state_grad).reshape(groups, 8, LANES)
        for shift in (1, 2, 4):
            inside = row < 8 - shift
            moved = jnp.where(inside, pltpu.roll(total, 8 - shift, 1), 0.0)
            total = total + prod * moved
            prod = prod * jnp.where(inside, pltpu.roll(prod, 8 - shift, 1), 1.0)
        pieces = [None] * groups
        after = carry
        for group in reversed(range(groups)):
            piece = total[group] + prod[group] * after
            after = piece[0:1]
            pieces[group] = piece
        passed = jnp.concatenate(pieces, axis=0)
        shifted = jnp.where(flat_row == CHUNK - 1, carry, pltpu.roll(passed, CHUNK - 1, 0))
        adjoint = state_grad + shifted
        before = states_ref[pl.ds(pl.multiple_of(jnp.maximum(first - 8, 0), 8), 8), :][7:8]
        before = jnp.where(step == 0, par[3:4], before)
        previous = jnp.where(flat_row == 0, before, pltpu.roll(states, 1, 0))
        rate = rate_ref[rows, :]
        opened = open_ref[rows, :]
        conv = conv_ref[rows, :]
        log_decay = -RATE_SCALE * rate * soft
        scale = jnp.sqrt(neg_expm1(2.0 * log_decay))
        opened_conv = opened * conv
        ratio = jnp.where(scale > 0.0, decay / scale, 0.0)
        log_grad = decay * (adjoint * previous - adjoint * opened_conv * ratio)
        scaled = adjoint * scale
        direct_out[rows, :] = scaled * opened
        input_grad = (scaled * conv * opened * (1.0 - opened)).astype(BF)
        rate_grad = log_grad * rate
        gate_grad = (rate_grad * (1.0 - rate) * (-RATE_SCALE * soft)).astype(BF)
        gate_out[rows, :] = gate_grad
        input_out[rows, :] = input_grad

        def folded(value):
            return jnp.sum(value.astype(F32).reshape(groups, 8, LANES), axis=0)

        return (
            after,
            gate_sum + folded(gate_grad),
            input_sum + folded(input_grad),
            logit_sum + folded(rate_grad),
        )

    zero = jnp.zeros((8, LANES), F32)
    after, gate_sum, input_sum, logit_sum = lax.fori_loop(
        0, steps, body, (jnp.zeros((1, LANES), F32), zero, zero, zero)
    )
    sums_out[...] = jnp.concatenate(
        [
            jnp.sum(gate_sum, axis=0, keepdims=True),
            jnp.sum(input_sum, axis=0, keepdims=True),
            jnp.sum(logit_sum, axis=0, keepdims=True) * (-RATE_SCALE * par[4:5]),
            after,
            jnp.zeros((4, LANES), F32),
        ],
        axis=0,
    )

    @pl.when(pl.program_id(0) == strip_ref[0])
    def _():
        strips_out[0] = gate_out[...]
        strips_out[1] = input_out[...]


def scan_backward(rows, strip_tile, params, mixed_grad, projected, states, decays, rate, opened, conv_out):
    length, width = conv_out.shape
    tiles = width // LANES
    tile = pl.BlockSpec((length, LANES), lambda i, *_: (0, i))
    small = pl.BlockSpec((8, LANES), lambda i, *_: (0, i))
    low = jax.ShapeDtypeStruct((length, width), BF)
    return pl.pallas_call(
        back_kernel,
        grid_spec=pltpu.PrefetchScalarGridSpec(
            num_scalar_prefetch=2,
            grid=(tiles,),
            in_specs=[
                small,
            ]
            + [tile] * 7,
            out_specs=[tile] * 4 + [small, pl.BlockSpec((2, length, LANES), lambda i, *_: (0, 0, 0))],
            scratch_shapes=[pltpu.VMEM((length, LANES), F32)],
        ),
        out_shape=[
            jax.ShapeDtypeStruct((length, 2 * width), BF),
            low,
            low,
            jax.ShapeDtypeStruct((length, width), F32),
            jax.ShapeDtypeStruct((8, width), F32),
            jax.ShapeDtypeStruct((2, length, LANES), BF),
        ],
        compiler_params=pltpu.CompilerParams(vmem_limit_bytes=40 * 2**20),
        cost_estimate=pl.CostEstimate(
            flops=100 * length * width, bytes_accessed=length * width * 44, transcendentals=0
        ),
        name="scan_backward",
    )(rows, strip_tile, params, mixed_grad, projected, states, decays, rate, opened, conv_out)


def gates_kernel(
    blk_ref, near_ref, edge_ref, par_ref, sums_ref, gate_ref, gate_near, input_ref, input_near, strips_ref,
    wd_ref, wi_ref, direct_ref, low_t_ref, conv_in_ref, proj_in, proj_out, small_out, single_out,
):
    length = direct_ref.shape[0]
    block = low_t_ref.shape[0]
    edge = edge_ref[pl.program_id(0)] == 1
    gate, opened = gate_ref[...], input_ref[...]
    gate_both = jnp.concatenate([gate, jnp.where(edge, strips_ref[0], gate_near[...])], axis=1)
    input_both = jnp.concatenate([opened, jnp.where(edge, strips_ref[1], input_near[...])], axis=1)
    conv_grad = direct_ref[...] + contract_last(gate_both, wd_ref[0]) + contract_last(input_both, wi_ref[0])
    row = lax.broadcasted_iota(jnp.int32, (length, LANES), 0)
    par = par_ref[...]
    conv_in = conv_in_ref[...]
    conv_in_grad = par[0:1] * conv_grad
    tap_sums = [jnp.sum(conv_grad * conv_in, axis=0, keepdims=True)]
    for k in range(1, 4):
        moved = jnp.where(row < length - k, pltpu.roll(conv_grad, length - k, 0), 0.0)
        conv_in_grad = conv_in_grad + par[k : k + 1] * moved
        total = jnp.sum(moved * conv_in, axis=0, keepdims=True)
        for t in range(k):
            total = total + conv_grad[t : t + 1] * par[7 + t - k : 8 + t - k]
        tap_sums.append(total)
    proj_out[...] = conv_in_grad.astype(BF)
    window = []
    for s in range(3):
        total = par[3 - s : 4 - s] * conv_grad[0:1]
        for k in range(4 - s, 4):
            total = total + par[k : k + 1] * conv_grad[s - 3 + k : s - 2 + k]
        window.append(total)
    sums = sums_ref[...]
    zero = jnp.zeros((8, LANES), F32)
    vectors = jnp.concatenate(
        tap_sums + [jnp.sum(conv_grad, axis=0, keepdims=True), sums[0:3], zero], axis=0
    ).astype(BF)
    low_t = low_t_ref[...]
    small_out[0, :block, :] = contract(low_t, gate).astype(BF)
    small_out[1, :block, :] = contract(low_t, opened).astype(BF)
    small_out[0, block:, :] = vectors
    small_out[1, block:, :] = vectors
    single_out[...] = jnp.concatenate([sums[3:4]] + window + [zero, zero[:4]], axis=0).astype(BF)


def gates_backward(blk, near, edge, params, sums, gate, opened, strips, decay_w, input_w, direct, low_t, projected, proj):
    length, width = direct.shape
    tiles = width // LANES
    block = decay_w.shape[2]
    tile = pl.BlockSpec((length, LANES), lambda i, *_: (0, i))
    beside = pl.BlockSpec((length, LANES), lambda i, blk, near, edge: (0, near[i]))
    small = pl.BlockSpec((8, LANES), lambda i, *_: (0, i))
    weight = pl.BlockSpec((1, LANES, block), lambda i, *_: (i, 0, 0))
    second = pl.BlockSpec((length, LANES), lambda i, *_: (0, tiles + i))
    return pl.pallas_call(
        gates_kernel,
        grid_spec=pltpu.PrefetchScalarGridSpec(
            num_scalar_prefetch=3,
            grid=(tiles,),
            in_specs=[
                small,
                small,
                tile,
                beside,
                tile,
                beside,
                pl.BlockSpec(strips.shape, lambda i, *_: (0, 0, 0)),
                weight,
                weight,
                tile,
                pl.BlockSpec((block, length), lambda i, blk, near, edge: (blk[i], 0)),
                second,
                pl.BlockSpec(memory_space=pl.ANY),
            ],
            out_specs=[
                second,
                pl.BlockSpec((2, block + 16, LANES), lambda i, *_: (0, 0, i)),
                pl.BlockSpec((16, LANES), lambda i, *_: (0, i)),
            ],
        ),
        out_shape=[
            jax.ShapeDtypeStruct(proj.shape, BF),
            jax.ShapeDtypeStruct((2, block + 16, width), BF),
            jax.ShapeDtypeStruct((16, width), BF),
        ],
        input_output_aliases={15: 0},
        compiler_params=pltpu.CompilerParams(vmem_limit_bytes=32 * 2**20),
        cost_estimate=pl.CostEstimate(
            flops=8 * length * width * block, bytes_accessed=length * width * 20, transcendentals=0
        ),
        name="gates_backward",
    )(blk, near, edge, params, sums, gate, gate, opened, opened, strips, decay_w, input_w, direct, low_t, projected, proj)


def mlp_data(tile, low_ref, cot_ref, weight_ref):
    gate_up = contract(low_ref[...], weight_ref[:, : 2 * tile])
    hidden_grad = contract(cot_ref[...], weight_ref[:, 2 * tile :])
    gate_val, up_val = gate_up[:, :tile], gate_up[:, tile:]
    gate_act, pull = jax.vjp(gelu_tanh, gate_val)
    hidden = (gate_act * up_val).astype(BF)
    gate_grad = pull(hidden_grad * up_val)[0].astype(BF)
    up_grad = (hidden_grad * gate_act).astype(BF)
    return jnp.concatenate([gate_grad, up_grad], axis=1), hidden


def add_term(total_ref, term):
    @pl.when(pl.program_id(0) == 0)
    def _():
        total_ref[...] = term

    @pl.when(pl.program_id(0) > 0)
    def _():
        total_ref[...] += term


def give_halves(total_ref, before_ref, one_ref, two_ref, keep_ref):
    @pl.when(pl.program_id(0) == pl.num_programs(0) - 1)
    def _():
        part = total_ref.shape[0] // 4
        one_ref[...] = (total_ref[:part] + before_ref[:part]).astype(BF)
        two_ref[...] = (total_ref[part : 2 * part] + before_ref[part : 2 * part]).astype(BF)
        keep_ref[...] = total_ref[2 * part :] + before_ref[2 * part :]


def mlp_first_kernel(tile, low_ref, cot_ref, weight_ref, units_ref, back_ref, out_ref):
    both, hidden = mlp_data(tile, low_ref, cot_ref, weight_ref)
    units_ref[:, : 2 * tile] = both
    units_ref[:, 2 * tile :] = hidden
    add_term(back_ref, contract_last(both, weight_ref[:, : 2 * tile]))
    add_term(out_ref, contract_last(hidden, weight_ref[:, 2 * tile :]))


def mlp_last_kernel(tile, low_ref, cot_ref, weight_ref, before_ref, units_ref, one_ref, two_ref, keep_ref, back_ref):
    both, hidden = mlp_data(tile, low_ref, cot_ref, weight_ref)
    units_ref[:, : 2 * tile] = both
    units_ref[:, 2 * tile :] = hidden
    add_term(back_ref, contract_last(both, weight_ref[:, : 2 * tile]))
    give_halves(back_ref, before_ref, one_ref, two_ref, keep_ref)


def mlp_out_kernel(tile, weight_ref, units_ref, before_ref, one_ref, two_ref, keep_ref, out_ref):
    add_term(out_ref, contract_last(units_ref[:, 2 * tile :], weight_ref[:, 2 * tile :]))
    give_halves(out_ref, before_ref, one_ref, two_ref, keep_ref)


def mlp_grad_kernel(tile, low_ref, low_other, cot_ref, cot_other, units_ref, units_other, grad_ref):
    cut = 2 * tile
    grad_ref[:, :cut] = (
        contract(low_ref[...], units_ref[:, :cut]) + contract(low_other[...], units_other[:, :cut])
    ).astype(BF)
    grad_ref[:, cut:] = (
        contract(cot_ref[...], units_ref[:, cut:]) + contract(cot_other[...], units_other[:, cut:])
    ).astype(BF)


def recur_grad_kernel(
    low_ref, low_other, mixer_ref, mixer_other, proj_ref, proj_other, mixed_ref, mixed_other, held_ref, grad_ref
):
    step = pl.program_id(0)

    @pl.when(step < 2)
    def _():
        grad_ref[...] = (
            contract(low_ref[...], proj_ref[...]) + contract(low_other[...], proj_other[...])
        ).astype(BF)

    @pl.when(step == 2)
    def _():
        grad_ref[...] = (
            contract(mixer_ref[...], mixed_ref[...]) + contract(mixer_other[...], mixed_other[...])
        ).astype(BF)


def recur_grad(low_t, mixer_t, proj, mixed, held):
    depth, length = low_t[0].shape
    width = mixed[0].shape[1]
    fixed = pl.BlockSpec((depth, length), lambda i: (0, 0), pipeline_mode=pl.Buffered(1))
    moving = pl.BlockSpec((length, width), lambda i: (0, jnp.minimum(i, 1)))
    whole = pl.BlockSpec((length, width), lambda i: (0, 0))
    return pl.pallas_call(
        recur_grad_kernel,
        grid=(3,),
        in_specs=[fixed] * 4 + [moving] * 2 + [whole] * 2 + [pl.BlockSpec(memory_space=pl.ANY)],
        out_specs=pl.BlockSpec((depth, width), lambda i: (0, i)),
        out_shape=jax.ShapeDtypeStruct(held.shape, BF),
        input_output_aliases={8: 0},
        compiler_params=pltpu.CompilerParams(vmem_limit_bytes=40 * 2**20),
        cost_estimate=pl.CostEstimate(
            flops=12 * depth * length * width, bytes_accessed=6 * depth * width + 8 * depth * length, transcendentals=0
        ),
        name="recur_grad",
    )(*low_t, *mixer_t, *proj, *mixed, held)


def mlp_grad_beside_kernel(
    tile, first, low_ref, low_other, cot_ref, cot_other, units_ref, units_other, held_ref, grad_ref, sem
):
    mlp_grad_kernel(tile, low_ref, low_other, cot_ref, cot_other, units_ref, units_other, grad_ref)
    columns = pl.ds(pl.multiple_of(first + pl.program_id(0) * 3 * tile, LANES), 3 * tile)
    copy = pltpu.make_async_copy(grad_ref, held_ref.at[:, columns], sem)
    copy.start()
    copy.wait()


def mlp_grad_beside(tile, low_t, cot_t, units, first):
    (depth, rows), columns = low_t[0].shape, units[0].shape[1]
    fixed = pl.BlockSpec((depth, rows), lambda i: (0, 0), pipeline_mode=pl.Buffered(1))
    moving = pl.BlockSpec((rows, 3 * tile), lambda i: (0, i))
    return pl.pallas_call(
        lambda *refs: mlp_grad_beside_kernel(tile, first, *refs),
        grid=(columns // (3 * tile),),
        in_specs=[fixed] * 4 + [moving] * 2,
        out_specs=pl.BlockSpec(memory_space=pl.ANY),
        out_shape=jax.ShapeDtypeStruct((depth, first + columns), BF),
        scratch_shapes=[pltpu.VMEM((depth, 3 * tile), BF), pltpu.SemaphoreType.DMA],
        compiler_params=pltpu.CompilerParams(vmem_limit_bytes=40 * 2**20),
        cost_estimate=pl.CostEstimate(
            flops=4 * rows * depth * columns, bytes_accessed=2 * depth * columns + 8 * rows * depth, transcendentals=0
        ),
        name="mlp_grad_last",
    )(*low_t, *cot_t, *units)


def unpack_kernel(tile, first, sums_ref, in_held, out_held, feed_in_ref, feed_out_ref, recur_in_ref, recur_out_ref):
    width = recur_out_ref.shape[1]
    for i in range(2):
        recur_in_ref[:, i, :] = sums_ref[:, i * width : (i + 1) * width].astype(F32)
    recur_out_ref[...] = sums_ref[:, 2 * width : 3 * width].astype(F32)
    for k in range(feed_out_ref.shape[1] // tile):
        at = slice(k * tile, (k + 1) * tile)
        start = first + 3 * tile * k
        for i in range(2):
            feed_in_ref[:, i, at] = sums_ref[:, start + i * tile : start + (i + 1) * tile].astype(F32)
        feed_out_ref[:, at] = sums_ref[:, start + 2 * tile : start + 3 * tile].astype(F32)


def unpack(tile, sums, feed_in, feed_out, recur_width, done):
    rows = sums.shape[0]
    units = feed_out.shape[1]
    part = units - done
    anywhere = pl.BlockSpec(memory_space=pl.ANY)
    return pl.pallas_call(
        lambda *refs: unpack_kernel(tile, 3 * recur_width, *refs),
        grid=(1,),
        in_specs=[pl.BlockSpec(sums.shape, lambda i: (0, 0)), anywhere, anywhere],
        out_specs=[
            pl.BlockSpec((rows, 2, part), lambda i: (0, 0, done // part)),
            pl.BlockSpec((rows, part), lambda i: (0, done // part)),
            pl.BlockSpec((rows, 2, recur_width), lambda i: (0, 0, 0)),
            pl.BlockSpec((rows, recur_width), lambda i: (0, 0)),
        ],
        out_shape=[
            jax.ShapeDtypeStruct(feed_in.shape, F32),
            jax.ShapeDtypeStruct(feed_out.shape, F32),
            jax.ShapeDtypeStruct((rows, 2, recur_width), F32),
            jax.ShapeDtypeStruct((rows, recur_width), F32),
        ],
        input_output_aliases={1: 0, 2: 1},
        compiler_params=pltpu.CompilerParams(vmem_limit_bytes=40 * 2**20),
        cost_estimate=pl.CostEstimate(flops=0, bytes_accessed=6 * rows * sums.shape[1], transcendentals=0),
        name="unpack",
    )(sums, feed_in, feed_out)


def mlp_call(kernel, tile, products, rows, width, columns, fixed_in, moving_in, fixed_out, moving_out, scratch, name):
    def fixed(shape, single):
        return pl.BlockSpec(shape, lambda i: (0, 0), pipeline_mode=pl.Buffered(1) if single else None)

    def moving(shape):
        return pl.BlockSpec((shape[0], 3 * tile), lambda i: (0, i))

    return pl.pallas_call(
        lambda *refs: kernel(tile, *refs),
        grid=(columns // (3 * tile),),
        in_specs=[
            fixed(value.shape, True) if kind == "fixed" else moving(value.shape)
            for kind, value in fixed_in + moving_in
        ],
        out_specs=[moving(shape) for shape, _ in moving_out] + [fixed(shape, False) for shape, _ in fixed_out],
        out_shape=[jax.ShapeDtypeStruct(shape, kind) for shape, kind in moving_out + fixed_out],
        scratch_shapes=[pltpu.VMEM(shape, kind) for shape, kind in scratch],
        compiler_params=pltpu.CompilerParams(vmem_limit_bytes=60 * 2**20),
        cost_estimate=pl.CostEstimate(
            flops=2 * products * rows * width * columns // 3,
            bytes_accessed=4 * width * columns + 16 * rows * width,
            transcendentals=0,
        ),
        name=name,
    )(*[value for _, value in fixed_in + moving_in])


def half_shapes(rows, width):
    part = rows // 4
    return [((part, width), BF), ((part, width), BF), ((2 * part, width), F32)]


def mlp_first(tile, low2, cot, weight):
    (rows, width), columns = low2.shape, weight.shape[1]
    ins = [("fixed", low2), ("fixed", cot), ("moving", weight)]
    return mlp_call(
        mlp_first_kernel, tile, 6, rows, width, columns, ins, [],
        [((rows, width), F32)] * 2, [((rows, columns), BF)], [], "mlp_first",
    )


def mlp_last(tile, low2, cot, weight, before):
    (rows, width), columns = low2.shape, weight.shape[1]
    ins = [("fixed", low2), ("fixed", cot), ("moving", weight), ("fixed", before)]
    return mlp_call(
        mlp_last_kernel, tile, 5, rows, width, columns, ins, [],
        half_shapes(rows, width), [((rows, columns), BF)], [((rows, width), F32)], "mlp_last",
    )


def mlp_out_last(tile, weight, units, before):
    (width, columns), rows = weight.shape, units.shape[0]
    ins = [("moving", weight), ("moving", units), ("fixed", before)]
    return mlp_call(
        mlp_out_kernel, tile, 1, rows, width, columns, ins, [],
        half_shapes(rows, width), [], [((rows, width), F32)], "mlp_out",
    )


def mlp_grad(tile, low_t, cot_t, units):
    (depth, rows), columns = low_t[0].shape, units[0].shape[1]
    ins = [("fixed", value) for value in (*low_t, *cot_t)] + [("moving", value) for value in units]
    return mlp_call(
        mlp_grad_kernel, tile, 3, rows, 2 * depth, columns, ins, [],
        [], [((depth, columns), BF)], [], "mlp_grad",
    )[0]


def shards(
    tokens,
    cotangent,
    start_state,
    start_window,
    first_gain,
    recur_in,
    conv_taps,
    conv_bias,
    decay_gate,
    input_gate,
    decay_bias,
    input_bias,
    decay_logit,
    recur_out,
    second_gain,
    feed_in,
    feed_out,
):
    segments, length, model_width = tokens.shape
    recur_width = conv_taps.shape[1]
    head_count, block_size = decay_gate.shape[:2]
    edge_rows = conv_taps.shape[0] - 1
    seq_parts = lax.axis_size("seq")
    place = lax.axis_index("seq")
    own_rows, _, recur_part = recur_in.shape
    feed_part = feed_in.shape[2]
    first_channel = place * recur_part
    first_block = first_channel // block_size
    block_count = -(-recur_part // block_size)
    strip = block_count * block_size - recur_part
    odd = place % 2 == 1

    def own(value):
        return lax.dynamic_slice_in_dim(value, first_channel, recur_part, value.ndim - 1)

    def strip_of(value):
        return jnp.where(odd, value[:, :strip], value[:, recur_part - strip :])

    def gather_seg(value):
        return lax.all_gather(value, "seg", axis=0, tiled=True)

    seg_parts = lax.axis_size("seg")
    core = lax.axis_index("seg") % 2

    def scatter_rows(value):
        groups = [list(range(c, seg_parts, 2)) for c in range(2)]
        return lax.psum_scatter(value, "seg", scatter_dimension=0, tiled=True, axis_index_groups=groups)

    def gathered(blocks, rows, name):
        whole, mine, other = assemble(rows, core[None].astype(jnp.int32), blocks, seg_parts // 2, name)
        return whole, (mine, swap_core(other))

    def of_both(value):
        return value, swap_core(value)

    unit = 2 * LANES
    first_part = 2 * feed_part // 3 // unit * unit
    cuts = [(0, first_part), (first_part, feed_part)]

    def feed_columns(first, count):
        return [feed_in[:, 0, first : first + count], feed_in[:, 1, first : first + count], feed_out[:, first : first + count]]

    feeds = [
        jnp.concatenate([c for first in range(a, b, unit) for c in feed_columns(first, unit)], axis=1)
        for a, b in cuts
    ]
    recur = gather_seg(jnp.concatenate([recur_in[:, 0], recur_in[:, 1], recur_out], axis=1))
    feed_first = gather_seg(feeds[0])
    feed_last = gather_seg(feeds[1])

    inputs = tokens.astype(F32).reshape(length, model_width)
    upstream = cotangent.reshape(length, model_width)
    low1 = rms_norm(inputs, first_gain).astype(BF)
    rows = arranged_rows(place, length // 2)
    straight = jnp.arange(8, dtype=jnp.int32) * (length // 2)
    all_low1, low1_rows = gathered(gather_halves(low1), rows, "gather_low1")
    all_cot, cot_rows = gathered(gather_halves(upstream), straight, "gather_cot")

    taps = own(conv_taps)
    logit = own(decay_logit[None])
    params = jnp.concatenate(
        [
            own(decay_bias[None]),
            own(input_bias[None]),
            jax.nn.softplus(logit),
            own(start_state),
            jax.nn.sigmoid(logit),
            jnp.zeros((3, recur_part), F32),
        ],
        axis=0,
    )
    window = own(start_window)[0]
    conv_params = jnp.concatenate([taps, window, jnp.zeros((1, recur_part), F32)], axis=0)
    tiles = recur_part // LANES
    halves = block_size // LANES
    first_tile = jnp.where(odd, strip // LANES, 0)
    tile_place = first_tile + jnp.arange(tiles)
    tile_block = (tile_place // halves).astype(jnp.int32)
    near = (tile_place ^ 1) - first_tile
    edge = ((near < 0) | (near >= tiles)).astype(jnp.int32)
    near = jnp.clip(near, 0, tiles - 1).astype(jnp.int32)
    strip_tile = jnp.where(odd, 0, tiles - 1).astype(jnp.int32)[None]

    def gate_tiles(blocks):
        blocks = lax.dynamic_slice_in_dim(blocks, first_block, block_count, 0)
        columns = blocks.reshape(block_count, block_size, halves, LANES).transpose(0, 2, 1, 3)
        columns = columns.reshape(block_count * halves, block_size, LANES)
        lines = blocks.reshape(block_count * halves, LANES, block_size)
        turned = jnp.concatenate([lines[:, :, LANES:], lines[:, :, :LANES]], axis=2)
        swapped = (jnp.arange(block_count * halves) % 2 == 1)[:, None, None]
        lines = jnp.where(swapped, turned, lines)
        return (
            lax.dynamic_slice_in_dim(columns, first_tile, tiles, 0),
            lax.dynamic_slice_in_dim(lines, first_tile, tiles, 0),
        )

    decay_columns, decay_lines = gate_tiles(decay_gate)
    input_columns, input_lines = gate_tiles(input_gate)

    projected = contract(all_low1, recur[:, : 2 * recur_part])
    padded = jnp.concatenate([window, projected[:, recur_part:]], axis=0)
    conv_out = conv_apply(padded, taps, own(conv_bias[None]))
    conv_low = conv_out.astype(BF)
    arrived = swap(strip_of(conv_low), 1)
    conv_ext = jnp.where(
        odd,
        jnp.concatenate([arrived, conv_low], axis=1),
        jnp.concatenate([conv_low, arrived], axis=1),
    )
    states, decays, rate, opened, mixed_low = scan_forward(
        tile_block, conv_ext, decay_columns, input_columns, params, conv_out, projected
    )
    *pieces, mixed_low = project(rows, mixed_low, recur, 2, "mixer_out")
    residual = inputs + scatter_halves(*pieces)

    low2 = rms_norm(residual, second_gain).astype(BF)
    all_low2, low2_rows = gathered(gather_halves(low2), straight, "gather_low2")
    units, back_first, out_first = mlp_first(unit, all_low2, all_cot, feed_first)
    grad_first = scatter_rows(mlp_grad(unit, low2_rows, cot_rows, of_both(units)))
    units, *pieces = mlp_last(unit, all_low2, all_cot, feed_last, back_first)
    normed2_grad = scatter_halves(*pieces)
    units_last = units
    residual_norm_grad, second_gain_grad = jax.vjp(rms_norm, residual, second_gain)[1](normed2_grad)
    residual_grad = upstream.astype(F32) + residual_norm_grad

    mixer_blocks = gather_halves(residual_grad.astype(BF))
    held = mlp_grad_beside(unit, low2_rows, cot_rows, of_both(units_last), 3 * recur_part)
    mixer_grad, mixer_rows = gathered(after(mixer_blocks, held), straight, "gather_mixer")
    proj_grad, gate_low_grad, input_low_grad, conv_direct, sums, strips = scan_backward(
        rows, strip_tile, params, contract(mixer_grad, recur[:, 2 * recur_part :]), projected, states, decays, rate,
        opened, conv_out,
    )
    proj_grad, small, single = gates_backward(
        tile_block, near, edge, conv_params, sums, gate_low_grad, input_low_grad, swap(strips, 1),
        decay_lines, input_lines, conv_direct, conv_ext.T, projected, proj_grad,
    )
    mlp_term = scatter_halves(*mlp_out_last(unit, feed_last, after(units_last, proj_grad), out_first))
    output = (residual + mlp_term).astype(BF).reshape(tokens.shape)
    grad_last_term = recur_grad(low1_rows, mixer_rows, of_both(proj_grad), of_both(mixed_low), held)
    *pieces, _ = project(rows, after(proj_grad, grad_last_term), recur, 0, "normed1_grad")
    normed1_grad = scatter_halves(*pieces)
    input_norm_grad, first_gain_grad = jax.vjp(rms_norm, inputs, first_gain)[1](normed1_grad)
    input_grad = (residual_grad + input_norm_grad).astype(BF).reshape(tokens.shape)

    grad_last = scatter_rows(after(grad_last_term, grad_first))

    def columns_of(value, which, start):
        return jnp.concatenate(
            [value[:, at : at + unit] for at in range(start + which * unit, value.shape[1], 3 * unit)], axis=1
        ).astype(F32)

    def feed_grads(value, start):
        return jnp.stack([columns_of(value, i, start) for i in range(2)], axis=1), columns_of(value, 2, start)

    feed_in_first, feed_out_first = feed_grads(grad_first, 0)
    feed_in_grad = jnp.pad(feed_in_first, ((0, 0), (0, 0), (0, feed_part - first_part)))
    feed_out_grad = jnp.pad(feed_out_first, ((0, 0), (0, feed_part - first_part)))
    grad_last = after(grad_last, (feed_in_grad, feed_out_grad))
    feed_in_grad, feed_out_grad, recur_in_grad, recur_out_grad = unpack(
        unit, grad_last, feed_in_grad, feed_out_grad, recur_part, first_part
    )

    mine = gather_seq(jnp.concatenate([sum_small(small, grad_last_term), single], axis=0))
    swapped = [jnp.where(odd, mine[i ^ 1], mine[i]) for i in range(4)]
    mine = jnp.concatenate([jnp.where(place >= 2, swapped[i ^ 2], swapped[i]) for i in range(4)], axis=1)
    vectors = mine[block_size:].astype(F32)
    other = swap_core(mine[:block_size])

    def as_blocks(which):
        value = jnp.where(core == which, mine[:block_size], other).astype(F32)
        return value.reshape(block_size, head_count, block_size).transpose(1, 0, 2)

    gains = sum_all(jnp.stack([first_gain_grad, second_gain_grad]))
    kernel_taps = conv_taps.shape[0]
    return (
        output,
        input_grad,
        vectors[16:17],
        vectors[17 : 17 + edge_rows][None],
        gains[0],
        recur_in_grad,
        vectors[:kernel_taps],
        vectors[kernel_taps],
        as_blocks(0),
        as_blocks(1),
        vectors[kernel_taps + 1],
        vectors[kernel_taps + 2],
        vectors[kernel_taps + 3],
        recur_out_grad,
        gains[1],
        feed_in_grad,
        feed_out_grad,
    )


def solution(mesh):
    placed = (
        P("seg", "seq", None),
        P("seg", "seq", None),
        P("seg", None),
        P("seg", None, None),
        P(),
        P("seg", None, "seq"),
        P(),
        P(),
        P(),
        P(),
        P(),
        P(),
        P(),
        P("seg", "seq"),
        P(),
        P("seg", None, "seq"),
        P("seg", "seq"),
    )
    return jax.shard_map(
        shards,
        mesh=mesh,
        in_specs=placed,
        out_specs=(
            P("seg", "seq", None),
            P("seg", "seq", None),
            P("seg", None),
            P("seg", None, None),
            P(),
            P("seg", None, "seq"),
            P(),
            P(),
            P(),
            P(),
            P(),
            P(),
            P(),
            P("seg", "seq"),
            P(),
            P("seg", None, "seq"),
            P("seg", "seq"),
        ),
        check_vma=False,
    )
```

```python
import jax
import jax.numpy as jnp
from jax import lax
from jax.experimental import pallas as pl
from jax.experimental.pallas import tpu as pltpu
from jax.sharding import PartitionSpec as P

EPSILON = 1e-06
RATE_SCALE = 8.0
LANES = 128
CHUNK = 64
BF = jnp.bfloat16
F32 = jnp.float32
ORDER = [(3, 0), (1, 0), (3, 1), (2, 1), (0, 0), (0, 1), (2, 0), (1, 1)]


def rms_norm(values, scale_gain):
    factor = lax.rsqrt(jnp.mean(values * values, axis=-1, keepdims=True) + EPSILON)
    return values * factor * scale_gain


def gelu_tanh(values):
    return jax.nn.gelu(values, approximate=True)


def gelu_back(values, grads):
    return jax.vjp(gelu_tanh, values)[1](grads)[0]


def contract_last(left, right):
    return lax.dot_general(left, right, (((1,), (1,)), ((), ())), preferred_element_type=F32)


def contract_first(left, right):
    return lax.dot_general(left, right, (((0,), (0,)), ((), ())), preferred_element_type=F32)


def contract(left, right):
    return jnp.dot(left, right, preferred_element_type=F32)


def conv_apply(padded, taps, offset):
    edge_rows = taps.shape[0] - 1
    length = padded.shape[-2] - edge_rows
    summed = padded[..., edge_rows:, :] * taps[0] + offset
    for back_step in range(1, taps.shape[0]):
        first = edge_rows - back_step
        summed = summed + padded[..., first : first + length, :] * taps[back_step]
    return summed


def swap(value, bit):
    return lax.ppermute(value, "seq", [(i, i ^ bit) for i in range(lax.axis_size("seq"))])


def gather_halves(value):
    half = value.shape[0] // 2
    one = swap(value, 1)
    two = swap(value, 2)
    return value, one, two, swap(one[:half], 2), swap(two[half:], 1)


def gather_seq(value):
    own, one, two, *three = gather_halves(value)
    return own, one, two, jnp.concatenate(three, axis=0)


def assemble_kernel(rows_ref, core_ref, own_ref, one_ref, two_ref, top_ref, bottom_ref, whole_ref, mine_ref, other_ref):
    half = top_ref.shape[0]
    blocks = {
        (0, 0): own_ref[:half], (0, 1): own_ref[half:], (1, 0): one_ref[:half], (1, 1): one_ref[half:],
        (2, 0): two_ref[:half], (2, 1): two_ref[half:], (3, 0): top_ref[...], (3, 1): bottom_ref[...],
    }
    for k, which in enumerate(ORDER):
        whole_ref[pl.ds(pl.multiple_of(rows_ref[k], half), half), :] = blocks[which]

    @pl.when(pl.program_id(1) == 0)
    def _():
        mine_ref[...] = whole_ref[...].T

    @pl.when(pl.program_id(1) == 1)
    def _():
        other_ref[...] = whole_ref[...].T


def assemble(rows, core, blocks, chips, name):
    length, width = 4 * blocks[0].shape[0], blocks[0].shape[1]
    part = width // (2 * chips)
    if part % LANES:
        return assemble_plain(rows, core, blocks, chips)

    def column(i, j, rows, core):
        return (0, 2 * i + (core[0] ^ j))

    def turned():
        return pl.BlockSpec((part, length), lambda i, j, *_: (i, 0))

    return pl.pallas_call(
        assemble_kernel,
        grid_spec=pltpu.PrefetchScalarGridSpec(
            num_scalar_prefetch=2,
            grid=(chips, 2),
            in_specs=[pl.BlockSpec((value.shape[0], part), column) for value in blocks],
            out_specs=[pl.BlockSpec((length, part), column), turned(), turned()],
        ),
        out_shape=[
            jax.ShapeDtypeStruct((length, width), BF),
            jax.ShapeDtypeStruct((width // 2, length), BF),
            jax.ShapeDtypeStruct((width // 2, length), BF),
        ],
        compiler_params=pltpu.CompilerParams(vmem_limit_bytes=32 * 2**20),
        cost_estimate=pl.CostEstimate(flops=0, bytes_accessed=6 * length * width, transcendentals=0),
        name=name,
    )(rows, core, *blocks)


def assemble_plain(rows, core, blocks, chips):
    own, one, two, top, bottom = blocks
    half = top.shape[0]
    halves = {
        (0, 0): own[:half], (0, 1): own[half:], (1, 0): one[:half], (1, 1): one[half:],
        (2, 0): two[:half], (2, 1): two[half:], (3, 0): top, (3, 1): bottom,
    }
    length, width = 8 * half, own.shape[1]
    whole = jnp.zeros((length, width), BF)
    for k, which in enumerate(ORDER):
        whole = lax.dynamic_update_slice_in_dim(whole, halves[which], rows[k], 0)
    turned = whole.T.reshape(chips, 2, width // (2 * chips), length)
    mine, other = (
        lax.dynamic_index_in_dim(turned, which, 1, False).reshape(width // 2, length)
        for which in (core[0], 1 - core[0])
    )
    return whole, mine, other


def scatter_halves(send_one, send_two, keep):
    half = send_one.shape[0] // 2
    from_one = swap(send_one, 1)
    from_two = swap(send_two, 2)
    pass_two = (keep[2 * half : 3 * half] + from_one[:half].astype(F32)).astype(BF)
    pass_one = (keep[3 * half :] + from_two[:half].astype(F32)).astype(BF)
    last_two = swap(pass_two, 2)
    last_one = swap(pass_one, 1)
    near = jnp.concatenate([from_one[half:], from_two[half:]], axis=0).astype(F32)
    far = jnp.concatenate([last_two, last_one], axis=0).astype(F32)
    return keep[: 2 * half] + near + far


def arranged_rows(place, half):
    return jnp.stack([((place ^ step) * 2 + part) * half for step, part in ORDER]).astype(jnp.int32)


def project_kernel(rows_ref, left_ref, right_ref, one_ref, two_ref, keep_ref, order_ref):
    half = left_ref.shape[0] // 8

    @pl.when(pl.program_id(0) == 0)
    def _():
        for k in range(8):
            first = pl.multiple_of(rows_ref[k], half)
            order_ref[k * half : (k + 1) * half, :] = left_ref[pl.ds(first, half), :]

    terms = contract_last(order_ref[...], right_ref[...])
    one_ref[...] = terms[: 2 * half].astype(BF)
    two_ref[...] = terms[2 * half : 4 * half].astype(BF)
    keep_ref[...] = terms[4 * half :]


def project(rows, left, right, column, name):
    length, depth = left.shape
    width = right.shape[0]
    tile = 512
    part = length // 4
    return pl.pallas_call(
        project_kernel,
        grid_spec=pltpu.PrefetchScalarGridSpec(
            num_scalar_prefetch=1,
            grid=(width // tile,),
            in_specs=[
                pl.BlockSpec((length, depth), lambda i, rows: (0, 0), pipeline_mode=pl.Buffered(1)),
                pl.BlockSpec((tile, depth), lambda i, rows: (i, column)),
            ],
            out_specs=[
                pl.BlockSpec((part, tile), lambda i, rows: (0, i)),
                pl.BlockSpec((part, tile), lambda i, rows: (0, i)),
                pl.BlockSpec((2 * part, tile), lambda i, rows: (0, i)),
                pl.BlockSpec((length, depth), lambda i, rows: (0, 0)),
            ],
        ),
        out_shape=[
            jax.ShapeDtypeStruct((part, width), BF),
            jax.ShapeDtypeStruct((part, width), BF),
            jax.ShapeDtypeStruct((2 * part, width), F32),
            jax.ShapeDtypeStruct((length, depth), BF),
        ],
        compiler_params=pltpu.CompilerParams(vmem_limit_bytes=40 * 2**20),
        cost_estimate=pl.CostEstimate(
            flops=2 * length * depth * width,
            bytes_accessed=2 * width * depth + 8 * length * width,
            transcendentals=0,
        ),
        name=name,
    )(rows, left, right)


def swap_core(value):
    return lax.ppermute(value, "seg", [(i, i ^ 1) for i in range(lax.axis_size("seg"))])


def along(value, sources, step):
    pairs = [(2 * i + core, 2 * (i + step) + core) for i in sources for core in range(2)]
    return lax.ppermute(value, "seg", pairs)


def short_chain():
    return lax.axis_size("seg") == 8


def sum_small(value, middle):
    core = lax.axis_index("seg") % 2
    mine = lax.dynamic_index_in_dim(value, core, 0, False)
    if not short_chain():
        return lax.dynamic_index_in_dim(lax.psum(value, "seg"), core, 0, False)
    total = mine.astype(F32) + swap_core(lax.dynamic_index_in_dim(value, 1 - core, 0, False)).astype(F32)
    rows = value.shape[1]
    cut = rows // 32 * 16
    chip = lax.axis_index("seg") // 2 % 2
    low = total.astype(BF)

    def half(which):
        return lax.dynamic_slice_in_dim(low, which * cut, rows - cut, 0)

    def exchange(value, bit):
        return lax.ppermute(value, "seg", [(i, i ^ bit) for i in range(8)])

    part = (half(chip).astype(F32) + after(exchange(half(1 - chip), 2), middle).astype(F32)).astype(BF)
    part = (part.astype(F32) + exchange(part, 4).astype(F32)).astype(BF)
    other = exchange(part, 2)
    shared = rows - 2 * cut
    return jnp.where(
        chip == 0,
        jnp.concatenate([part, other[shared:]], axis=0),
        jnp.concatenate([other, part[shared:]], axis=0),
    )


def sum_all(value):
    if not short_chain():
        return lax.psum(value, ("seq", "seg"))
    for axis, bits in (("seg", (1, 2, 4)), ("seq", (1, 2))):
        for bit in bits:
            pairs = [(i, i ^ bit) for i in range(lax.axis_size(axis))]
            value = value + lax.ppermute(value, axis, pairs)
    return value


def after(value, earlier):
    return lax.optimization_barrier((value, earlier))[0]


def neg_expm1(values):
    total = 1.0 + values * (1.0 / 9.0)
    for order in range(8, 1, -1):
        total = 1.0 + values * (1.0 / order) * total
    return jnp.where(values > -0.7, -values * total, 1.0 - jnp.exp(values))


def scan_kernel(
    blk_ref, low_ref, wd_ref, wi_ref, par_ref, conv_ref, branch_ref,
    states_ref, decay_ref, rate_ref, open_ref, mixed_ref,
):
    length = conv_ref.shape[0]
    par = par_ref[...]
    soft = par[2:3]
    row = lax.broadcasted_iota(jnp.int32, (CHUNK // 8, 8, LANES), 1)

    def body(step, carry):
        rows = pl.ds(pl.multiple_of(step * CHUNK, CHUNK), CHUNK)
        low = low_ref[rows, :]
        rate = jax.nn.sigmoid(contract(low, wd_ref[0]) + par[0:1])
        opened = jax.nn.sigmoid(contract(low, wi_ref[0]) + par[1:2])
        log_decay = -RATE_SCALE * rate * soft
        decay = jnp.exp(log_decay)
        drive = jnp.sqrt(neg_expm1(2.0 * log_decay)) * opened * conv_ref[rows, :]
        rate_ref[rows, :] = rate
        open_ref[rows, :] = opened
        decay_ref[rows, :] = decay
        prod = decay.reshape(CHUNK // 8, 8, LANES)
        total = drive.reshape(CHUNK // 8, 8, LANES)
        for shift in (1, 2, 4):
            inside = row >= shift
            moved = jnp.where(inside, pltpu.roll(total, shift, 1), 0.0)
            total = total + prod * moved
            prod = prod * jnp.where(inside, pltpu.roll(prod, shift, 1), 1.0)
        pieces = []
        for group in range(CHUNK // 8):
            piece = total[group] + prod[group] * carry
            carry = piece[7:8]
            pieces.append(piece)
        states = jnp.concatenate(pieces, axis=0)
        states_ref[rows, :] = states
        mixed_ref[rows, :] = (states * gelu_tanh(branch_ref[rows, :])).astype(BF)
        return carry

    lax.fori_loop(0, length // CHUNK, body, par[3:4])


def scan_forward(blk, conv_ext, decay_w, input_w, params, conv_out, projected):
    length, width = conv_out.shape
    tiles = width // LANES
    tile = pl.BlockSpec((length, LANES), lambda i, blk: (0, i))
    weight = pl.BlockSpec((1, decay_w.shape[1], LANES), lambda i, blk: (i, 0, 0))
    whole = jax.ShapeDtypeStruct((length, width), F32)
    return pl.pallas_call(
        scan_kernel,
        grid_spec=pltpu.PrefetchScalarGridSpec(
            num_scalar_prefetch=1,
            grid=(tiles,),
            in_specs=[
                pl.BlockSpec((length, decay_w.shape[1]), lambda i, blk: (0, blk[i])),
                weight,
                weight,
                pl.BlockSpec((8, LANES), lambda i, blk: (0, i)),
                tile,
                tile,
            ],
            out_specs=[tile] * 5,
        ),
        out_shape=[whole, whole, whole, whole, jax.ShapeDtypeStruct((length, width), BF)],
        compiler_params=pltpu.CompilerParams(vmem_limit_bytes=32 * 2**20),
        cost_estimate=pl.CostEstimate(
            flops=4 * length * width * 256, bytes_accessed=length * width * 28, transcendentals=0
        ),
        name="scan_forward",
    )(blk, conv_ext, decay_w, input_w, params, conv_out, projected)


def back_kernel(
    rows_ref, strip_ref, par_ref, mixed_in, branch_ref, states_ref, decay_ref, rate_ref, open_ref, conv_ref,
    proj_out, gate_out, input_out, direct_out, sums_out, strips_out, mixed_ref,
):
    length = conv_ref.shape[0]
    groups = CHUNK // 8
    par = par_ref[...]
    soft = par[2:3]
    row = lax.broadcasted_iota(jnp.int32, (groups, 8, LANES), 1)
    flat_row = lax.broadcasted_iota(jnp.int32, (CHUNK, LANES), 0)
    steps = length // CHUNK
    half = length // 8
    for k in range(8):
        mixed_ref[pl.ds(pl.multiple_of(rows_ref[k], half), half), :] = mixed_in[k * half : (k + 1) * half, :]

    def body(turn, carried):
        carry, gate_sum, input_sum, logit_sum = carried
        step = steps - 1 - turn
        first = pl.multiple_of(step * CHUNK, CHUNK)
        rows = pl.ds(first, CHUNK)
        mixed_grad = mixed_ref[rows, :]
        branch = branch_ref[rows, :]
        states = states_ref[rows, :]
        decay = decay_ref[rows, :]
        branch_act, pull = jax.vjp(gelu_tanh, branch)
        proj_out[rows, :] = pull(mixed_grad * states)[0].astype(BF)
        state_grad = mixed_grad * branch_act
        prod = decay.reshape(groups, 8, LANES)
        total = (decay * state_grad).reshape(groups, 8, LANES)
        for shift in (1, 2, 4):
            inside = row < 8 - shift
            moved = jnp.where(inside, pltpu.roll(total, 8 - shift, 1), 0.0)
            total = total + prod * moved
            prod = prod * jnp.where(inside, pltpu.roll(prod, 8 - shift, 1), 1.0)
        pieces = [None] * groups
        after = carry
        for group in reversed(range(groups)):
            piece = total[group] + prod[group] * after
            after = piece[0:1]
            pieces[group] = piece
        passed = jnp.concatenate(pieces, axis=0)
        shifted = jnp.where(flat_row == CHUNK - 1, carry, pltpu.roll(passed, CHUNK - 1, 0))
        adjoint = state_grad + shifted
        before = states_ref[pl.ds(pl.multiple_of(jnp.maximum(first - 8, 0), 8), 8), :][7:8]
        before = jnp.where(step == 0, par[3:4], before)
        previous = jnp.where(flat_row == 0, before, pltpu.roll(states, 1, 0))
        rate = rate_ref[rows, :]
        opened = open_ref[rows, :]
        conv = conv_ref[rows, :]
        log_decay = -RATE_SCALE * rate * soft
        scale = jnp.sqrt(neg_expm1(2.0 * log_decay))
        opened_conv = opened * conv
        ratio = jnp.where(scale > 0.0, decay / scale, 0.0)
        log_grad = decay * (adjoint * previous - adjoint * opened_conv * ratio)
        scaled = adjoint * scale
        direct_out[rows, :] = scaled * opened
        input_grad = (scaled * conv * opened * (1.0 - opened)).astype(BF)
        rate_grad = log_grad * rate
        gate_grad = (rate_grad * (1.0 - rate) * (-RATE_SCALE * soft)).astype(BF)
        gate_out[rows, :] = gate_grad
        input_out[rows, :] = input_grad

        def folded(value):
            return jnp.sum(value.astype(F32).reshape(groups, 8, LANES), axis=0)

        return (
            after,
            gate_sum + folded(gate_grad),
            input_sum + folded(input_grad),
            logit_sum + folded(rate_grad),
        )

    zero = jnp.zeros((8, LANES), F32)
    after, gate_sum, input_sum, logit_sum = lax.fori_loop(
        0, steps, body, (jnp.zeros((1, LANES), F32), zero, zero, zero)
    )
    sums_out[...] = jnp.concatenate(
        [
            jnp.sum(gate_sum, axis=0, keepdims=True),
            jnp.sum(input_sum, axis=0, keepdims=True),
            jnp.sum(logit_sum, axis=0, keepdims=True) * (-RATE_SCALE * par[4:5]),
            after,
            jnp.zeros((4, LANES), F32),
        ],
        axis=0,
    )

    @pl.when(pl.program_id(0) == strip_ref[0])
    def _():
        strips_out[0] = gate_out[...]
        strips_out[1] = input_out[...]


def scan_backward(rows, strip_tile, params, mixed_grad, projected, states, decays, rate, opened, conv_out):
    length, width = conv_out.shape
    tiles = width // LANES
    tile = pl.BlockSpec((length, LANES), lambda i, *_: (0, i))
    small = pl.BlockSpec((8, LANES), lambda i, *_: (0, i))
    low = jax.ShapeDtypeStruct((length, width), BF)
    return pl.pallas_call(
        back_kernel,
        grid_spec=pltpu.PrefetchScalarGridSpec(
            num_scalar_prefetch=2,
            grid=(tiles,),
            in_specs=[
                small,
            ]
            + [tile] * 7,
            out_specs=[tile] * 4 + [small, pl.BlockSpec((2, length, LANES), lambda i, *_: (0, 0, 0))],
            scratch_shapes=[pltpu.VMEM((length, LANES), F32)],
        ),
        out_shape=[
            jax.ShapeDtypeStruct((length, 2 * width), BF),
            low,
            low,
            jax.ShapeDtypeStruct((length, width), F32),
            jax.ShapeDtypeStruct((8, width), F32),
            jax.ShapeDtypeStruct((2, length, LANES), BF),
        ],
        compiler_params=pltpu.CompilerParams(vmem_limit_bytes=40 * 2**20),
        cost_estimate=pl.CostEstimate(
            flops=100 * length * width, bytes_accessed=length * width * 44, transcendentals=0
        ),
        name="scan_backward",
    )(rows, strip_tile, params, mixed_grad, projected, states, decays, rate, opened, conv_out)


def gates_kernel(
    blk_ref, near_ref, edge_ref, par_ref, sums_ref, gate_ref, gate_near, input_ref, input_near, strips_ref,
    wd_ref, wi_ref, direct_ref, low_t_ref, conv_in_ref, proj_in, proj_out, small_out, single_out,
):
    length = direct_ref.shape[0]
    block = low_t_ref.shape[0]
    edge = edge_ref[pl.program_id(0)] == 1
    gate, opened = gate_ref[...], input_ref[...]
    gate_both = jnp.concatenate([gate, jnp.where(edge, strips_ref[0], gate_near[...])], axis=1)
    input_both = jnp.concatenate([opened, jnp.where(edge, strips_ref[1], input_near[...])], axis=1)
    conv_grad = direct_ref[...] + contract_last(gate_both, wd_ref[0]) + contract_last(input_both, wi_ref[0])
    row = lax.broadcasted_iota(jnp.int32, (length, LANES), 0)
    par = par_ref[...]
    conv_in = conv_in_ref[...]
    conv_in_grad = par[0:1] * conv_grad
    tap_sums = [jnp.sum(conv_grad * conv_in, axis=0, keepdims=True)]
    for k in range(1, 4):
        moved = jnp.where(row < length - k, pltpu.roll(conv_grad, length - k, 0), 0.0)
        conv_in_grad = conv_in_grad + par[k : k + 1] * moved
        total = jnp.sum(moved * conv_in, axis=0, keepdims=True)
        for t in range(k):
            total = total + conv_grad[t : t + 1] * par[7 + t - k : 8 + t - k]
        tap_sums.append(total)
    proj_out[...] = conv_in_grad.astype(BF)
    window = []
    for s in range(3):
        total = par[3 - s : 4 - s] * conv_grad[0:1]
        for k in range(4 - s, 4):
            total = total + par[k : k + 1] * conv_grad[s - 3 + k : s - 2 + k]
        window.append(total)
    sums = sums_ref[...]
    zero = jnp.zeros((8, LANES), F32)
    vectors = jnp.concatenate(
        tap_sums + [jnp.sum(conv_grad, axis=0, keepdims=True), sums[0:3], zero], axis=0
    ).astype(BF)
    low_t = low_t_ref[...]
    small_out[0, :block, :] = contract(low_t, gate).astype(BF)
    small_out[1, :block, :] = contract(low_t, opened).astype(BF)
    small_out[0, block:, :] = vectors
    small_out[1, block:, :] = vectors
    single_out[...] = jnp.concatenate([sums[3:4]] + window + [zero, zero[:4]], axis=0).astype(BF)


def gates_backward(blk, near, edge, params, sums, gate, opened, strips, decay_w, input_w, direct, low_t, projected, proj):
    length, width = direct.shape
    tiles = width // LANES
    block = decay_w.shape[2]
    tile = pl.BlockSpec((length, LANES), lambda i, *_: (0, i))
    beside = pl.BlockSpec((length, LANES), lambda i, blk, near, edge: (0, near[i]))
    small = pl.BlockSpec((8, LANES), lambda i, *_: (0, i))
    weight = pl.BlockSpec((1, LANES, block), lambda i, *_: (i, 0, 0))
    second = pl.BlockSpec((length, LANES), lambda i, *_: (0, tiles + i))
    return pl.pallas_call(
        gates_kernel,
        grid_spec=pltpu.PrefetchScalarGridSpec(
            num_scalar_prefetch=3,
            grid=(tiles,),
            in_specs=[
                small,
                small,
                tile,
                beside,
                tile,
                beside,
                pl.BlockSpec(strips.shape, lambda i, *_: (0, 0, 0)),
                weight,
                weight,
                tile,
                pl.BlockSpec((block, length), lambda i, blk, near, edge: (blk[i], 0)),
                second,
                pl.BlockSpec(memory_space=pl.ANY),
            ],
            out_specs=[
                second,
                pl.BlockSpec((2, block + 16, LANES), lambda i, *_: (0, 0, i)),
                pl.BlockSpec((16, LANES), lambda i, *_: (0, i)),
            ],
        ),
        out_shape=[
            jax.ShapeDtypeStruct(proj.shape, BF),
            jax.ShapeDtypeStruct((2, block + 16, width), BF),
            jax.ShapeDtypeStruct((16, width), BF),
        ],
        input_output_aliases={15: 0},
        compiler_params=pltpu.CompilerParams(vmem_limit_bytes=32 * 2**20),
        cost_estimate=pl.CostEstimate(
            flops=8 * length * width * block, bytes_accessed=length * width * 20, transcendentals=0
        ),
        name="gates_backward",
    )(blk, near, edge, params, sums, gate, gate, opened, opened, strips, decay_w, input_w, direct, low_t, projected, proj)


def mlp_data(tile, low_ref, cot_ref, weight_ref):
    gate_up = contract(low_ref[...], weight_ref[:, : 2 * tile])
    hidden_grad = contract(cot_ref[...], weight_ref[:, 2 * tile :])
    gate_val, up_val = gate_up[:, :tile], gate_up[:, tile:]
    gate_act, pull = jax.vjp(gelu_tanh, gate_val)
    hidden = (gate_act * up_val).astype(BF)
    gate_grad = pull(hidden_grad * up_val)[0].astype(BF)
    up_grad = (hidden_grad * gate_act).astype(BF)
    return jnp.concatenate([gate_grad, up_grad], axis=1), hidden


def add_term(total_ref, term):
    @pl.when(pl.program_id(0) == 0)
    def _():
        total_ref[...] = term

    @pl.when(pl.program_id(0) > 0)
    def _():
        total_ref[...] += term


def give_halves(total_ref, before_ref, one_ref, two_ref, keep_ref):
    @pl.when(pl.program_id(0) == pl.num_programs(0) - 1)
    def _():
        part = total_ref.shape[0] // 4
        one_ref[...] = (total_ref[:part] + before_ref[:part]).astype(BF)
        two_ref[...] = (total_ref[part : 2 * part] + before_ref[part : 2 * part]).astype(BF)
        keep_ref[...] = total_ref[2 * part :] + before_ref[2 * part :]


def mlp_first_kernel(tile, low_ref, cot_ref, weight_ref, units_ref, back_ref, out_ref):
    both, hidden = mlp_data(tile, low_ref, cot_ref, weight_ref)
    units_ref[:, : 2 * tile] = both
    units_ref[:, 2 * tile :] = hidden
    add_term(back_ref, contract_last(both, weight_ref[:, : 2 * tile]))
    add_term(out_ref, contract_last(hidden, weight_ref[:, 2 * tile :]))


def mlp_last_kernel(tile, low_ref, cot_ref, weight_ref, before_ref, units_ref, one_ref, two_ref, keep_ref, back_ref):
    both, hidden = mlp_data(tile, low_ref, cot_ref, weight_ref)
    units_ref[:, : 2 * tile] = both
    units_ref[:, 2 * tile :] = hidden
    add_term(back_ref, contract_last(both, weight_ref[:, : 2 * tile]))
    give_halves(back_ref, before_ref, one_ref, two_ref, keep_ref)


def mlp_out_kernel(tile, weight_ref, units_ref, before_ref, one_ref, two_ref, keep_ref, out_ref):
    add_term(out_ref, contract_last(units_ref[:, 2 * tile :], weight_ref[:, 2 * tile :]))
    give_halves(out_ref, before_ref, one_ref, two_ref, keep_ref)


def mlp_grad_kernel(tile, low_ref, low_other, cot_ref, cot_other, units_ref, units_other, grad_ref):
    cut = 2 * tile
    grad_ref[:, :cut] = (
        contract(low_ref[...], units_ref[:, :cut]) + contract(low_other[...], units_other[:, :cut])
    ).astype(BF)
    grad_ref[:, cut:] = (
        contract(cot_ref[...], units_ref[:, cut:]) + contract(cot_other[...], units_other[:, cut:])
    ).astype(BF)


def recur_grad_kernel(
    low_ref, low_other, mixer_ref, mixer_other, proj_ref, proj_other, mixed_ref, mixed_other, held_ref, grad_ref
):
    step = pl.program_id(0)

    @pl.when(step < 2)
    def _():
        grad_ref[...] = (
            contract(low_ref[...], proj_ref[...]) + contract(low_other[...], proj_other[...])
        ).astype(BF)

    @pl.when(step == 2)
    def _():
        grad_ref[...] = (
            contract(mixer_ref[...], mixed_ref[...]) + contract(mixer_other[...], mixed_other[...])
        ).astype(BF)


def recur_grad(low_t, mixer_t, proj, mixed, held):
    depth, length = low_t[0].shape
    width = mixed[0].shape[1]
    fixed = pl.BlockSpec((depth, length), lambda i: (0, 0), pipeline_mode=pl.Buffered(1))
    moving = pl.BlockSpec((length, width), lambda i: (0, jnp.minimum(i, 1)))
    whole = pl.BlockSpec((length, width), lambda i: (0, 0))
    return pl.pallas_call(
        recur_grad_kernel,
        grid=(3,),
        in_specs=[fixed] * 4 + [moving] * 2 + [whole] * 2 + [pl.BlockSpec(memory_space=pl.ANY)],
        out_specs=pl.BlockSpec((depth, width), lambda i: (0, i)),
        out_shape=jax.ShapeDtypeStruct(held.shape, BF),
        input_output_aliases={8: 0},
        compiler_params=pltpu.CompilerParams(vmem_limit_bytes=40 * 2**20),
        cost_estimate=pl.CostEstimate(
            flops=12 * depth * length * width, bytes_accessed=6 * depth * width + 8 * depth * length, transcendentals=0
        ),
        name="recur_grad",
    )(*low_t, *mixer_t, *proj, *mixed, held)


def mlp_grad_beside_kernel(
    tile, first, low_ref, low_other, cot_ref, cot_other, units_ref, units_other, held_ref, grad_ref, sem
):
    mlp_grad_kernel(tile, low_ref, low_other, cot_ref, cot_other, units_ref, units_other, grad_ref)
    columns = pl.ds(pl.multiple_of(first + pl.program_id(0) * 3 * tile, LANES), 3 * tile)
    copy = pltpu.make_async_copy(grad_ref, held_ref.at[:, columns], sem)
    copy.start()
    copy.wait()


def mlp_grad_beside(tile, low_t, cot_t, units, first):
    (depth, rows), columns = low_t[0].shape, units[0].shape[1]
    fixed = pl.BlockSpec((depth, rows), lambda i: (0, 0), pipeline_mode=pl.Buffered(1))
    moving = pl.BlockSpec((rows, 3 * tile), lambda i: (0, i))
    return pl.pallas_call(
        lambda *refs: mlp_grad_beside_kernel(tile, first, *refs),
        grid=(columns // (3 * tile),),
        in_specs=[fixed] * 4 + [moving] * 2,
        out_specs=pl.BlockSpec(memory_space=pl.ANY),
        out_shape=jax.ShapeDtypeStruct((depth, first + columns), BF),
        scratch_shapes=[pltpu.VMEM((depth, 3 * tile), BF), pltpu.SemaphoreType.DMA],
        compiler_params=pltpu.CompilerParams(vmem_limit_bytes=40 * 2**20),
        cost_estimate=pl.CostEstimate(
            flops=4 * rows * depth * columns, bytes_accessed=2 * depth * columns + 8 * rows * depth, transcendentals=0
        ),
        name="mlp_grad_last",
    )(*low_t, *cot_t, *units)


def unpack_kernel(tile, first, sums_ref, in_held, out_held, feed_in_ref, feed_out_ref, recur_in_ref, recur_out_ref):
    width = recur_out_ref.shape[1]
    for i in range(2):
        recur_in_ref[:, i, :] = sums_ref[:, i * width : (i + 1) * width].astype(F32)
    recur_out_ref[...] = sums_ref[:, 2 * width : 3 * width].astype(F32)
    for k in range(feed_out_ref.shape[1] // tile):
        at = slice(k * tile, (k + 1) * tile)
        start = first + 3 * tile * k
        for i in range(2):
            feed_in_ref[:, i, at] = sums_ref[:, start + i * tile : start + (i + 1) * tile].astype(F32)
        feed_out_ref[:, at] = sums_ref[:, start + 2 * tile : start + 3 * tile].astype(F32)


def unpack(tile, sums, feed_in, feed_out, recur_width, done):
    rows = sums.shape[0]
    units = feed_out.shape[1]
    part = units - done
    anywhere = pl.BlockSpec(memory_space=pl.ANY)
    return pl.pallas_call(
        lambda *refs: unpack_kernel(tile, 3 * recur_width, *refs),
        grid=(1,),
        in_specs=[pl.BlockSpec(sums.shape, lambda i: (0, 0)), anywhere, anywhere],
        out_specs=[
            pl.BlockSpec((rows, 2, part), lambda i: (0, 0, done // part)),
            pl.BlockSpec((rows, part), lambda i: (0, done // part)),
            pl.BlockSpec((rows, 2, recur_width), lambda i: (0, 0, 0)),
            pl.BlockSpec((rows, recur_width), lambda i: (0, 0)),
        ],
        out_shape=[
            jax.ShapeDtypeStruct(feed_in.shape, F32),
            jax.ShapeDtypeStruct(feed_out.shape, F32),
            jax.ShapeDtypeStruct((rows, 2, recur_width), F32),
            jax.ShapeDtypeStruct((rows, recur_width), F32),
        ],
        input_output_aliases={1: 0, 2: 1},
        compiler_params=pltpu.CompilerParams(vmem_limit_bytes=40 * 2**20),
        cost_estimate=pl.CostEstimate(flops=0, bytes_accessed=6 * rows * sums.shape[1], transcendentals=0),
        name="unpack",
    )(sums, feed_in, feed_out)


def mlp_call(kernel, tile, products, rows, width, columns, fixed_in, moving_in, fixed_out, moving_out, scratch, name):
    def fixed(shape, single):
        return pl.BlockSpec(shape, lambda i: (0, 0), pipeline_mode=pl.Buffered(1) if single else None)

    def moving(shape):
        return pl.BlockSpec((shape[0], 3 * tile), lambda i: (0, i))

    return pl.pallas_call(
        lambda *refs: kernel(tile, *refs),
        grid=(columns // (3 * tile),),
        in_specs=[
            fixed(value.shape, True) if kind == "fixed" else moving(value.shape)
            for kind, value in fixed_in + moving_in
        ],
        out_specs=[moving(shape) for shape, _ in moving_out] + [fixed(shape, False) for shape, _ in fixed_out],
        out_shape=[jax.ShapeDtypeStruct(shape, kind) for shape, kind in moving_out + fixed_out],
        scratch_shapes=[pltpu.VMEM(shape, kind) for shape, kind in scratch],
        compiler_params=pltpu.CompilerParams(vmem_limit_bytes=60 * 2**20),
        cost_estimate=pl.CostEstimate(
            flops=2 * products * rows * width * columns // 3,
            bytes_accessed=4 * width * columns + 16 * rows * width,
            transcendentals=0,
        ),
        name=name,
    )(*[value for _, value in fixed_in + moving_in])


def half_shapes(rows, width):
    part = rows // 4
    return [((part, width), BF), ((part, width), BF), ((2 * part, width), F32)]


def mlp_first(tile, low2, cot, weight):
    (rows, width), columns = low2.shape, weight.shape[1]
    ins = [("fixed", low2), ("fixed", cot), ("moving", weight)]
    return mlp_call(
        mlp_first_kernel, tile, 6, rows, width, columns, ins, [],
        [((rows, width), F32)] * 2, [((rows, columns), BF)], [], "mlp_first",
    )


def mlp_last(tile, low2, cot, weight, before):
    (rows, width), columns = low2.shape, weight.shape[1]
    ins = [("fixed", low2), ("fixed", cot), ("moving", weight), ("fixed", before)]
    return mlp_call(
        mlp_last_kernel, tile, 5, rows, width, columns, ins, [],
        half_shapes(rows, width), [((rows, columns), BF)], [((rows, width), F32)], "mlp_last",
    )


def mlp_out_last(tile, weight, units, before):
    (width, columns), rows = weight.shape, units.shape[0]
    ins = [("moving", weight), ("moving", units), ("fixed", before)]
    return mlp_call(
        mlp_out_kernel, tile, 1, rows, width, columns, ins, [],
        half_shapes(rows, width), [], [((rows, width), F32)], "mlp_out",
    )


def mlp_grad(tile, low_t, cot_t, units):
    (depth, rows), columns = low_t[0].shape, units[0].shape[1]
    ins = [("fixed", value) for value in (*low_t, *cot_t)] + [("moving", value) for value in units]
    return mlp_call(
        mlp_grad_kernel, tile, 3, rows, 2 * depth, columns, ins, [],
        [], [((depth, columns), BF)], [], "mlp_grad",
    )[0]


def shards(
    tokens,
    cotangent,
    start_state,
    start_window,
    first_gain,
    recur_in,
    conv_taps,
    conv_bias,
    decay_gate,
    input_gate,
    decay_bias,
    input_bias,
    decay_logit,
    recur_out,
    second_gain,
    feed_in,
    feed_out,
):
    segments, length, model_width = tokens.shape
    recur_width = conv_taps.shape[1]
    head_count, block_size = decay_gate.shape[:2]
    edge_rows = conv_taps.shape[0] - 1
    seq_parts = lax.axis_size("seq")
    place = lax.axis_index("seq")
    own_rows, _, recur_part = recur_in.shape
    feed_part = feed_in.shape[2]
    first_channel = place * recur_part
    first_block = first_channel // block_size
    block_count = -(-recur_part // block_size)
    strip = block_count * block_size - recur_part
    odd = place % 2 == 1

    def own(value):
        return lax.dynamic_slice_in_dim(value, first_channel, recur_part, value.ndim - 1)

    def strip_of(value):
        return jnp.where(odd, value[:, :strip], value[:, recur_part - strip :])

    def gather_seg(value):
        return lax.all_gather(value, "seg", axis=0, tiled=True)

    seg_parts = lax.axis_size("seg")
    core = lax.axis_index("seg") % 2

    def scatter_rows(value):
        groups = [list(range(c, seg_parts, 2)) for c in range(2)]
        return lax.psum_scatter(value, "seg", scatter_dimension=0, tiled=True, axis_index_groups=groups)

    def gathered(blocks, rows, name):
        whole, mine, other = assemble(rows, core[None].astype(jnp.int32), blocks, seg_parts // 2, name)
        return whole, (mine, swap_core(other))

    def of_both(value):
        return value, swap_core(value)

    unit = 2 * LANES
    first_part = 2 * feed_part // 3 // unit * unit
    cuts = [(0, first_part), (first_part, feed_part)]

    def feed_columns(first, count):
        return [feed_in[:, 0, first : first + count], feed_in[:, 1, first : first + count], feed_out[:, first : first + count]]

    feeds = [
        jnp.concatenate([c for first in range(a, b, unit) for c in feed_columns(first, unit)], axis=1)
        for a, b in cuts
    ]
    recur = gather_seg(jnp.concatenate([recur_in.reshape(own_rows, 2 * recur_part), recur_out], axis=1))
    feed_first = gather_seg(feeds[0])
    feed_last = gather_seg(feeds[1])

    inputs = tokens.astype(F32).reshape(length, model_width)
    upstream = cotangent.reshape(length, model_width)
    low1 = rms_norm(inputs, first_gain).astype(BF)
    rows = arranged_rows(place, length // 2)
    straight = jnp.arange(8, dtype=jnp.int32) * (length // 2)
    all_low1, low1_rows = gathered(gather_halves(low1), rows, "gather_low1")
    all_cot, cot_rows = gathered(gather_halves(upstream), straight, "gather_cot")

    taps = own(conv_taps)
    logit = own(decay_logit[None])
    params = jnp.concatenate(
        [
            own(decay_bias[None]),
            own(input_bias[None]),
            jax.nn.softplus(logit),
            own(start_state),
            jax.nn.sigmoid(logit),
            jnp.zeros((3, recur_part), F32),
        ],
        axis=0,
    )
    window = own(start_window)[0]
    conv_params = jnp.concatenate([taps, window, jnp.zeros((1, recur_part), F32)], axis=0)
    tiles = recur_part // LANES
    halves = block_size // LANES
    first_tile = jnp.where(odd, strip // LANES, 0)
    tile_place = first_tile + jnp.arange(tiles)
    tile_block = (tile_place // halves).astype(jnp.int32)
    near = (tile_place ^ 1) - first_tile
    edge = ((near < 0) | (near >= tiles)).astype(jnp.int32)
    near = jnp.clip(near, 0, tiles - 1).astype(jnp.int32)
    strip_tile = jnp.where(odd, 0, tiles - 1).astype(jnp.int32)[None]

    def gate_tiles(blocks):
        blocks = lax.dynamic_slice_in_dim(blocks, first_block, block_count, 0)
        columns = blocks.reshape(block_count, block_size, halves, LANES).transpose(0, 2, 1, 3)
        columns = columns.reshape(block_count * halves, block_size, LANES)
        lines = blocks.reshape(block_count * halves, LANES, block_size)
        turned = jnp.concatenate([lines[:, :, LANES:], lines[:, :, :LANES]], axis=2)
        swapped = (jnp.arange(block_count * halves) % 2 == 1)[:, None, None]
        lines = jnp.where(swapped, turned, lines)
        return (
            lax.dynamic_slice_in_dim(columns, first_tile, tiles, 0),
            lax.dynamic_slice_in_dim(lines, first_tile, tiles, 0),
        )

    decay_columns, decay_lines = gate_tiles(decay_gate)
    input_columns, input_lines = gate_tiles(input_gate)

    projected = contract(all_low1, recur[:, : 2 * recur_part])
    padded = jnp.concatenate([window, projected[:, recur_part:]], axis=0)
    conv_out = conv_apply(padded, taps, own(conv_bias[None]))
    conv_low = conv_out.astype(BF)
    arrived = swap(strip_of(conv_low), 1)
    conv_ext = jnp.where(
        odd,
        jnp.concatenate([arrived, conv_low], axis=1),
        jnp.concatenate([conv_low, arrived], axis=1),
    )
    states, decays, rate, opened, mixed_low = scan_forward(
        tile_block, conv_ext, decay_columns, input_columns, params, conv_out, projected
    )
    *pieces, mixed_low = project(rows, mixed_low, recur, 2, "mixer_out")
    residual = inputs + scatter_halves(*pieces)

    low2 = rms_norm(residual, second_gain).astype(BF)
    all_low2, low2_rows = gathered(gather_halves(low2), straight, "gather_low2")
    units, back_first, out_first = mlp_first(unit, all_low2, all_cot, feed_first)
    grad_first = scatter_rows(mlp_grad(unit, low2_rows, cot_rows, of_both(units)))
    units, *pieces = mlp_last(unit, all_low2, all_cot, feed_last, back_first)
    normed2_grad = scatter_halves(*pieces)
    units_last = units
    residual_norm_grad, second_gain_grad = jax.vjp(rms_norm, residual, second_gain)[1](normed2_grad)
    residual_grad = upstream.astype(F32) + residual_norm_grad

    mixer_blocks = gather_halves(residual_grad.astype(BF))
    held = mlp_grad_beside(unit, low2_rows, cot_rows, of_both(units_last), 3 * recur_part)
    mixer_grad, mixer_rows = gathered(after(mixer_blocks, held), straight, "gather_mixer")
    proj_grad, gate_low_grad, input_low_grad, conv_direct, sums, strips = scan_backward(
        rows, strip_tile, params, contract(mixer_grad, recur[:, 2 * recur_part :]), projected, states, decays, rate,
        opened, conv_out,
    )
    proj_grad, small, single = gates_backward(
        tile_block, near, edge, conv_params, sums, gate_low_grad, input_low_grad, swap(strips, 1),
        decay_lines, input_lines, conv_direct, conv_ext.T, projected, proj_grad,
    )
    mlp_term = scatter_halves(*mlp_out_last(unit, feed_last, after(units_last, proj_grad), out_first))
    output = (residual + mlp_term).astype(BF).reshape(tokens.shape)
    grad_last_term = recur_grad(low1_rows, mixer_rows, of_both(proj_grad), of_both(mixed_low), held)
    *pieces, _ = project(rows, after(proj_grad, grad_last_term), recur, 0, "normed1_grad")
    normed1_grad = scatter_halves(*pieces)
    input_norm_grad, first_gain_grad = jax.vjp(rms_norm, inputs, first_gain)[1](normed1_grad)
    input_grad = (residual_grad + input_norm_grad).astype(BF).reshape(tokens.shape)

    grad_last = scatter_rows(after(grad_last_term, grad_first))

    def columns_of(value, which, start):
        return jnp.concatenate(
            [value[:, at : at + unit] for at in range(start + which * unit, value.shape[1], 3 * unit)], axis=1
        ).astype(F32)

    def feed_grads(value, start):
        return jnp.stack([columns_of(value, i, start) for i in range(2)], axis=1), columns_of(value, 2, start)

    feed_in_first, feed_out_first = feed_grads(grad_first, 0)
    feed_in_grad = jnp.pad(feed_in_first, ((0, 0), (0, 0), (0, feed_part - first_part)))
    feed_out_grad = jnp.pad(feed_out_first, ((0, 0), (0, feed_part - first_part)))
    grad_last = after(grad_last, (feed_in_grad, feed_out_grad))
    feed_in_grad, feed_out_grad, recur_in_grad, recur_out_grad = unpack(
        unit, grad_last, feed_in_grad, feed_out_grad, recur_part, first_part
    )

    mine = gather_seq(jnp.concatenate([sum_small(small, grad_last_term), single], axis=0))
    swapped = [jnp.where(odd, mine[i ^ 1], mine[i]) for i in range(4)]
    mine = jnp.concatenate([jnp.where(place >= 2, swapped[i ^ 2], swapped[i]) for i in range(4)], axis=1)
    vectors = mine[block_size:].astype(F32)
    other = swap_core(mine[:block_size])

    def as_blocks(which):
        value = jnp.where(core == which, mine[:block_size], other).astype(F32)
        return value.reshape(block_size, head_count, block_size).transpose(1, 0, 2)

    gains = sum_all(jnp.stack([first_gain_grad, second_gain_grad]))
    kernel_taps = conv_taps.shape[0]
    return (
        output,
        input_grad,
        vectors[16:17],
        vectors[17 : 17 + edge_rows][None],
        gains[0],
        recur_in_grad,
        vectors[:kernel_taps],
        vectors[kernel_taps],
        as_blocks(0),
        as_blocks(1),
        vectors[kernel_taps + 1],
        vectors[kernel_taps + 2],
        vectors[kernel_taps + 3],
        recur_out_grad,
        gains[1],
        feed_in_grad,
        feed_out_grad,
    )


def solution(mesh):
    placed = (
        P("seg", "seq", None),
        P("seg", "seq", None),
        P("seg", None),
        P("seg", None, None),
        P(),
        P("seg", None, "seq"),
        P(),
        P(),
        P(),
        P(),
        P(),
        P(),
        P(),
        P("seg", "seq"),
        P(),
        P("seg", None, "seq"),
        P("seg", "seq"),
    )
    return jax.shard_map(
        shards,
        mesh=mesh,
        in_specs=placed,
        out_specs=(
            P("seg", "seq", None),
            P("seg", "seq", None),
            P("seg", None),
            P("seg", None, None),
            P(),
            P("seg", None, "seq"),
            P(),
            P(),
            P(),
            P(),
            P(),
            P(),
            P(),
            P("seg", "seq"),
            P(),
            P("seg", None, "seq"),
            P("seg", "seq"),
        ),
        check_vma=False,
    )
```

```python
import jax
import jax.numpy as jnp
from jax import lax
from jax.experimental import pallas as pl
from jax.experimental.pallas import tpu as pltpu
from jax.sharding import PartitionSpec as P

EPSILON = 1e-06
RATE_SCALE = 8.0
LANES = 128
CHUNK = 64
BF = jnp.bfloat16
F32 = jnp.float32
ORDER = [(3, 0), (1, 0), (3, 1), (2, 1), (0, 0), (0, 1), (2, 0), (1, 1)]


def rms_norm(values, scale_gain):
    factor = lax.rsqrt(jnp.mean(values * values, axis=-1, keepdims=True) + EPSILON)
    return values * factor * scale_gain


def gelu_tanh(values):
    return jax.nn.gelu(values, approximate=True)


def gelu_back(values, grads):
    return jax.vjp(gelu_tanh, values)[1](grads)[0]


def contract_last(left, right):
    return lax.dot_general(left, right, (((1,), (1,)), ((), ())), preferred_element_type=F32)


def contract_first(left, right):
    return lax.dot_general(left, right, (((0,), (0,)), ((), ())), preferred_element_type=F32)


def contract(left, right):
    return jnp.dot(left, right, preferred_element_type=F32)


def conv_apply(padded, taps, offset):
    edge_rows = taps.shape[0] - 1
    length = padded.shape[-2] - edge_rows
    summed = padded[..., edge_rows:, :] * taps[0] + offset
    for back_step in range(1, taps.shape[0]):
        first = edge_rows - back_step
        summed = summed + padded[..., first : first + length, :] * taps[back_step]
    return summed


def swap(value, bit):
    return lax.ppermute(value, "seq", [(i, i ^ bit) for i in range(lax.axis_size("seq"))])


def gather_halves(value):
    half = value.shape[0] // 2
    one = swap(value, 1)
    two = swap(value, 2)
    return value, one, two, swap(one[:half], 2), swap(two[half:], 1)


def gather_seq(value):
    own, one, two, *three = gather_halves(value)
    return own, one, two, jnp.concatenate(three, axis=0)


def assemble_kernel(rows_ref, core_ref, own_ref, one_ref, two_ref, top_ref, bottom_ref, whole_ref, mine_ref, other_ref):
    half = top_ref.shape[0]
    blocks = {
        (0, 0): own_ref[:half], (0, 1): own_ref[half:], (1, 0): one_ref[:half], (1, 1): one_ref[half:],
        (2, 0): two_ref[:half], (2, 1): two_ref[half:], (3, 0): top_ref[...], (3, 1): bottom_ref[...],
    }
    for k, which in enumerate(ORDER):
        whole_ref[pl.ds(pl.multiple_of(rows_ref[k], half), half), :] = blocks[which]

    @pl.when(pl.program_id(1) == 0)
    def _():
        mine_ref[...] = whole_ref[...].T

    @pl.when(pl.program_id(1) == 1)
    def _():
        other_ref[...] = whole_ref[...].T


def assemble(rows, core, blocks, chips, name):
    length, width = 4 * blocks[0].shape[0], blocks[0].shape[1]
    part = width // (2 * chips)
    if part % LANES:
        return assemble_plain(rows, core, blocks, chips)

    def column(i, j, rows, core):
        return (0, 2 * i + (core[0] ^ j))

    def turned():
        return pl.BlockSpec((part, length), lambda i, j, *_: (i, 0))

    return pl.pallas_call(
        assemble_kernel,
        grid_spec=pltpu.PrefetchScalarGridSpec(
            num_scalar_prefetch=2,
            grid=(chips, 2),
            in_specs=[pl.BlockSpec((value.shape[0], part), column) for value in blocks],
            out_specs=[pl.BlockSpec((length, part), column), turned(), turned()],
        ),
        out_shape=[
            jax.ShapeDtypeStruct((length, width), BF),
            jax.ShapeDtypeStruct((width // 2, length), BF),
            jax.ShapeDtypeStruct((width // 2, length), BF),
        ],
        compiler_params=pltpu.CompilerParams(vmem_limit_bytes=32 * 2**20),
        cost_estimate=pl.CostEstimate(flops=0, bytes_accessed=6 * length * width, transcendentals=0),
        name=name,
    )(rows, core, *blocks)


def assemble_plain(rows, core, blocks, chips):
    own, one, two, top, bottom = blocks
    half = top.shape[0]
    halves = {
        (0, 0): own[:half], (0, 1): own[half:], (1, 0): one[:half], (1, 1): one[half:],
        (2, 0): two[:half], (2, 1): two[half:], (3, 0): top, (3, 1): bottom,
    }
    length, width = 8 * half, own.shape[1]
    whole = jnp.zeros((length, width), BF)
    for k, which in enumerate(ORDER):
        whole = lax.dynamic_update_slice_in_dim(whole, halves[which], rows[k], 0)
    turned = whole.T.reshape(chips, 2, width // (2 * chips), length)
    mine, other = (
        lax.dynamic_index_in_dim(turned, which, 1, False).reshape(width // 2, length)
        for which in (core[0], 1 - core[0])
    )
    return whole, mine, other


def scatter_halves(send_one, send_two, keep):
    half = send_one.shape[0] // 2
    from_one = swap(send_one, 1)
    from_two = swap(send_two, 2)
    pass_two = (keep[2 * half : 3 * half] + from_one[:half].astype(F32)).astype(BF)
    pass_one = (keep[3 * half :] + from_two[:half].astype(F32)).astype(BF)
    last_two = swap(pass_two, 2)
    last_one = swap(pass_one, 1)
    near = jnp.concatenate([from_one[half:], from_two[half:]], axis=0).astype(F32)
    far = jnp.concatenate([last_two, last_one], axis=0).astype(F32)
    return keep[: 2 * half] + near + far


def arranged_rows(place, half):
    return jnp.stack([((place ^ step) * 2 + part) * half for step, part in ORDER]).astype(jnp.int32)


def project_kernel(rows_ref, left_ref, right_ref, one_ref, two_ref, keep_ref, order_ref):
    half = left_ref.shape[0] // 8

    @pl.when(pl.program_id(0) == 0)
    def _():
        for k in range(8):
            first = pl.multiple_of(rows_ref[k], half)
            order_ref[k * half : (k + 1) * half, :] = left_ref[pl.ds(first, half), :]

    terms = contract_last(order_ref[...], right_ref[...])
    one_ref[...] = terms[: 2 * half].astype(BF)
    two_ref[...] = terms[2 * half : 4 * half].astype(BF)
    keep_ref[...] = terms[4 * half :]


def project(rows, left, right, column, name):
    length, depth = left.shape
    width = right.shape[0]
    tile = 512
    part = length // 4
    return pl.pallas_call(
        project_kernel,
        grid_spec=pltpu.PrefetchScalarGridSpec(
            num_scalar_prefetch=1,
            grid=(width // tile,),
            in_specs=[
                pl.BlockSpec((length, depth), lambda i, rows: (0, 0), pipeline_mode=pl.Buffered(1)),
                pl.BlockSpec((tile, depth), lambda i, rows: (i, column)),
            ],
            out_specs=[
                pl.BlockSpec((part, tile), lambda i, rows: (0, i)),
                pl.BlockSpec((part, tile), lambda i, rows: (0, i)),
                pl.BlockSpec((2 * part, tile), lambda i, rows: (0, i)),
                pl.BlockSpec((length, depth), lambda i, rows: (0, 0)),
            ],
        ),
        out_shape=[
            jax.ShapeDtypeStruct((part, width), BF),
            jax.ShapeDtypeStruct((part, width), BF),
            jax.ShapeDtypeStruct((2 * part, width), F32),
            jax.ShapeDtypeStruct((length, depth), BF),
        ],
        compiler_params=pltpu.CompilerParams(vmem_limit_bytes=40 * 2**20),
        cost_estimate=pl.CostEstimate(
            flops=2 * length * depth * width,
            bytes_accessed=2 * width * depth + 8 * length * width,
            transcendentals=0,
        ),
        name=name,
    )(rows, left, right)


def swap_core(value):
    return lax.ppermute(value, "seg", [(i, i ^ 1) for i in range(lax.axis_size("seg"))])


def along(value, sources, step):
    pairs = [(2 * i + core, 2 * (i + step) + core) for i in sources for core in range(2)]
    return lax.ppermute(value, "seg", pairs)


def short_chain():
    return lax.axis_size("seg") == 8


def sum_small(value, middle):
    core = lax.axis_index("seg") % 2
    mine = lax.dynamic_index_in_dim(value, core, 0, False)
    if not short_chain():
        return lax.dynamic_index_in_dim(lax.psum(value, "seg"), core, 0, False)
    total = mine.astype(F32) + swap_core(lax.dynamic_index_in_dim(value, 1 - core, 0, False)).astype(F32)
    rows = value.shape[1]
    cut = rows // 32 * 16
    chip = lax.axis_index("seg") // 2 % 2
    low = total.astype(BF)

    def half(which):
        return lax.dynamic_slice_in_dim(low, which * cut, rows - cut, 0)

    def exchange(value, bit):
        return lax.ppermute(value, "seg", [(i, i ^ bit) for i in range(8)])

    part = (half(chip).astype(F32) + after(exchange(half(1 - chip), 2), middle).astype(F32)).astype(BF)
    part = (part.astype(F32) + exchange(part, 4).astype(F32)).astype(BF)
    other = exchange(part, 2)
    shared = rows - 2 * cut
    return jnp.where(
        chip == 0,
        jnp.concatenate([part, other[shared:]], axis=0),
        jnp.concatenate([other, part[shared:]], axis=0),
    )


def sum_all(value):
    if not short_chain():
        return lax.psum(value, ("seq", "seg"))
    for axis, bits in (("seg", (1, 2, 4)), ("seq", (1, 2))):
        for bit in bits:
            pairs = [(i, i ^ bit) for i in range(lax.axis_size(axis))]
            value = value + lax.ppermute(value, axis, pairs)
    return value


def after(value, earlier):
    return lax.optimization_barrier((value, earlier))[0]


def neg_expm1(values):
    total = 1.0 + values * (1.0 / 9.0)
    for order in range(8, 1, -1):
        total = 1.0 + values * (1.0 / order) * total
    return jnp.where(values > -0.7, -values * total, 1.0 - jnp.exp(values))


def scan_kernel(
    blk_ref, low_ref, wd_ref, wi_ref, par_ref, conv_ref, branch_ref,
    states_ref, decay_ref, rate_ref, open_ref, mixed_ref,
):
    length = conv_ref.shape[0]
    par = par_ref[...]
    soft = par[2:3]
    row = lax.broadcasted_iota(jnp.int32, (CHUNK // 8, 8, LANES), 1)

    def body(step, carry):
        rows = pl.ds(pl.multiple_of(step * CHUNK, CHUNK), CHUNK)
        low = low_ref[rows, :]
        rate = jax.nn.sigmoid(contract(low, wd_ref[0]) + par[0:1])
        opened = jax.nn.sigmoid(contract(low, wi_ref[0]) + par[1:2])
        log_decay = -RATE_SCALE * rate * soft
        decay = jnp.exp(log_decay)
        drive = jnp.sqrt(neg_expm1(2.0 * log_decay)) * opened * conv_ref[rows, :]
        rate_ref[rows, :] = rate
        open_ref[rows, :] = opened
        decay_ref[rows, :] = decay
        prod = decay.reshape(CHUNK // 8, 8, LANES)
        total = drive.reshape(CHUNK // 8, 8, LANES)
        for shift in (1, 2, 4):
            inside = row >= shift
            moved = jnp.where(inside, pltpu.roll(total, shift, 1), 0.0)
            total = total + prod * moved
            prod = prod * jnp.where(inside, pltpu.roll(prod, shift, 1), 1.0)
        pieces = []
        for group in range(CHUNK // 8):
            piece = total[group] + prod[group] * carry
            carry = piece[7:8]
            pieces.append(piece)
        states = jnp.concatenate(pieces, axis=0)
        states_ref[rows, :] = states
        mixed_ref[rows, :] = (states * gelu_tanh(branch_ref[rows, :])).astype(BF)
        return carry

    lax.fori_loop(0, length // CHUNK, body, par[3:4])


def scan_forward(blk, conv_ext, decay_w, input_w, params, conv_out, projected):
    length, width = conv_out.shape
    tiles = width // LANES
    tile = pl.BlockSpec((length, LANES), lambda i, blk: (0, i))
    weight = pl.BlockSpec((1, decay_w.shape[1], LANES), lambda i, blk: (i, 0, 0))
    whole = jax.ShapeDtypeStruct((length, width), F32)
    return pl.pallas_call(
        scan_kernel,
        grid_spec=pltpu.PrefetchScalarGridSpec(
            num_scalar_prefetch=1,
            grid=(tiles,),
            in_specs=[
                pl.BlockSpec((length, decay_w.shape[1]), lambda i, blk: (0, blk[i])),
                weight,
                weight,
                pl.BlockSpec((8, LANES), lambda i, blk: (0, i)),
                tile,
                tile,
            ],
            out_specs=[tile] * 5,
        ),
        out_shape=[whole, whole, whole, whole, jax.ShapeDtypeStruct((length, width), BF)],
        compiler_params=pltpu.CompilerParams(vmem_limit_bytes=32 * 2**20),
        cost_estimate=pl.CostEstimate(
            flops=4 * length * width * 256, bytes_accessed=length * width * 28, transcendentals=0
        ),
        name="scan_forward",
    )(blk, conv_ext, decay_w, input_w, params, conv_out, projected)


def back_kernel(
    rows_ref, strip_ref, par_ref, mixed_in, branch_ref, states_ref, decay_ref, rate_ref, open_ref, conv_ref,
    proj_out, gate_out, input_out, direct_out, sums_out, strips_out, mixed_ref,
):
    length = conv_ref.shape[0]
    groups = CHUNK // 8
    par = par_ref[...]
    soft = par[2:3]
    row = lax.broadcasted_iota(jnp.int32, (groups, 8, LANES), 1)
    flat_row = lax.broadcasted_iota(jnp.int32, (CHUNK, LANES), 0)
    steps = length // CHUNK
    half = length // 8
    for k in range(8):
        mixed_ref[pl.ds(pl.multiple_of(rows_ref[k], half), half), :] = mixed_in[k * half : (k + 1) * half, :]

    def body(turn, carried):
        carry, gate_sum, input_sum, logit_sum = carried
        step = steps - 1 - turn
        first = pl.multiple_of(step * CHUNK, CHUNK)
        rows = pl.ds(first, CHUNK)
        mixed_grad = mixed_ref[rows, :]
        branch = branch_ref[rows, :]
        states = states_ref[rows, :]
        decay = decay_ref[rows, :]
        branch_act, pull = jax.vjp(gelu_tanh, branch)
        proj_out[rows, :] = pull(mixed_grad * states)[0].astype(BF)
        state_grad = mixed_grad * branch_act
        prod = decay.reshape(groups, 8, LANES)
        total = (decay * state_grad).reshape(groups, 8, LANES)
        for shift in (1, 2, 4):
            inside = row < 8 - shift
            moved = jnp.where(inside, pltpu.roll(total, 8 - shift, 1), 0.0)
            total = total + prod * moved
            prod = prod * jnp.where(inside, pltpu.roll(prod, 8 - shift, 1), 1.0)
        pieces = [None] * groups
        after = carry
        for group in reversed(range(groups)):
            piece = total[group] + prod[group] * after
            after = piece[0:1]
            pieces[group] = piece
        passed = jnp.concatenate(pieces, axis=0)
        shifted = jnp.where(flat_row == CHUNK - 1, carry, pltpu.roll(passed, CHUNK - 1, 0))
        adjoint = state_grad + shifted
        before = states_ref[pl.ds(pl.multiple_of(jnp.maximum(first - 8, 0), 8), 8), :][7:8]
        before = jnp.where(step == 0, par[3:4], before)
        previous = jnp.where(flat_row == 0, before, pltpu.roll(states, 1, 0))
        rate = rate_ref[rows, :]
        opened = open_ref[rows, :]
        conv = conv_ref[rows, :]
        log_decay = -RATE_SCALE * rate * soft
        scale = jnp.sqrt(neg_expm1(2.0 * log_decay))
        opened_conv = opened * conv
        ratio = jnp.where(scale > 0.0, decay / scale, 0.0)
        log_grad = decay * (adjoint * previous - adjoint * opened_conv * ratio)
        scaled = adjoint * scale
        direct_out[rows, :] = scaled * opened
        input_grad = (scaled * conv * opened * (1.0 - opened)).astype(BF)
        rate_grad = log_grad * rate
        gate_grad = (rate_grad * (1.0 - rate) * (-RATE_SCALE * soft)).astype(BF)
        gate_out[rows, :] = gate_grad
        input_out[rows, :] = input_grad

        def folded(value):
            return jnp.sum(value.astype(F32).reshape(groups, 8, LANES), axis=0)

        return (
            after,
            gate_sum + folded(gate_grad),
            input_sum + folded(input_grad),
            logit_sum + folded(rate_grad),
        )

    zero = jnp.zeros((8, LANES), F32)
    after, gate_sum, input_sum, logit_sum = lax.fori_loop(
        0, steps, body, (jnp.zeros((1, LANES), F32), zero, zero, zero)
    )
    sums_out[...] = jnp.concatenate(
        [
            jnp.sum(gate_sum, axis=0, keepdims=True),
            jnp.sum(input_sum, axis=0, keepdims=True),
            jnp.sum(logit_sum, axis=0, keepdims=True) * (-RATE_SCALE * par[4:5]),
            after,
            jnp.zeros((4, LANES), F32),
        ],
        axis=0,
    )

    @pl.when(pl.program_id(0) == strip_ref[0])
    def _():
        strips_out[0] = gate_out[...]
        strips_out[1] = input_out[...]


def scan_backward(rows, strip_tile, params, mixed_grad, projected, states, decays, rate, opened, conv_out):
    length, width = conv_out.shape
    tiles = width // LANES
    tile = pl.BlockSpec((length, LANES), lambda i, *_: (0, i))
    small = pl.BlockSpec((8, LANES), lambda i, *_: (0, i))
    low = jax.ShapeDtypeStruct((length, width), BF)
    return pl.pallas_call(
        back_kernel,
        grid_spec=pltpu.PrefetchScalarGridSpec(
            num_scalar_prefetch=2,
            grid=(tiles,),
            in_specs=[
                small,
            ]
            + [tile] * 7,
            out_specs=[tile] * 4 + [small, pl.BlockSpec((2, length, LANES), lambda i, *_: (0, 0, 0))],
            scratch_shapes=[pltpu.VMEM((length, LANES), F32)],
        ),
        out_shape=[
            jax.ShapeDtypeStruct((length, 2 * width), BF),
            low,
            low,
            jax.ShapeDtypeStruct((length, width), F32),
            jax.ShapeDtypeStruct((8, width), F32),
            jax.ShapeDtypeStruct((2, length, LANES), BF),
        ],
        compiler_params=pltpu.CompilerParams(vmem_limit_bytes=40 * 2**20),
        cost_estimate=pl.CostEstimate(
            flops=100 * length * width, bytes_accessed=length * width * 44, transcendentals=0
        ),
        name="scan_backward",
    )(rows, strip_tile, params, mixed_grad, projected, states, decays, rate, opened, conv_out)


def gates_kernel(
    blk_ref, near_ref, edge_ref, par_ref, sums_ref, gate_ref, gate_near, input_ref, input_near, strips_ref,
    wd_ref, wi_ref, direct_ref, low_t_ref, conv_in_ref, proj_in, proj_out, small_out, single_out,
):
    length = direct_ref.shape[0]
    block = low_t_ref.shape[0]
    edge = edge_ref[pl.program_id(0)] == 1
    gate, opened = gate_ref[...], input_ref[...]
    gate_both = jnp.concatenate([gate, jnp.where(edge, strips_ref[0], gate_near[...])], axis=1)
    input_both = jnp.concatenate([opened, jnp.where(edge, strips_ref[1], input_near[...])], axis=1)
    conv_grad = direct_ref[...] + contract_last(gate_both, wd_ref[0]) + contract_last(input_both, wi_ref[0])
    row = lax.broadcasted_iota(jnp.int32, (length, LANES), 0)
    par = par_ref[...]
    conv_in = conv_in_ref[...]
    conv_in_grad = par[0:1] * conv_grad
    tap_sums = [jnp.sum(conv_grad * conv_in, axis=0, keepdims=True)]
    for k in range(1, 4):
        moved = jnp.where(row < length - k, pltpu.roll(conv_grad, length - k, 0), 0.0)
        conv_in_grad = conv_in_grad + par[k : k + 1] * moved
        total = jnp.sum(moved * conv_in, axis=0, keepdims=True)
        for t in range(k):
            total = total + conv_grad[t : t + 1] * par[7 + t - k : 8 + t - k]
        tap_sums.append(total)
    proj_out[...] = conv_in_grad.astype(BF)
    window = []
    for s in range(3):
        total = par[3 - s : 4 - s] * conv_grad[0:1]
        for k in range(4 - s, 4):
            total = total + par[k : k + 1] * conv_grad[s - 3 + k : s - 2 + k]
        window.append(total)
    sums = sums_ref[...]
    zero = jnp.zeros((8, LANES), F32)
    vectors = jnp.concatenate(
        tap_sums + [jnp.sum(conv_grad, axis=0, keepdims=True), sums[0:3], zero], axis=0
    ).astype(BF)
    low_t = low_t_ref[...]
    small_out[0, :block, :] = contract(low_t, gate).astype(BF)
    small_out[1, :block, :] = contract(low_t, opened).astype(BF)
    small_out[0, block:, :] = vectors
    small_out[1, block:, :] = vectors
    single_out[...] = jnp.concatenate([sums[3:4]] + window + [zero, zero[:4]], axis=0).astype(BF)


def gates_backward(blk, near, edge, params, sums, gate, opened, strips, decay_w, input_w, direct, low_t, projected, proj):
    length, width = direct.shape
    tiles = width // LANES
    block = decay_w.shape[2]
    tile = pl.BlockSpec((length, LANES), lambda i, *_: (0, i))
    beside = pl.BlockSpec((length, LANES), lambda i, blk, near, edge: (0, near[i]))
    small = pl.BlockSpec((8, LANES), lambda i, *_: (0, i))
    weight = pl.BlockSpec((1, LANES, block), lambda i, *_: (i, 0, 0))
    second = pl.BlockSpec((length, LANES), lambda i, *_: (0, tiles + i))
    return pl.pallas_call(
        gates_kernel,
        grid_spec=pltpu.PrefetchScalarGridSpec(
            num_scalar_prefetch=3,
            grid=(tiles,),
            in_specs=[
                small,
                small,
                tile,
                beside,
                tile,
                beside,
                pl.BlockSpec(strips.shape, lambda i, *_: (0, 0, 0)),
                weight,
                weight,
                tile,
                pl.BlockSpec((block, length), lambda i, blk, near, edge: (blk[i], 0)),
                second,
                pl.BlockSpec(memory_space=pl.ANY),
            ],
            out_specs=[
                second,
                pl.BlockSpec((2, block + 16, LANES), lambda i, *_: (0, 0, i)),
                pl.BlockSpec((16, LANES), lambda i, *_: (0, i)),
            ],
        ),
        out_shape=[
            jax.ShapeDtypeStruct(proj.shape, BF),
            jax.ShapeDtypeStruct((2, block + 16, width), BF),
            jax.ShapeDtypeStruct((16, width), BF),
        ],
        input_output_aliases={15: 0},
        compiler_params=pltpu.CompilerParams(vmem_limit_bytes=32 * 2**20),
        cost_estimate=pl.CostEstimate(
            flops=8 * length * width * block, bytes_accessed=length * width * 20, transcendentals=0
        ),
        name="gates_backward",
    )(blk, near, edge, params, sums, gate, gate, opened, opened, strips, decay_w, input_w, direct, low_t, projected, proj)


def mlp_data(tile, low_ref, cot_ref, weight_ref):
    gate_up = contract(low_ref[...], weight_ref[:, : 2 * tile])
    hidden_grad = contract(cot_ref[...], weight_ref[:, 2 * tile :])
    gate_val, up_val = gate_up[:, :tile], gate_up[:, tile:]
    gate_act, pull = jax.vjp(gelu_tanh, gate_val)
    hidden = (gate_act * up_val).astype(BF)
    gate_grad = pull(hidden_grad * up_val)[0].astype(BF)
    up_grad = (hidden_grad * gate_act).astype(BF)
    return jnp.concatenate([gate_grad, up_grad], axis=1), hidden


def add_term(total_ref, term):
    @pl.when(pl.program_id(0) == 0)
    def _():
        total_ref[...] = term

    @pl.when(pl.program_id(0) > 0)
    def _():
        total_ref[...] += term


def give_halves(total_ref, before_ref, one_ref, two_ref, keep_ref):
    @pl.when(pl.program_id(0) == pl.num_programs(0) - 1)
    def _():
        part = total_ref.shape[0] // 4
        one_ref[...] = (total_ref[:part] + before_ref[:part]).astype(BF)
        two_ref[...] = (total_ref[part : 2 * part] + before_ref[part : 2 * part]).astype(BF)
        keep_ref[...] = total_ref[2 * part :] + before_ref[2 * part :]


def mlp_first_kernel(tile, low_ref, cot_ref, weight_ref, units_ref, back_ref, out_ref):
    both, hidden = mlp_data(tile, low_ref, cot_ref, weight_ref)
    units_ref[:, : 2 * tile] = both
    units_ref[:, 2 * tile :] = hidden
    add_term(back_ref, contract_last(both, weight_ref[:, : 2 * tile]))
    add_term(out_ref, contract_last(hidden, weight_ref[:, 2 * tile :]))


def mlp_last_kernel(tile, low_ref, cot_ref, weight_ref, before_ref, units_ref, one_ref, two_ref, keep_ref, back_ref):
    both, hidden = mlp_data(tile, low_ref, cot_ref, weight_ref)
    units_ref[:, : 2 * tile] = both
    units_ref[:, 2 * tile :] = hidden
    add_term(back_ref, contract_last(both, weight_ref[:, : 2 * tile]))
    give_halves(back_ref, before_ref, one_ref, two_ref, keep_ref)


def mlp_out_kernel(tile, weight_ref, units_ref, before_ref, one_ref, two_ref, keep_ref, out_ref):
    add_term(out_ref, contract_last(units_ref[:, 2 * tile :], weight_ref[:, 2 * tile :]))
    give_halves(out_ref, before_ref, one_ref, two_ref, keep_ref)


def mlp_grad_kernel(tile, low_ref, low_other, cot_ref, cot_other, units_ref, units_other, grad_ref):
    cut = 2 * tile
    grad_ref[:, :cut] = (
        contract(low_ref[...], units_ref[:, :cut]) + contract(low_other[...], units_other[:, :cut])
    ).astype(BF)
    grad_ref[:, cut:] = (
        contract(cot_ref[...], units_ref[:, cut:]) + contract(cot_other[...], units_other[:, cut:])
    ).astype(BF)


def outer_grad_kernel(left_ref, left_other, right_ref, right_other, held_ref, grad_ref):
    grad_ref[...] = (
        contract(left_ref[...], right_ref[...]) + contract(left_other[...], right_other[...])
    ).astype(BF)


def outer_grad(left_t, right, held, width, first, name):
    depth, length = left_t[0].shape
    steps = right[0].shape[1] // width
    fixed = pl.BlockSpec((depth, length), lambda i: (0, 0), pipeline_mode=pl.Buffered(1))
    moving = pl.BlockSpec((length, width), lambda i: (0, i))
    return pl.pallas_call(
        outer_grad_kernel,
        grid=(steps,),
        in_specs=[fixed] * 2 + [moving] * 2 + [pl.BlockSpec(memory_space=pl.ANY)],
        out_specs=pl.BlockSpec((depth, width), lambda i: (0, first + i)),
        out_shape=jax.ShapeDtypeStruct(held.shape, BF),
        input_output_aliases={4: 0},
        compiler_params=pltpu.CompilerParams(vmem_limit_bytes=40 * 2**20),
        cost_estimate=pl.CostEstimate(
            flops=4 * depth * length * width * steps,
            bytes_accessed=2 * steps * width * (depth + 2 * length) + 4 * depth * length,
            transcendentals=0,
        ),
        name=name,
    )(*left_t, *right, held)


def mlp_grad_beside_kernel(
    tile, first, low_ref, low_other, cot_ref, cot_other, units_ref, units_other, held_ref, grad_ref, sem
):
    mlp_grad_kernel(tile, low_ref, low_other, cot_ref, cot_other, units_ref, units_other, grad_ref)
    columns = pl.ds(pl.multiple_of(first + pl.program_id(0) * 3 * tile, LANES), 3 * tile)
    copy = pltpu.make_async_copy(grad_ref, held_ref.at[:, columns], sem)
    copy.start()
    copy.wait()


def mlp_grad_beside(tile, low_t, cot_t, units, first):
    (depth, rows), columns = low_t[0].shape, units[0].shape[1]
    fixed = pl.BlockSpec((depth, rows), lambda i: (0, 0), pipeline_mode=pl.Buffered(1))
    moving = pl.BlockSpec((rows, 3 * tile), lambda i: (0, i))
    return pl.pallas_call(
        lambda *refs: mlp_grad_beside_kernel(tile, first, *refs),
        grid=(columns // (3 * tile),),
        in_specs=[fixed] * 4 + [moving] * 2,
        out_specs=pl.BlockSpec(memory_space=pl.ANY),
        out_shape=jax.ShapeDtypeStruct((depth, first + columns), BF),
        scratch_shapes=[pltpu.VMEM((depth, 3 * tile), BF), pltpu.SemaphoreType.DMA],
        compiler_params=pltpu.CompilerParams(vmem_limit_bytes=40 * 2**20),
        cost_estimate=pl.CostEstimate(
            flops=4 * rows * depth * columns, bytes_accessed=2 * depth * columns + 8 * rows * depth, transcendentals=0
        ),
        name="mlp_grad_last",
    )(*low_t, *cot_t, *units)


def unpack_kernel(tile, first, sums_ref, in_held, out_held, feed_in_ref, feed_out_ref, recur_in_ref, recur_out_ref):
    width = recur_out_ref.shape[1]
    for i in range(2):
        recur_in_ref[:, i, :] = sums_ref[:, i * width : (i + 1) * width].astype(F32)
    recur_out_ref[...] = sums_ref[:, 2 * width : 3 * width].astype(F32)
    for k in range(feed_out_ref.shape[1] // tile):
        at = slice(k * tile, (k + 1) * tile)
        start = first + 3 * tile * k
        for i in range(2):
            feed_in_ref[:, i, at] = sums_ref[:, start + i * tile : start + (i + 1) * tile].astype(F32)
        feed_out_ref[:, at] = sums_ref[:, start + 2 * tile : start + 3 * tile].astype(F32)


def unpack(tile, sums, feed_in, feed_out, recur_width, done):
    rows = sums.shape[0]
    units = feed_out.shape[1]
    part = units - done
    anywhere = pl.BlockSpec(memory_space=pl.ANY)
    return pl.pallas_call(
        lambda *refs: unpack_kernel(tile, 3 * recur_width, *refs),
        grid=(1,),
        in_specs=[pl.BlockSpec(sums.shape, lambda i: (0, 0)), anywhere, anywhere],
        out_specs=[
            pl.BlockSpec((rows, 2, part), lambda i: (0, 0, done // part)),
            pl.BlockSpec((rows, part), lambda i: (0, done // part)),
            pl.BlockSpec((rows, 2, recur_width), lambda i: (0, 0, 0)),
            pl.BlockSpec((rows, recur_width), lambda i: (0, 0)),
        ],
        out_shape=[
            jax.ShapeDtypeStruct(feed_in.shape, F32),
            jax.ShapeDtypeStruct(feed_out.shape, F32),
            jax.ShapeDtypeStruct((rows, 2, recur_width), F32),
            jax.ShapeDtypeStruct((rows, recur_width), F32),
        ],
        input_output_aliases={1: 0, 2: 1},
        compiler_params=pltpu.CompilerParams(vmem_limit_bytes=40 * 2**20),
        cost_estimate=pl.CostEstimate(flops=0, bytes_accessed=6 * rows * sums.shape[1], transcendentals=0),
        name="unpack",
    )(sums, feed_in, feed_out)


def mlp_call(kernel, tile, products, rows, width, columns, fixed_in, moving_in, fixed_out, moving_out, scratch, name):
    def fixed(shape, single):
        return pl.BlockSpec(shape, lambda i: (0, 0), pipeline_mode=pl.Buffered(1) if single else None)

    def moving(shape):
        return pl.BlockSpec((shape[0], 3 * tile), lambda i: (0, i))

    return pl.pallas_call(
        lambda *refs: kernel(tile, *refs),
        grid=(columns // (3 * tile),),
        in_specs=[
            fixed(value.shape, True) if kind == "fixed" else moving(value.shape)
            for kind, value in fixed_in + moving_in
        ],
        out_specs=[moving(shape) for shape, _ in moving_out] + [fixed(shape, False) for shape, _ in fixed_out],
        out_shape=[jax.ShapeDtypeStruct(shape, kind) for shape, kind in moving_out + fixed_out],
        scratch_shapes=[pltpu.VMEM(shape, kind) for shape, kind in scratch],
        compiler_params=pltpu.CompilerParams(vmem_limit_bytes=60 * 2**20),
        cost_estimate=pl.CostEstimate(
            flops=2 * products * rows * width * columns // 3,
            bytes_accessed=4 * width * columns + 16 * rows * width,
            transcendentals=0,
        ),
        name=name,
    )(*[value for _, value in fixed_in + moving_in])


def half_shapes(rows, width):
    part = rows // 4
    return [((part, width), BF), ((part, width), BF), ((2 * part, width), F32)]


def mlp_first(tile, low2, cot, weight):
    (rows, width), columns = low2.shape, weight.shape[1]
    ins = [("fixed", low2), ("fixed", cot), ("moving", weight)]
    return mlp_call(
        mlp_first_kernel, tile, 6, rows, width, columns, ins, [],
        [((rows, width), F32)] * 2, [((rows, columns), BF)], [], "mlp_first",
    )


def mlp_last(tile, low2, cot, weight, before):
    (rows, width), columns = low2.shape, weight.shape[1]
    ins = [("fixed", low2), ("fixed", cot), ("moving", weight), ("fixed", before)]
    return mlp_call(
        mlp_last_kernel, tile, 5, rows, width, columns, ins, [],
        half_shapes(rows, width), [((rows, columns), BF)], [((rows, width), F32)], "mlp_last",
    )


def mlp_out_last(tile, weight, units, before):
    (width, columns), rows = weight.shape, units.shape[0]
    ins = [("moving", weight), ("moving", units), ("fixed", before)]
    return mlp_call(
        mlp_out_kernel, tile, 1, rows, width, columns, ins, [],
        half_shapes(rows, width), [], [((rows, width), F32)], "mlp_out",
    )


def mlp_grad(tile, low_t, cot_t, units):
    (depth, rows), columns = low_t[0].shape, units[0].shape[1]
    ins = [("fixed", value) for value in (*low_t, *cot_t)] + [("moving", value) for value in units]
    return mlp_call(
        mlp_grad_kernel, tile, 3, rows, 2 * depth, columns, ins, [],
        [], [((depth, columns), BF)], [], "mlp_grad",
    )[0]


def shards(
    tokens,
    cotangent,
    start_state,
    start_window,
    first_gain,
    recur_in,
    conv_taps,
    conv_bias,
    decay_gate,
    input_gate,
    decay_bias,
    input_bias,
    decay_logit,
    recur_out,
    second_gain,
    feed_in,
    feed_out,
):
    segments, length, model_width = tokens.shape
    recur_width = conv_taps.shape[1]
    head_count, block_size = decay_gate.shape[:2]
    edge_rows = conv_taps.shape[0] - 1
    seq_parts = lax.axis_size("seq")
    place = lax.axis_index("seq")
    own_rows, _, recur_part = recur_in.shape
    feed_part = feed_in.shape[2]
    first_channel = place * recur_part
    first_block = first_channel // block_size
    block_count = -(-recur_part // block_size)
    strip = block_count * block_size - recur_part
    odd = place % 2 == 1

    def own(value):
        return lax.dynamic_slice_in_dim(value, first_channel, recur_part, value.ndim - 1)

    def strip_of(value):
        return jnp.where(odd, value[:, :strip], value[:, recur_part - strip :])

    def gather_seg(value):
        return lax.all_gather(value, "seg", axis=0, tiled=True)

    seg_parts = lax.axis_size("seg")
    core = lax.axis_index("seg") % 2

    def scatter_rows(value):
        groups = [list(range(c, seg_parts, 2)) for c in range(2)]
        return lax.psum_scatter(value, "seg", scatter_dimension=0, tiled=True, axis_index_groups=groups)

    def gathered(blocks, rows, name):
        whole, mine, other = assemble(rows, core[None].astype(jnp.int32), blocks, seg_parts // 2, name)
        return whole, (mine, swap_core(other))

    def of_both(value):
        return value, swap_core(value)

    unit = 2 * LANES
    first_part = 2 * feed_part // 3 // unit * unit
    cuts = [(0, first_part), (first_part, feed_part)]

    def feed_columns(first, count):
        return [feed_in[:, 0, first : first + count], feed_in[:, 1, first : first + count], feed_out[:, first : first + count]]

    feeds = [
        jnp.concatenate([c for first in range(a, b, unit) for c in feed_columns(first, unit)], axis=1)
        for a, b in cuts
    ]
    recur = gather_seg(jnp.concatenate([recur_in[:, 0], recur_in[:, 1], recur_out], axis=1))
    feed_first = gather_seg(feeds[0])
    feed_last = gather_seg(feeds[1])

    inputs = tokens.astype(F32).reshape(length, model_width)
    upstream = cotangent.reshape(length, model_width)
    low1 = rms_norm(inputs, first_gain).astype(BF)
    rows = arranged_rows(place, length // 2)
    straight = jnp.arange(8, dtype=jnp.int32) * (length // 2)
    all_low1, low1_rows = gathered(gather_halves(low1), rows, "gather_low1")
    all_cot, cot_rows = gathered(gather_halves(upstream), straight, "gather_cot")

    taps = own(conv_taps)
    logit = own(decay_logit[None])
    params = jnp.concatenate(
        [
            own(decay_bias[None]),
            own(input_bias[None]),
            jax.nn.softplus(logit),
            own(start_state),
            jax.nn.sigmoid(logit),
            jnp.zeros((3, recur_part), F32),
        ],
        axis=0,
    )
    window = own(start_window)[0]
    conv_params = jnp.concatenate([taps, window, jnp.zeros((1, recur_part), F32)], axis=0)
    tiles = recur_part // LANES
    halves = block_size // LANES
    first_tile = jnp.where(odd, strip // LANES, 0)
    tile_place = first_tile + jnp.arange(tiles)
    tile_block = (tile_place // halves).astype(jnp.int32)
    near = (tile_place ^ 1) - first_tile
    edge = ((near < 0) | (near >= tiles)).astype(jnp.int32)
    near = jnp.clip(near, 0, tiles - 1).astype(jnp.int32)
    strip_tile = jnp.where(odd, 0, tiles - 1).astype(jnp.int32)[None]

    def gate_tiles(blocks):
        blocks = lax.dynamic_slice_in_dim(blocks, first_block, block_count, 0)
        columns = blocks.reshape(block_count, block_size, halves, LANES).transpose(0, 2, 1, 3)
        columns = columns.reshape(block_count * halves, block_size, LANES)
        lines = blocks.reshape(block_count * halves, LANES, block_size)
        turned = jnp.concatenate([lines[:, :, LANES:], lines[:, :, :LANES]], axis=2)
        swapped = (jnp.arange(block_count * halves) % 2 == 1)[:, None, None]
        lines = jnp.where(swapped, turned, lines)
        return (
            lax.dynamic_slice_in_dim(columns, first_tile, tiles, 0),
            lax.dynamic_slice_in_dim(lines, first_tile, tiles, 0),
        )

    decay_columns, decay_lines = gate_tiles(decay_gate)
    input_columns, input_lines = gate_tiles(input_gate)

    projected = contract(all_low1, recur[:, : 2 * recur_part])
    padded = jnp.concatenate([window, projected[:, recur_part:]], axis=0)
    conv_out = conv_apply(padded, taps, own(conv_bias[None]))
    conv_low = conv_out.astype(BF)
    arrived = swap(strip_of(conv_low), 1)
    conv_ext = jnp.where(
        odd,
        jnp.concatenate([arrived, conv_low], axis=1),
        jnp.concatenate([conv_low, arrived], axis=1),
    )
    states, decays, rate, opened, mixed_low = scan_forward(
        tile_block, conv_ext, decay_columns, input_columns, params, conv_out, projected
    )
    *pieces, mixed_low = project(rows, mixed_low, recur, 2, "mixer_out")
    residual = inputs + scatter_halves(*pieces)

    low2 = rms_norm(residual, second_gain).astype(BF)
    all_low2, low2_rows = gathered(gather_halves(low2), straight, "gather_low2")
    units, back_first, out_first = mlp_first(unit, all_low2, all_cot, feed_first)
    grad_first = scatter_rows(mlp_grad(unit, low2_rows, cot_rows, of_both(units)))
    units, *pieces = mlp_last(unit, all_low2, all_cot, feed_last, back_first)
    normed2_grad = scatter_halves(*pieces)
    units_last = units
    residual_norm_grad, second_gain_grad = jax.vjp(rms_norm, residual, second_gain)[1](normed2_grad)
    residual_grad = upstream.astype(F32) + residual_norm_grad

    mixer_blocks = gather_halves(residual_grad.astype(BF))
    held = mlp_grad_beside(unit, low2_rows, cot_rows, of_both(units_last), 3 * recur_part)
    mixer_grad, mixer_rows = gathered(after(mixer_blocks, held), straight, "gather_mixer")
    proj_grad, gate_low_grad, input_low_grad, conv_direct, sums, strips = scan_backward(
        rows, strip_tile, params, contract(mixer_grad, recur[:, 2 * recur_part :]), projected, states, decays, rate,
        opened, conv_out,
    )
    held = outer_grad(mixer_rows, of_both(mixed_low), held, recur_part, 2, "recur_out_grad")
    strips = after(swap(strips, 1), held)
    proj_grad, small, single = gates_backward(
        tile_block, near, edge, conv_params, sums, gate_low_grad, input_low_grad, strips,
        decay_lines, input_lines, conv_direct, conv_ext.T, projected, proj_grad,
    )
    mlp_term = scatter_halves(*mlp_out_last(unit, feed_last, after(units_last, proj_grad), out_first))
    output = (residual + mlp_term).astype(BF).reshape(tokens.shape)
    grad_last_term = outer_grad(low1_rows, of_both(proj_grad), held, recur_part, 0, "recur_in_grad")
    *pieces, _ = project(rows, after(proj_grad, grad_last_term), recur, 0, "normed1_grad")
    normed1_grad = scatter_halves(*pieces)
    input_norm_grad, first_gain_grad = jax.vjp(rms_norm, inputs, first_gain)[1](normed1_grad)
    input_grad = (residual_grad + input_norm_grad).astype(BF).reshape(tokens.shape)

    grad_last = scatter_rows(after(grad_last_term, grad_first))

    def columns_of(value, which, start):
        return jnp.concatenate(
            [value[:, at : at + unit] for at in range(start + which * unit, value.shape[1], 3 * unit)], axis=1
        ).astype(F32)

    def feed_grads(value, start):
        return jnp.stack([columns_of(value, i, start) for i in range(2)], axis=1), columns_of(value, 2, start)

    feed_in_first, feed_out_first = feed_grads(grad_first, 0)
    feed_in_grad = jnp.pad(feed_in_first, ((0, 0), (0, 0), (0, feed_part - first_part)))
    feed_out_grad = jnp.pad(feed_out_first, ((0, 0), (0, feed_part - first_part)))
    grad_last = after(grad_last, (feed_in_grad, feed_out_grad))
    feed_in_grad, feed_out_grad, recur_in_grad, recur_out_grad = unpack(
        unit, grad_last, feed_in_grad, feed_out_grad, recur_part, first_part
    )

    mine = gather_seq(jnp.concatenate([sum_small(small, grad_last_term), single], axis=0))
    swapped = [jnp.where(odd, mine[i ^ 1], mine[i]) for i in range(4)]
    mine = jnp.concatenate([jnp.where(place >= 2, swapped[i ^ 2], swapped[i]) for i in range(4)], axis=1)
    vectors = mine[block_size:].astype(F32)
    other = swap_core(mine[:block_size])

    def as_blocks(which):
        value = jnp.where(core == which, mine[:block_size], other).astype(F32)
        return value.reshape(block_size, head_count, block_size).transpose(1, 0, 2)

    gains = sum_all(jnp.stack([first_gain_grad, second_gain_grad]))
    kernel_taps = conv_taps.shape[0]
    return (
        output,
        input_grad,
        vectors[16:17],
        vectors[17 : 17 + edge_rows][None],
        gains[0],
        recur_in_grad,
        vectors[:kernel_taps],
        vectors[kernel_taps],
        as_blocks(0),
        as_blocks(1),
        vectors[kernel_taps + 1],
        vectors[kernel_taps + 2],
        vectors[kernel_taps + 3],
        recur_out_grad,
        gains[1],
        feed_in_grad,
        feed_out_grad,
    )


def solution(mesh):
    placed = (
        P("seg", "seq", None),
        P("seg", "seq", None),
        P("seg", None),
        P("seg", None, None),
        P(),
        P("seg", None, "seq"),
        P(),
        P(),
        P(),
        P(),
        P(),
        P(),
        P(),
        P("seg", "seq"),
        P(),
        P("seg", None, "seq"),
        P("seg", "seq"),
    )
    return jax.shard_map(
        shards,
        mesh=mesh,
        in_specs=placed,
        out_specs=(
            P("seg", "seq", None),
            P("seg", "seq", None),
            P("seg", None),
            P("seg", None, None),
            P(),
            P("seg", None, "seq"),
            P(),
            P(),
            P(),
            P(),
            P(),
            P(),
            P(),
            P("seg", "seq"),
            P(),
            P("seg", None, "seq"),
            P("seg", "seq"),
        ),
        check_vma=False,
    )
```
